32 devices in a mesh: fsdp: 8 (over z, x), tp: 4 (over y, core).
Axes of the slice: x: 2, y: 2, z: 4, core: 2. Of those that a mesh axis runs over, the one named last changes fastest.
Arguments:
- tokens: bfloat16 [4096, 2048], P('fsdp'), may hold values from -6 to 6
- qkv_weight: bfloat16 [2048, 3, 2048], P('fsdp', None, 'tp'), may hold values from -0.125 to 0.125
- qkv_bias: bfloat16 [3, 8, 256], P(None, 'tp', 'fsdp'), may hold values from -1.796875 to 1.796875
- dense_weight: bfloat16 [2048, 2048], P('tp', 'fsdp'), may hold values from -0.75 to 0.75
- dense_bias: bfloat16 [2048], P('fsdp'), may hold values from -1.796875 to 1.796875
- fc_in_weight: bfloat16 [2048, 8192], P('fsdp', 'tp'), may hold values from -0.125 to 0.125
- fc_in_bias: bfloat16 [128, 64], P('tp', 'fsdp'), may hold values from -1.796875 to 1.796875
- fc_out_weight: bfloat16 [8192, 2048], P('tp', 'fsdp'), may hold values from -0.0625 to 0.0625
- fc_out_bias: bfloat16 [2048], P('fsdp'), may hold values from -1.796875 to 1.796875
- norm1_gain: bfloat16 [2048], P('fsdp'), may hold values from 0.099609375 to 1.8984375
- norm1_shift: bfloat16 [2048], P('fsdp'), may hold values from -1.796875 to 1.796875
- norm2_gain: bfloat16 [2048], P('fsdp'), may hold values from 0.099609375 to 1.8984375
- norm2_shift: bfloat16 [2048], P('fsdp'), may hold values from -1.796875 to 1.796875
- cotangent: bfloat16 [4096, 2048], P('fsdp'), may hold values from -6 to 6
- subset_ids: int32 [4096], P('fsdp'), may hold values from 0 to 21, as said below
- seq_starts: int32 [4], replicated, may hold values from 0 to 4096, as said below
Outputs:
- mixed: bfloat16 [4096, 2048], P('fsdp', 'tp')
- tokens_grad: bfloat16 [4096, 2048], P('fsdp', 'tp')
- qkv_weight_grad: float32 [2048, 3, 2048], P('fsdp', None, 'tp')
- qkv_bias_grad: float32 [3, 8, 256], P(None, 'tp', 'fsdp')
- dense_weight_grad: float32 [2048, 2048], P('tp', 'fsdp')
- dense_bias_grad: float32 [2048], P('fsdp')
- fc_in_weight_grad: float32 [2048, 8192], P('fsdp', 'tp')
- fc_in_bias_grad: float32 [128, 64], P('tp', 'fsdp')
- fc_out_weight_grad: float32 [8192, 2048], P('tp', 'fsdp')
- fc_out_bias_grad: float32 [2048], P('fsdp')
- norm1_gain_grad: float32 [2048], P('fsdp')
- norm1_shift_grad: float32 [2048], P('fsdp')
- norm2_gain_grad: float32 [2048], P('fsdp')
- norm2_shift_grad: float32 [2048], P('fsdp')
The draws below stay inside these ranges and needn't reach their ends.
Inputs may be any that keep to these rules, and one draw needn't show every extreme that they name: `subset_ids`: rows are mostly grouped in order: about half of the rows carry the subset of their place among 22 equal runs of rows, the rest a random subset; every subset appears. seq_starts[0] = 0; the starts increase until they reach 4096, and all later entries equal 4096 and start no document. Every document has at most 2048 rows and at least one has 2048; every document but the last has at least 1536 rows.
All inputs are finite; a program needn't handle non-finite values.
Results may differ from the reference program's by a relative error of at most 0.012.
Values may be sent and summed in bfloat16 or wider, within the bound.
A program may use at most 256 MiB of HBM per device.

```python
import math
import jax
import jax.numpy as jnp
from jax import lax

D = 2048
HEADS = 8
HDIM = 256
ROT = 64
FF = 8192
SEQ_LEN = 2048
KBLOCK = 1024
SUBSETS = 22
TOKENS = 4096
SEQS = 4


def draw_subset_ids(key, part):
    key = jax.random.fold_in(key, 11)
    coin_key, pick_key = jax.random.split(key)
    coin = jax.random.randint(coin_key, (TOKENS,), 0, 2)
    random_ids = jax.random.randint(pick_key, (TOKENS,), 0, SUBSETS)
    grouped = jnp.arange(TOKENS, dtype=jnp.int32) * SUBSETS // TOKENS
    return jnp.where(coin == 1, random_ids, grouped).astype(jnp.int32)


def draw_seq_starts(key, part):
    key = jax.random.fold_in(key, 23)
    length_key, pick_key = jax.random.split(key, 2)
    lengths = jax.random.randint(length_key, (SEQS,), 3 * SEQ_LEN // 4, SEQ_LEN + 1).astype(jnp.int32)
    longest = jax.random.randint(pick_key, (), 0, TOKENS // SEQ_LEN).astype(jnp.int32)
    lengths = jnp.where(jnp.arange(SEQS, dtype=jnp.int32) == longest, SEQ_LEN, lengths).astype(jnp.int32)
    ends = jnp.cumsum(lengths).astype(jnp.int32)
    starts = jnp.concatenate([jnp.zeros((1,), jnp.int32), ends[:-1]])
    return jnp.minimum(starts, TOKENS).astype(jnp.int32)


def block_scale(stream_key, dims, cuts, low, high):
    def one(position, blocks):
        draws = jax.random.uniform(jax.random.fold_in(jax.random.fold_in(stream_key, 6), position), (blocks,), jnp.float32, low / len(cuts), high / len(cuts))
        return jnp.repeat(jnp.exp(draws), dims[position] // blocks).reshape((-1,) + (1,) * (len(dims) - position - 1))

    level = one(*cuts[0])
    for cut in cuts[1:]:
        level = level * one(*cut)
    return level


def bell_draw(stream_key, dims, scale, limit, cuts=(), kind=jnp.bfloat16):
    drawn = jax.random.normal(stream_key, dims, jnp.float32) * scale
    if len(cuts) > 0:
        drawn = block_scale(stream_key, dims, cuts, -0.22, 0.18) * drawn
    return jnp.clip(drawn, min=-limit, max=limit).astype(kind)


def setup_inputs(seed: int = 0) -> dict:
    key_list = jax.random.split(jax.random.key(seed), 17)
    tokens = bell_draw(key_list[0], (TOKENS, D), 1.0, 6.0, ((0, 8),))
    qkv_weight = bell_draw(key_list[1], (D, 3, D), D ** -0.5, 0.125, ((0, 8), (2, 4)))
    qkv_bias = bell_draw(key_list[2], (3, HEADS, HDIM), 0.3, 1.796875, ((1, 4), (2, 8)))
    dense_weight = bell_draw(key_list[3], (D, D), (D // 32) ** -0.5, 0.75, ((0, 4), (1, 8)))
    dense_bias = bell_draw(key_list[4], (D,), 0.3, 1.796875, ((0, 8),))
    fc_in_weight = bell_draw(key_list[5], (D, FF), D ** -0.5, 0.125, ((0, 8), (1, 4)))
    fc_in_bias = bell_draw(key_list[6], (FF // 64, 64), 0.3, 1.796875, ((0, 4), (1, 8)))
    fc_out_weight = bell_draw(key_list[7], (FF, D), FF ** -0.5, 0.0625, ((0, 4), (1, 8)))
    fc_out_bias = bell_draw(key_list[8], (D,), 0.3, 1.796875, ((0, 8),))
    norm1_gain = jnp.clip(1.0 + 0.18 * jax.random.normal(key_list[9], (D,), jnp.float32), 0.099609375, 1.8984375).astype(jnp.bfloat16)
    norm1_shift = bell_draw(key_list[10], (D,), 0.3, 1.796875, ((0, 8),))
    norm2_gain = jnp.clip(1.0 + 0.18 * jax.random.normal(key_list[11], (D,), jnp.float32), 0.099609375, 1.8984375).astype(jnp.bfloat16)
    norm2_shift = bell_draw(key_list[12], (D,), 0.3, 1.796875, ((0, 8),))
    cotangent = bell_draw(key_list[13], (TOKENS, D), 1.0, 6.0, ((0, 8),))
    subset_ids = draw_subset_ids(jax.random.fold_in(key_list[16], 71), 0)
    seq_starts = draw_seq_starts(jax.random.fold_in(key_list[16], 71), 0)
    return dict(tokens=tokens, qkv_weight=qkv_weight, qkv_bias=qkv_bias, dense_weight=dense_weight, dense_bias=dense_bias, fc_in_weight=fc_in_weight, fc_in_bias=fc_in_bias, fc_out_weight=fc_out_weight, fc_out_bias=fc_out_bias, norm1_gain=norm1_gain, norm1_shift=norm1_shift, norm2_gain=norm2_gain, norm2_shift=norm2_shift, cotangent=cotangent, subset_ids=subset_ids, seq_starts=seq_starts)


EPS = 1e-05
HIGH = lax.Precision.HIGHEST

@jax.custom_vjp
def low(v):
    return lax.optimization_barrier(v.astype(jnp.bfloat16)).astype(jnp.float32)

@jax.custom_vjp
def low_back(v):
    return v

def low_keep(v):
    return (low(v), None)

def low_pass(kept, grad):
    return (grad,)

def back_keep(v):
    return (v, None)

def back_low(kept, grad):
    return (low(grad),)
low.defvjp(low_keep, low_pass)
low_back.defvjp(back_keep, back_low)

def norm_rows(values, gain, shift):
    mean = lax.optimization_barrier(jnp.mean(values, axis=-1, keepdims=True))
    centred = values - mean
    spread = lax.optimization_barrier(jnp.mean(centred * centred, axis=-1, keepdims=True))
    return centred * lax.rsqrt(spread + EPS) * gain + shift

def gelu_exact(values):
    return jax.nn.gelu(values, approximate=False)

def rotate(values, positions):
    half = ROT // 2
    steps = jnp.arange(half, dtype=jnp.float32)
    freq = 1.0 / 10000.0 ** (steps * 2.0 / ROT)
    angle = positions[:, None] * freq[None, :]
    cosine = jnp.cos(angle)[:, None, :]
    sine = jnp.sin(angle)[:, None, :]
    first = values[..., :half]
    second = values[..., half:ROT]
    return jnp.concatenate([first * cosine - second * sine, second * cosine + first * sine, values[..., ROT:]], axis=-1)

def locate(indices, starts):
    above = indices[:, None] >= starts[None, :]
    doc_ids = lax.optimization_barrier(jnp.sum(above.astype(jnp.int32), axis=1)) - 1
    pick = doc_ids[:, None] == jnp.arange(starts.shape[0], dtype=jnp.int32)[None, :]
    first = lax.optimization_barrier(jnp.sum(jnp.where(pick, starts[None, :], 0), axis=1))
    return (doc_ids, (indices - first).astype(jnp.float32))

def product(left, right):
    return jnp.dot(left, right, precision=HIGH)

def reference(tokens, qkv_weight, qkv_bias, dense_weight, dense_bias, fc_in_weight, fc_in_bias, fc_out_weight, fc_out_bias, norm1_gain, norm1_shift, norm2_gain, norm2_shift, cotangent, subset_ids, seq_starts):
    indices = jnp.arange(TOKENS, dtype=jnp.int32)
    doc_ids, positions = locate(indices, seq_starts)
    scale = 1.0 / math.sqrt(HDIM)
    block_starts = jnp.arange(TOKENS // KBLOCK, dtype=jnp.int32) * KBLOCK

    def attend(queries, keys, values):

        def block(begin):
            part = lax.dynamic_slice_in_dim(queries, begin, KBLOCK, 0)
            rows = begin + jnp.arange(KBLOCK, dtype=jnp.int32)
            row_docs = lax.dynamic_slice_in_dim(doc_ids, begin, KBLOCK, 0)
            allowed = (indices[None, :] <= rows[:, None]) & (doc_ids[None, :] == row_docs[:, None])
            scores = low_back(jnp.einsum('qhd,khd->hqk', part, keys, precision=HIGH) * scale)
            scores = jnp.where(allowed[None], scores, -1e+30)
            top = lax.optimization_barrier(jnp.max(scores, axis=2, keepdims=True))
            expo = jnp.exp(scores - top)
            probs = expo / lax.optimization_barrier(jnp.sum(expo, axis=2, keepdims=True))
            return jnp.einsum('hqk,khd->qhd', low(probs), values, precision=HIGH)
        out = lax.map(jax.checkpoint(block), block_starts)
        return out.reshape(TOKENS, HEADS, HDIM)

    def forward(x, w_qkv, b_qkv, w_dense, b_dense, w_in, b_in, w_out, b_out, g_one, s_one, g_two, s_two):
        h_one = low(norm_rows(x, g_one, s_one))
        qkv = low_back(product(h_one, w_qkv.reshape(D, 3 * D)) + b_qkv.reshape(3 * D))
        qkv = qkv.reshape(TOKENS, 3, HEADS, HDIM)
        queries = low(rotate(qkv[:, 0], positions))
        keys = low(rotate(qkv[:, 1], positions))
        values = low(qkv[:, 2])
        attended = low(low_back(attend(queries, keys, values).reshape(TOKENS, D)))
        h_two = low(norm_rows(x, g_two, s_two))
        pre = low_back(product(h_two, w_in) + b_in.reshape(FF))
        act = low(gelu_exact(pre))
        branch = low_back(product(attended, w_dense) + b_dense + product(act, w_out) + b_out)
        return x + branch
    f32 = jnp.float32
    match = subset_ids[:, None] == jnp.arange(SUBSETS, dtype=jnp.int32)[None, :]
    counts = lax.optimization_barrier(jnp.sum(match.astype(f32), axis=0))
    table = TOKENS / (SUBSETS * counts)
    row_scale = lax.optimization_barrier(jnp.sum(jnp.where(match, table[None, :], 0.0), axis=1))
    mixed, pull = jax.vjp(forward, tokens.astype(f32), qkv_weight.astype(f32), qkv_bias.astype(f32), dense_weight.astype(f32), dense_bias.astype(f32), fc_in_weight.astype(f32), fc_in_bias.astype(f32), fc_out_weight.astype(f32), fc_out_bias.astype(f32), norm1_gain.astype(f32), norm1_shift.astype(f32), norm2_gain.astype(f32), norm2_shift.astype(f32))
    grads = pull(cotangent.astype(f32) * row_scale[:, None])
    return (mixed.astype(jnp.bfloat16), grads[0].astype(jnp.bfloat16), grads[1], grads[2], grads[3], grads[4], grads[5], grads[6], grads[7], grads[8], grads[9], grads[10], grads[11], grads[12])
```

```python
import math

import jax
import jax.numpy as jnp
from jax import lax
from jax.sharding import PartitionSpec as P

HDIM = 256
ROT = 64
SUBSETS = 22
SEQ_LEN = 2048
EPS = 1e-05
F32 = jnp.float32
BF16 = jnp.bfloat16


def mm(left, right, dims):
    return lax.dot_general(left, right, (dims, ((), ())), preferred_element_type=F32)


def plain(left, right):
    return mm(left, right, ((1,), (0,)))


def inner(left, right):
    return mm(left, right, ((0,), (0,)))


def against(left, right):
    return mm(left, right, ((1,), (1,)))


def rotary_tables(positions):
    half = ROT // 2
    steps = jnp.arange(half, dtype=F32)
    freq = 1.0 / 10000.0 ** (steps * 2.0 / ROT)
    angle = positions[:, None] * freq[None, :]
    return jnp.cos(angle), jnp.sin(angle)


def rotate(values, cosine, sine):
    half = ROT // 2
    first = values[..., :half]
    second = values[..., half:ROT]
    return jnp.concatenate(
        [first * cosine - second * sine, second * cosine + first * sine, values[..., ROT:]], axis=-1
    )


def locate(indices, starts):
    above = indices[:, None] >= starts[None, :]
    doc_ids = jnp.sum(above.astype(jnp.int32), axis=1) - 1
    pick = doc_ids[:, None] == jnp.arange(starts.shape[0], dtype=jnp.int32)[None, :]
    first = jnp.sum(jnp.where(pick, starts[None, :], 0), axis=1)
    return (doc_ids, (indices - first).astype(F32))


def swap(value):
    count = lax.axis_size("fsdp")
    return lax.ppermute(value, "fsdp", [(s, s ^ 1) for s in range(count)])


def planes(value, steps, reach=None):
    count = lax.axis_size("fsdp")
    pairs = []
    for s in range(count):
        d = s + 2 * steps
        if 0 <= d < count:
            if reach is None or 0 <= s + 2 * reach < count:
                pairs.append((s, d))
    return lax.ppermute(value, "fsdp", pairs)


def gather_planes(chunk, d, dp):
    ups, downs = [chunk], [chunk]
    for _ in range(dp - 1):
        ups.append(planes(ups[-1], 1))
        downs.append(planes(downs[-1], -1))
    rows = chunk.shape[0]
    full = jnp.zeros((dp * rows, chunk.shape[1]), chunk.dtype)
    for s in range(dp):
        piece = chunk if s == 0 else jnp.where(d >= s, ups[s], downs[dp - s])
        full = lax.dynamic_update_slice_in_dim(full, piece, lax.rem(d - s + dp, dp) * rows, 0)
    return full


def reduce_planes(parts, d, dp):
    rows = parts.shape[0] // dp

    def block(k):
        where = jnp.clip(d + k, 0, dp - 1) * rows
        return lax.dynamic_slice_in_dim(parts, where, rows, 0).astype(F32)

    total = block(0)
    for sign in (1, -1):
        held = None
        for s in range(dp - 1):
            k = sign * (dp - 1 - s)
            value = block(k) if held is None else block(k) + held.astype(F32)
            held = planes(value.astype(BF16), sign, k)
        if held is not None:
            total = total + held.astype(F32)
    return total


def tp_scatter(value, t, count):
    rows, cols = value.shape
    part = cols // count
    value = value.reshape(rows, count, part)
    bit = 1
    while bit < count:
        n = value.shape[1]
        view = value.reshape(rows, n // 2, 2, part)
        mine = lax.rem(t // bit, 2)
        keep = lax.dynamic_index_in_dim(view, mine, 2, keepdims=False)
        send = lax.dynamic_index_in_dim(view, 1 - mine, 2, keepdims=False)
        got = lax.ppermute(send.astype(BF16), "tp", [(s, s ^ bit) for s in range(count)])
        value = keep.astype(F32) + got.astype(F32)
        bit *= 2
    return value.reshape(rows, part)


def tp_sum(value, count):
    bit = 1
    while bit < count:
        value = value + lax.ppermute(value, "tp", [(s, s ^ bit) for s in range(count)])
        bit *= 2
    return value


def half_of(value, which, axis):
    size = value.shape[axis] // 2
    return lax.dynamic_slice_in_dim(value, which * size, size, axis)


def pair_rows(value, i):
    got = swap(value)
    return jnp.where(i == 0, jnp.concatenate([value, got], 0), jnp.concatenate([got, value], 0))


def on_device(
    tokens,
    qkv_weight,
    qkv_bias,
    dense_weight,
    dense_bias,
    fc_in_weight,
    fc_in_bias,
    fc_out_weight,
    fc_out_bias,
    norm1_gain,
    norm1_shift,
    norm2_gain,
    norm2_shift,
    cotangent,
    subset_ids,
    seq_starts,
):
    rows, width = tokens.shape
    shards = lax.axis_size("fsdp")
    tps = lax.axis_size("tp")
    dp = shards // 2
    f = lax.axis_index("fsdp")
    t = lax.axis_index("tp")
    i = lax.rem(f, 2)
    d = f // 2
    total = rows * shards
    scale = 1.0 / math.sqrt(HDIM)
    feats = qkv_weight.shape[0]
    units = fc_in_weight.shape[1]
    head_cols = qkv_weight.shape[2]
    heads_here = head_cols // HDIM
    hd = qkv_bias.shape[2]
    ub = fc_in_bias.shape

    match = subset_ids[:, None] == jnp.arange(SUBSETS, dtype=jnp.int32)[None, :]
    counts = jnp.sum(match.astype(F32), axis=0)
    vecs = [norm1_gain, norm1_shift, norm2_gain, norm2_shift, dense_bias, fc_out_bias]
    pack = jnp.concatenate(
        [v.astype(F32) for v in vecs]
        + [qkv_bias.astype(F32).reshape(-1), fc_in_bias.astype(F32).reshape(-1), counts]
    )
    got = lax.all_gather(pack, "fsdp", axis=0, tiled=False)
    gain1, shift1, gain2, shift2, b_dense, b_out = [
        got[:, k * feats : (k + 1) * feats].reshape(width) for k in range(6)
    ]
    at = 6 * feats
    nq = 3 * heads_here * hd
    b_qkv = got[:, at : at + nq].reshape(shards, 3, heads_here, hd)
    b_qkv = b_qkv.transpose(1, 2, 0, 3).reshape(3, heads_here, HDIM)
    b_qkv = lax.dynamic_index_in_dim(b_qkv, i, 1, keepdims=False).reshape(3 * HDIM)
    at += nq
    b_in = got[:, at : at + units // shards].reshape(shards, ub[0], ub[1])
    b_in = half_of(b_in.transpose(1, 0, 2).reshape(units), i, 0)
    at += units // shards
    counts = jnp.sum(got[:, at:], axis=0)
    table = total / (SUBSETS * counts)
    row_scale = jnp.sum(jnp.where(match, table[None, :], 0.0), axis=1)
    carried = cotangent.astype(F32) * row_scale[:, None]
    grad_here = carried.astype(BF16)

    wq = qkv_weight.reshape(feats, 3, heads_here, HDIM)
    wi = fc_in_weight.reshape(feats, 2, units // 2)
    wo = fc_out_weight.T.reshape(feats, 2, units // 2)
    wd = dense_weight.T.reshape(feats, 2, HDIM)

    def halves(which):
        pick = lambda v, ax: lax.dynamic_index_in_dim(v, which, ax, keepdims=False)
        return (
            jnp.concatenate([pick(wq, 2).reshape(feats, 3 * HDIM), pick(wd, 1)], axis=1),
            pick(wi, 1),
            pick(wo, 1),
        )

    x_b = pair_rows(tokens, i)
    mine, theirs = halves(i), halves(1 - i)
    full = []
    for own, other in zip(mine, theirs):
        back = swap(other)
        chunk = jnp.where(i == 0, jnp.concatenate([own, back], 0), jnp.concatenate([back, own], 0))
        full.append(gather_planes(chunk, d, dp))
    w_att, w_in, w_out = full
    w_qkv, w_dense = w_att[:, : 3 * HDIM], w_att[:, 3 * HDIM :]
    grad_b = pair_rows(grad_here, i)

    plane = 2 * rows
    start_row = d * plane
    x = x_b.astype(F32)
    mean = jnp.mean(x, axis=-1, keepdims=True)
    centred = x - mean
    spread = jnp.mean(centred * centred, axis=-1, keepdims=True)
    rstd = lax.rsqrt(spread + EPS)
    xhat = centred * rstd
    h_one = (xhat * gain1 + shift1).astype(BF16)
    h_two = (xhat * gain2 + shift2).astype(BF16)

    here = start_row + jnp.arange(plane, dtype=jnp.int32)
    docs_here, pos_here = locate(here, seq_starts)
    cosine, sine = rotary_tables(pos_here)
    qkv = plain(h_one, w_qkv) + b_qkv
    q = rotate(qkv[:, :HDIM], cosine, sine).astype(BF16)
    k = rotate(qkv[:, HDIM : 2 * HDIM], cosine, sine).astype(BF16)
    v = qkv[:, 2 * HDIM :].astype(BF16)
    reach = min(dp - 1, -(-(SEQ_LEN - 1) // plane))
    packed = jnp.concatenate([k, v], axis=1)
    window = [packed]
    for _ in range(reach):
        window.insert(0, planes(window[0], 1))
    window = jnp.concatenate(window, axis=0)
    span = window.shape[0]
    cols = start_row - reach * plane + jnp.arange(span, dtype=jnp.int32)
    docs_cols, _ = locate(cols, seq_starts)
    allowed = (cols[None, :] <= here[:, None]) & (docs_cols[None, :] == docs_here[:, None])
    key_win, value_win = window[:, :HDIM], window[:, HDIM:]
    masked = jnp.where(allowed, against(q, key_win) * scale, -1e30)
    top = jnp.max(masked, axis=1, keepdims=True)
    expo = jnp.exp(masked - top)
    probs = expo / jnp.sum(expo, axis=1, keepdims=True)
    probs_b = probs.astype(BF16)
    att_b = plain(probs_b, value_win).astype(BF16)

    pre = plain(h_two, w_in) + b_in
    act, gelu_pull = jax.vjp(lambda u: jax.nn.gelu(u, approximate=False), pre)
    act_b = act.astype(BF16)
    d_pre = gelu_pull(plain(grad_b, w_out))[0].astype(BF16)

    d_att = plain(grad_b, w_dense).astype(BF16)
    dprob = against(d_att, value_win)
    delta = jnp.sum(probs * dprob, axis=1, keepdims=True)
    dscore = (probs * (dprob - delta)).astype(BF16)
    dq = plain(dscore, key_win) * scale
    dk_win = inner(dscore, q) * scale
    dv_win = inner(probs_b, d_att)
    grads_win = jnp.concatenate([dk_win, dv_win], axis=1)
    held = None
    for r in range(reach):
        piece = grads_win[r * plane : (r + 1) * plane]
        moved = piece if held is None else piece + held
        held = planes(moved.astype(BF16), -1).astype(F32)
    dkv = grads_win[reach * plane :]
    if held is not None:
        dkv = dkv + held
    dq_raw = rotate(dq, cosine, -sine)
    dk_raw = rotate(dkv[:, :HDIM], cosine, -sine)
    d_qkv = jnp.concatenate([dq_raw, dk_raw, dkv[:, HDIM:]], axis=1).astype(BF16)

    partial_value = against(att_b, w_dense) + against(act_b, w_out)
    share = tp_scatter(partial_value, t, tps)
    share = half_of(share, i, 0) + swap(half_of(share, 1 - i, 0).astype(BF16)).astype(F32)
    part_w = width // tps
    offset = t * part_w
    cut = lambda vec: lax.dynamic_slice_in_dim(vec, offset, part_w, vec.ndim - 1)
    mixed = (cut(tokens).astype(F32) + share + cut(b_dense) + cut(b_out)).astype(BF16)

    g_out = reduce_planes(inner(grad_b, act_b), d, dp)
    g_in = reduce_planes(inner(h_two, d_pre), d, dp)
    g_att = reduce_planes(
        jnp.concatenate([inner(h_one, d_qkv), inner(grad_b, att_b)], axis=1), d, dp
    )
    e_two = against(d_pre, w_in)
    e_one = against(d_qkv, w_qkv)
    u = e_one * gain1 + e_two * gain2
    u_here = tp_scatter(u, t, tps)
    u_here = half_of(u_here, i, 0) + swap(half_of(u_here, 1 - i, 0).astype(BF16)).astype(F32)
    xhat_here = cut(half_of(xhat, i, 0))
    sums = jnp.stack([jnp.sum(u_here, axis=1), jnp.sum(u_here * xhat_here, axis=1)])
    sums = tp_sum(sums, tps) / width
    dx = half_of(rstd, i, 0) * (u_here - sums[0][:, None] - xhat_here * sums[1][:, None])
    tokens_grad = (cut(carried) + dx).astype(BF16)

    def pair_back(grad):
        own = half_of(grad, i, 0)
        got = swap(half_of(grad, 1 - i, 0).astype(BF16)).astype(F32)
        return jnp.where(i == 0, jnp.stack([own, got], 1), jnp.stack([got, own], 1))

    g_att, g_in, g_out = pair_back(g_att), pair_back(g_in), pair_back(g_out)
    qkv_weight_grad = (
        g_att[:, :, : 3 * HDIM].reshape(feats, 2, 3, HDIM).transpose(0, 2, 1, 3).reshape(feats, 3, head_cols)
    )
    dense_weight_grad = g_att[:, :, 3 * HDIM :].reshape(feats, head_cols).T
    fc_in_weight_grad = g_in.reshape(feats, units)
    fc_out_weight_grad = g_out.reshape(feats, units).T

    norms = jnp.stack(
        [
            jnp.sum(e_one * xhat, axis=0),
            jnp.sum(e_one, axis=0),
            jnp.sum(e_two * xhat, axis=0),
            jnp.sum(e_two, axis=0),
            jnp.sum(grad_here.astype(F32), axis=0),
        ]
    )
    norms = norms.reshape(5, shards, feats).transpose(1, 0, 2).reshape(shards, 5 * feats)
    in_b = jnp.where(jnp.arange(2)[:, None] == i, jnp.sum(d_pre.astype(F32), axis=0)[None], 0.0)
    in_b = in_b.reshape(ub[0], shards, ub[1]).transpose(1, 0, 2).reshape(shards, ub[0] * ub[1])
    qkv_b = jnp.sum(d_qkv.astype(F32), axis=0).reshape(3, 1, HDIM)
    qkv_b = jnp.where(jnp.arange(2)[None, :, None] == i, qkv_b, 0.0)
    qkv_b = qkv_b.reshape(3, 2, shards, hd).transpose(2, 0, 1, 3).reshape(shards, nq)
    small = jnp.concatenate([norms, in_b, qkv_b], axis=1)
    small = lax.psum_scatter(small, "fsdp", scatter_dimension=0, tiled=False)
    norm_grads = tp_sum(small[: 4 * feats].reshape(4, feats), tps)
    bias_grad = small[4 * feats : 5 * feats]
    in_bias_grad = small[5 * feats : 5 * feats + ub[0] * ub[1]].reshape(ub)
    qkv_bias_grad = small[5 * feats + ub[0] * ub[1] :].reshape(3, heads_here, hd)
    return (
        mixed,
        tokens_grad,
        qkv_weight_grad,
        qkv_bias_grad,
        dense_weight_grad,
        bias_grad,
        fc_in_weight_grad,
        in_bias_grad,
        fc_out_weight_grad,
        bias_grad,
        norm_grads[0],
        norm_grads[1],
        norm_grads[2],
        norm_grads[3],
    )


def solution(mesh):
    in_specs = (
        P("fsdp", None),
        P("fsdp", None, "tp"),
        P(None, "tp", "fsdp"),
        P("tp", "fsdp"),
        P("fsdp"),
        P("fsdp", "tp"),
        P("tp", "fsdp"),
        P("tp", "fsdp"),
        P("fsdp"),
        P("fsdp"),
        P("fsdp"),
        P("fsdp"),
        P("fsdp"),
        P("fsdp", None),
        P("fsdp"),
        P(),
    )
    out_specs = (
        P("fsdp", "tp"),
        P("fsdp", "tp"),
        P("fsdp", None, "tp"),
        P(None, "tp", "fsdp"),
        P("tp", "fsdp"),
        P("fsdp"),
        P("fsdp", "tp"),
        P("tp", "fsdp"),
        P("tp", "fsdp"),
        P("fsdp"),
        P("fsdp"),
        P("fsdp"),
        P("fsdp"),
        P("fsdp"),
    )
    return jax.shard_map(
        on_device, mesh=mesh, in_specs=in_specs, out_specs=out_specs, check_vma=False
    )
```

```python
import functools
import math

import jax
import jax.numpy as jnp
from jax import lax
from jax.experimental import pallas as pl
from jax.experimental.pallas import tpu as pltpu
from jax.sharding import PartitionSpec as P

HDIM = 256
ROT = 64
SUBSETS = 22
SEQ_LEN = 2048
EPS = 1e-05
F32 = jnp.float32
BF16 = jnp.bfloat16
MESH = pl.DeviceIdType.MESH
ANY = pl.BlockSpec(memory_space=pl.ANY)
VMEM = pl.BlockSpec(memory_space=pltpu.VMEM)


def mm(left, right, dims):
    return lax.dot_general(left, right, (dims, ((), ())), preferred_element_type=F32)


def plain(left, right):
    return mm(left, right, ((1,), (0,)))


def inner(left, right):
    return mm(left, right, ((0,), (0,)))


def against(left, right):
    return mm(left, right, ((1,), (1,)))


def rotary_tables(positions):
    half = ROT // 2
    steps = jnp.arange(half, dtype=F32)
    freq = 1.0 / 10000.0 ** (steps * 2.0 / ROT)
    angle = positions[:, None] * freq[None, :]
    return jnp.cos(angle), jnp.sin(angle)


def locate(indices, starts):
    above = indices[:, None] >= starts[None, :]
    doc_ids = jnp.sum(above.astype(jnp.int32), axis=1) - 1
    pick = doc_ids[:, None] == jnp.arange(starts.shape[0], dtype=jnp.int32)[None, :]
    first = jnp.sum(jnp.where(pick, starts[None, :], 0), axis=1)
    return (doc_ids, (indices - first).astype(F32))


def swap(value):
    count = lax.axis_size("fsdp")
    return lax.ppermute(value, "fsdp", [(s, s ^ 1) for s in range(count)])


def planes(value, steps, reach=None):
    count = lax.axis_size("fsdp")
    pairs = []
    for s in range(count):
        d = s + 2 * steps
        if 0 <= d < count:
            if reach is None or 0 <= s + 2 * reach < count:
                pairs.append((s, d))
    return lax.ppermute(value, "fsdp", pairs)


def reduce_planes(parts, d, dp):
    rows = parts.shape[0] // dp

    def block(k):
        where = jnp.clip(d + k, 0, dp - 1) * rows
        return lax.dynamic_slice_in_dim(parts, where, rows, 0).astype(F32)

    total = block(0)
    for sign in (1, -1):
        held = None
        for s in range(dp - 1):
            k = sign * (dp - 1 - s)
            value = block(k) if held is None else block(k) + held.astype(F32)
            held = planes(value.astype(BF16), sign, k)
        if held is not None:
            total = total + held.astype(F32)
    return total


def tp_scatter(value, t, count):
    rows, cols = value.shape
    part = cols // count
    value = value.reshape(rows, count, part)
    bit = 1
    while bit < count:
        n = value.shape[1]
        view = value.reshape(rows, n // 2, 2, part)
        mine = lax.rem(t // bit, 2)
        keep = lax.dynamic_index_in_dim(view, mine, 2, keepdims=False)
        send = lax.dynamic_index_in_dim(view, 1 - mine, 2, keepdims=False)
        got = lax.ppermute(send.astype(BF16), "tp", [(s, s ^ bit) for s in range(count)])
        value = keep.astype(F32) + got.astype(F32)
        bit *= 2
    return value.reshape(rows, part)


def tp_sum(value, count):
    bit = 1
    while bit < count:
        value = value + lax.ppermute(value, "tp", [(s, s ^ bit) for s in range(count)])
        bit *= 2
    return value


def half_of(value, which, axis):
    size = value.shape[axis] // 2
    return lax.dynamic_slice_in_dim(value, which * size, size, axis)


def exchange_kernel(axis, spread, v_ref, o_ref, ssem, rsem):
    count = o_ref.shape[0]
    me = lax.axis_index(axis)

    def peer(step):
        return lax.rem(me + step, count)

    barrier = pltpu.get_barrier_semaphore()
    for step in range(1, count):
        pl.semaphore_signal(barrier, 1, device_id={axis: peer(step)}, device_id_type=MESH)
    pl.semaphore_wait(barrier, count - 1)

    def copy(step):
        return pltpu.make_async_remote_copy(
            src_ref=v_ref.at[peer(step)] if spread else v_ref,
            dst_ref=o_ref.at[me],
            send_sem=ssem.at[step],
            recv_sem=rsem.at[step],
            device_id={axis: peer(step)},
            device_id_type=MESH,
        )

    for step in range(1, count):
        copy(step).start()
    o_ref[me] = v_ref[me] if spread else v_ref[...]
    for step in range(1, count):
        copy(step).wait()


def exchange(value, axis, spread, cid):
    count = lax.axis_size(axis)
    block = value.shape[1:] if spread else value.shape
    return pl.pallas_call(
        functools.partial(exchange_kernel, axis, spread),
        out_shape=jax.ShapeDtypeStruct((count,) + block, value.dtype),
        in_specs=[VMEM],
        out_specs=VMEM,
        scratch_shapes=[pltpu.SemaphoreType.DMA((count,)), pltpu.SemaphoreType.DMA((count,))],
        compiler_params=pltpu.CompilerParams(collective_id=cid, has_side_effects=True),
        name="exchange",
    )(value)


GROUPS = 3


def attend_kernel(
    dims,
    tok, gh, w2, vecs, bq, tabs, first,
    x_o, g_o, wa_o, wi_o, wo_o, att_o, dqkv_o,
    xs, h1s, was, gs, win, qs, das, acc, down,
    rcv, lsem, tsem, psem, zsem, zrec, ksem, dsem,
):
    R, D, feats, dp, reach = dims
    f = lax.axis_index("fsdp")
    t = lax.axis_index("tp")
    d, i = f // 2, lax.rem(f, 2)
    core = lax.rem(t, 2)
    plane = 2 * R
    qb = min(256, plane)
    nb = plane // qb
    mate = (f + 1 - 2 * i, t)
    near = (f, t + 1 - 2 * core)
    dirs = ((f + 2, t), (f - 2, t))
    has = (d + 1 < dp, d >= 1)
    outs = (wa_o, wi_o, wo_o)
    gw = w2.shape[2] // GROUPS

    barrier = pltpu.get_barrier_semaphore()
    for who in (mate, near):
        pl.semaphore_signal(barrier, 1, device_id=who, device_id_type=MESH)
    for k in range(2):
        @pl.when(has[k])
        def _():
            pl.semaphore_signal(barrier, 1, device_id=dirs[k], device_id_type=MESH)
    pl.semaphore_wait(barrier, 2 + has[0].astype(jnp.int32) + has[1].astype(jnp.int32))

    def rc(src, dst, ssem, rsem, who):
        return pltpu.make_async_remote_copy(
            src_ref=src, dst_ref=dst, send_sem=ssem, recv_sem=rsem, device_id=who, device_id_type=MESH
        )

    def slot(g, s):
        return outs[g].at[pl.ds(s * feats, feats), :]

    def part(half, g):
        return w2.at[half, :, pl.ds(g * gw, gw)]

    def pair_copy(g):
        return rc(part(1 - i, g), slot(g, f), psem.at[0, g], psem.at[1, g], mate)

    def own_copy(g):
        return pltpu.make_async_copy(part(i, g), slot(g, f), lsem.at[g])

    def z_own(g, way):
        return rc(part(i, g), slot(g, f), zsem.at[g, 0, way, 0], zrec.at[g, f], dirs[way])

    def z_mate(g, way):
        s = f + 1 - 2 * i
        return rc(slot(g, s), slot(g, s), zsem.at[g, 0, way, 1], zrec.at[g, s], dirs[way])

    def z_fwd(g, k, way, j):
        s = (d - k) * 2 + j if way == 0 else (d + k) * 2 + j
        return rc(slot(g, s), slot(g, s), zsem.at[g, k, way, j], zrec.at[g, s], dirs[way])

    def send_own(g):
        for way in range(2):
            @pl.when(has[way])
            def _():
                z_own(g, way).start()

    def send_mate(g):
        pair_copy(g).wait_recv()
        for way in range(2):
            @pl.when(has[way])
            def _():
                z_mate(g, way).start()

    def from_dist(k, way):
        return d >= k if way == 0 else d + k < dp

    def arrive(g, k):
        for way in range(2):
            @pl.when(from_dist(k, way))
            def _():
                for j in range(2):
                    z_fwd(g, k, way, j).wait_recv()

                    @pl.when(has[way])
                    def _():
                        z_fwd(g, k, way, j).start()

    def finish(g):
        own_copy(g).wait()
        pair_copy(g).wait_send()
        for way in range(2):
            @pl.when(has[way])
            def _():
                z_own(g, way).wait_send()
                z_mate(g, way).wait_send()
            for k in range(1, dp - 1):
                @pl.when(from_dist(k, way) & has[way])
                def _():
                    for j in range(2):
                        z_fwd(g, k, way, j).wait_send()

    hr = R // 2

    def rows_x(a, ref, out):
        return rc(
            ref.at[pl.ds(core * hr, hr), :], out.at[pl.ds(i * R + core * hr, hr), :],
            tsem.at[a, 0], tsem.at[a, 1], mate,
        )

    def rows_c(a, out):
        at = out.at[pl.ds((1 - i) * R + core * hr, hr), :]
        return rc(at, at, tsem.at[a, 2], tsem.at[a, 3], near)

    def rows_own(a, ref, out):
        return pltpu.make_async_copy(ref, out.at[pl.ds(i * R, R), :], lsem.at[GROUPS + a])

    pair_copy(0).start()
    send_own(0)
    rows_x(0, tok, x_o).start()
    own_copy(0).start()
    rows_own(0, tok, x_o).start()
    rows_own(1, gh, g_o).start()
    send_mate(0)
    rows_x(1, gh, g_o).start()
    pair_copy(1).start()
    pair_copy(2).start()
    own_copy(1).start()
    own_copy(2).start()
    rows_x(0, tok, x_o).wait_recv()
    rows_c(0, x_o).start()
    send_own(1)
    rows_c(0, x_o).wait_recv()
    rows_own(0, tok, x_o).wait()
    load_x = pltpu.make_async_copy(x_o, xs, lsem.at[5])
    load_x.start()
    arrive(0, 1)
    load_x.wait()

    def norm_block(b, _):
        at = pl.ds(pl.multiple_of(b * qb, qb), qb)
        x = xs[at, :].astype(F32)
        mean = jnp.mean(x, axis=-1, keepdims=True)
        c = x - mean
        var = jnp.mean(c * c, axis=-1, keepdims=True)
        h1s[at, :] = (c * lax.rsqrt(var + EPS) * vecs[0:1, :] + vecs[1:2, :]).astype(BF16)
        return 0

    lax.fori_loop(0, nb // 2, norm_block, 0)
    for k in range(2, dp):
        arrive(0, k)
        if k == 2:
            send_mate(1)
    lax.fori_loop(nb // 2, nb, norm_block, 0)
    own_copy(0).wait()
    load_w = pltpu.make_async_copy(wa_o, was, lsem.at[5])
    load_w.start()
    rows_x(1, gh, g_o).wait_recv()
    rows_c(1, g_o).start()
    send_own(2)
    send_mate(2)
    arrive(1, 1)
    rows_c(1, g_o).wait_recv()
    rows_own(1, gh, g_o).wait()
    load_g = pltpu.make_async_copy(g_o, gs, lsem.at[6])
    load_g.start()
    load_w.wait()
    load_g.wait()

    def turn(u, at, sign):
        lo, hi = u[:, :128], u[:, 128:]
        a = pltpu.roll(lo, ROT // 2, 1) * tabs[1, at, :] + pltpu.roll(lo, 128 - ROT // 2, 1) * tabs[2, at, :]
        lo = lo * tabs[0, at, :] + (a if sign > 0 else -a)
        return jnp.concatenate([lo, hi], axis=1)

    scale = 1.0 / math.sqrt(HDIM)

    def proj_block(b, _):
        at = pl.ds(pl.multiple_of(b * qb, qb), qb)
        y = plain(h1s[at, :], was[:, : 3 * HDIM]) + bq[...]
        qs[at, :] = (turn(y[:, :HDIM], at, 1).astype(BF16).astype(F32) * scale).astype(BF16)
        win[reach, at, :HDIM] = turn(y[:, HDIM : 2 * HDIM], at, 1).astype(BF16)
        win[reach, at, HDIM:] = y[:, 2 * HDIM :].astype(BF16)
        das[at, :] = plain(gs[at, :], was[:, 3 * HDIM :]).astype(BF16)
        return 0

    lax.fori_loop(0, nb, proj_block, 0)

    def kv_copy(k):
        return rc(win.at[reach - k], win.at[reach - k - 1], ksem.at[0, k], ksem.at[1, k + 1], dirs[0])

    def kv_recv(k):
        return rc(win.at[reach - k], win.at[reach - k], ksem.at[0, k - 1], ksem.at[1, k], dirs[0])

    @pl.when(has[0])
    def _():
        kv_copy(0).start()

    arrive(2, 1)
    arrive(1, 2)
    for k in range(1, reach + 1):
        @pl.when(d >= k)
        def _():
            kv_recv(k).wait_recv()
            if k < reach:
                @pl.when(has[0])
                def _():
                    kv_copy(k).start()

        @pl.when(d < k)
        def _():
            win[reach - k] = jnp.zeros((plane, 2 * HDIM), BF16)

    acc[...] = jnp.zeros_like(acc)
    span = SEQ_LEN + qb
    base = reach * plane - SEQ_LEN

    def attend_block(b, _):
        at = pl.ds(pl.multiple_of(b * qb, qb), qb)
        keys_at = pl.ds(pl.multiple_of(base + b * qb, qb), span)
        flat = win.reshape((reach + 1) * plane, 2 * HDIM)
        keys = flat[keys_at, :HDIM]
        vals = flat[keys_at, HDIM:]
        q = qs[at, :]
        s = against(q, keys)
        c = base + b * qb + lax.broadcasted_iota(jnp.int32, (qb, span), 1)
        r = reach * plane + b * qb + lax.broadcasted_iota(jnp.int32, (qb, span), 0)
        s = jnp.where((c >= first[at, :]) & (c <= r), s, -1e30)
        e = jnp.exp(s - jnp.max(s, axis=1, keepdims=True))
        p = e * (1.0 / jnp.sum(e, axis=1, keepdims=True))
        pb = p.astype(BF16)
        att_o[at, :] = plain(pb, vals).astype(BF16)
        da = das[at, :]
        dpr = against(da, vals)
        delta = jnp.sum(p * dpr, axis=1, keepdims=True)
        ds = (p * (dpr - delta)).astype(BF16)
        dq = plain(ds, keys) * scale
        dqkv_o[at, :HDIM] = turn(dq, at, -1).astype(BF16)
        acc[keys_at, :HDIM] += inner(ds, q)
        acc[keys_at, HDIM:] += inner(pb, da)
        return 0

    lax.fori_loop(0, nb // 2, attend_block, 0)
    arrive(2, 2)
    for k in range(3, dp):
        arrive(1, k)
    lax.fori_loop(nb // 2, nb, attend_block, 0)

    def down_copy(r):
        return rc(down.at[r], rcv.at[r], dsem.at[0, r], dsem.at[1, r], dirs[1])

    for r in range(reach + 1):
        at = pl.ds(r * plane, plane)
        if r > 0:
            @pl.when(has[0])
            def _():
                down_copy(r - 1).wait_recv()
                acc[at, :] += rcv[r - 1].astype(F32)
        if r < reach:
            down[r] = acc[at, :].astype(BF16)

            @pl.when(has[1])
            def _():
                down_copy(r).start()
        else:
            def tail_block(b, _):
                here = pl.ds(pl.multiple_of(b * qb, qb), qb)
                a = acc[pl.ds(pl.multiple_of(reach * plane + b * qb, qb), qb), :]
                dqkv_o[here, HDIM : 2 * HDIM] = turn(a[:, :HDIM], here, -1).astype(BF16)
                dqkv_o[here, 2 * HDIM :] = a[:, HDIM:].astype(BF16)
                return 0

            lax.fori_loop(0, nb, tail_block, 0)
        if r == 0:
            for k in range(3, dp):
                arrive(2, k)

    for r in range(reach):
        @pl.when(has[1])
        def _():
            down_copy(r).wait_send()
    for k in range(reach):
        @pl.when((d >= k) & has[0])
        def _():
            kv_copy(k).wait_send()
    for g in range(GROUPS):
        if g == 0:
            pair_copy(g).wait_send()
            for way in range(2):
                @pl.when(has[way])
                def _():
                    z_own(g, way).wait_send()
                    z_mate(g, way).wait_send()
                for k in range(1, dp - 1):
                    @pl.when(from_dist(k, way) & has[way])
                    def _():
                        for j in range(2):
                            z_fwd(g, k, way, j).wait_send()
        else:
            finish(g)
    for a, (ref, out) in enumerate(((tok, x_o), (gh, g_o))):
        rows_x(a, ref, out).wait_send()
        rows_c(a, out).wait_send()


def attend(tok, gh, w2, vecs, bq, tabs, first, dims):
    R, D, feats, dp, reach = dims
    plane = 2 * R
    gw = w2.shape[2] // GROUPS
    sds = jax.ShapeDtypeStruct
    return pl.pallas_call(
        functools.partial(attend_kernel, dims),
        out_shape=[
            sds((plane, D), BF16), sds((plane, D), BF16),
            sds((D, gw), BF16), sds((D, gw), BF16), sds((D, gw), BF16),
            sds((plane, HDIM), BF16), sds((plane, 3 * HDIM), BF16),
        ],
        in_specs=[ANY, ANY, ANY, VMEM, VMEM, VMEM, VMEM],
        out_specs=[ANY] * 5 + [VMEM] * 2,
        scratch_shapes=[
            pltpu.VMEM((plane, D), BF16),
            pltpu.VMEM((plane, D), BF16),
            pltpu.VMEM((D, gw), BF16),
            pltpu.VMEM((plane, D), BF16),
            pltpu.VMEM((reach + 1, plane, 2 * HDIM), BF16),
            pltpu.VMEM((plane, HDIM), BF16),
            pltpu.VMEM((plane, HDIM), BF16),
            pltpu.VMEM(((reach + 1) * plane, 2 * HDIM), F32),
            pltpu.VMEM((reach, plane, 2 * HDIM), BF16),
            pltpu.VMEM((reach, plane, 2 * HDIM), BF16),
            pltpu.SemaphoreType.DMA((8,)),
            pltpu.SemaphoreType.DMA((2, 4)),
            pltpu.SemaphoreType.DMA((2, GROUPS)),
            pltpu.SemaphoreType.DMA((GROUPS, dp, 2, 2)),
            pltpu.SemaphoreType.DMA((GROUPS, 2 * dp)),
            pltpu.SemaphoreType.DMA((2, reach + 1)),
            pltpu.SemaphoreType.DMA((2, reach)),
        ],
        compiler_params=pltpu.CompilerParams(
            collective_id=4, has_side_effects=True, vmem_limit_bytes=62 << 20
        ),
        name="attend",
    )(tok, gh, w2, vecs, bq, tabs, first)


def on_device(
    tokens,
    qkv_weight,
    qkv_bias,
    dense_weight,
    dense_bias,
    fc_in_weight,
    fc_in_bias,
    fc_out_weight,
    fc_out_bias,
    norm1_gain,
    norm1_shift,
    norm2_gain,
    norm2_shift,
    cotangent,
    subset_ids,
    seq_starts,
):
    rows, width = tokens.shape
    shards = lax.axis_size("fsdp")
    tps = lax.axis_size("tp")
    dp = shards // 2
    f = lax.axis_index("fsdp")
    t = lax.axis_index("tp")
    i = lax.rem(f, 2)
    d = f // 2
    total = rows * shards
    scale = 1.0 / math.sqrt(HDIM)
    feats = qkv_weight.shape[0]
    units = fc_in_weight.shape[1]
    head_cols = qkv_weight.shape[2]
    heads_here = head_cols // HDIM
    hd = qkv_bias.shape[2]
    ub = fc_in_bias.shape

    match = subset_ids[:, None] == jnp.arange(SUBSETS, dtype=jnp.int32)[None, :]
    counts = jnp.sum(match.astype(F32), axis=0)
    vecs = [norm1_gain, norm1_shift, norm2_gain, norm2_shift, dense_bias, fc_out_bias]
    pack = jnp.concatenate(
        [v.astype(F32) for v in vecs]
        + [qkv_bias.astype(F32).reshape(-1), fc_in_bias.astype(F32).reshape(-1), counts]
    )
    size = pack.shape[0]
    lanes = -(-size // 1024) * 128
    got = exchange(jnp.pad(pack, (0, 8 * lanes - size)).reshape(8, lanes), "fsdp", False, 1)
    got = got.reshape(shards, 8 * lanes)
    gain1, shift1, gain2, shift2, b_dense, b_out = [
        got[:, k * feats : (k + 1) * feats].reshape(width) for k in range(6)
    ]
    at = 6 * feats
    nq = 3 * heads_here * hd
    b_qkv = got[:, at : at + nq].reshape(shards, 3, heads_here, hd)
    b_qkv = b_qkv.transpose(1, 2, 0, 3).reshape(3, heads_here, HDIM)
    b_qkv = lax.dynamic_index_in_dim(b_qkv, i, 1, keepdims=False).reshape(3 * HDIM)
    at += nq
    b_in = got[:, at : at + units // shards].reshape(shards, ub[0], ub[1])
    b_in = half_of(b_in.transpose(1, 0, 2).reshape(units), i, 0)
    at += units // shards
    counts = jnp.sum(got[:, at : at + SUBSETS], axis=0)
    table = total / (SUBSETS * counts)
    row_scale = jnp.sum(jnp.where(match, table[None, :], 0.0), axis=1)
    carried = cotangent.astype(F32) * row_scale[:, None]
    grad_here = carried.astype(BF16)

    w2 = jnp.concatenate(
        [
            qkv_weight.reshape(feats, 3, heads_here, HDIM).transpose(2, 0, 1, 3).reshape(2, feats, 3 * HDIM),
            dense_weight.reshape(heads_here, HDIM, feats).transpose(0, 2, 1),
            fc_in_weight.reshape(feats, 2, units // 2).transpose(1, 0, 2),
            fc_out_weight.reshape(2, units // 2, feats).transpose(0, 2, 1),
        ],
        axis=2,
    )
    plane = 2 * rows
    start_row = d * plane
    reach = min(dp - 1, -(-(SEQ_LEN - 1) // plane))
    here = start_row + jnp.arange(plane, dtype=jnp.int32)
    docs_here, pos_here = locate(here, seq_starts)
    first = (here - pos_here.astype(jnp.int32)) - (start_row - reach * plane)
    cosine, sine = rotary_tables(pos_here)
    ones = jnp.ones((plane, 128 - ROT), F32)
    none = jnp.zeros((plane, 128 - ROT), F32)
    zero = jnp.zeros_like(sine)
    tabs = jnp.stack(
        [
            jnp.concatenate([cosine, cosine, ones], 1),
            jnp.concatenate([zero, sine, none], 1),
            jnp.concatenate([-sine, zero, none], 1),
        ]
    )
    vecs = jnp.stack([gain1, shift1, gain2, shift2] + [jnp.zeros_like(gain1)] * 4)
    x_b, grad_b, w_att, w_in, w_out, att_b, d_qkv = attend(
        tokens, grad_here, w2, vecs, b_qkv.reshape(1, -1), tabs, first[:, None],
        (rows, width, feats, dp, reach),
    )
    w_qkv, w_dense = w_att[:, : 3 * HDIM], w_att[:, 3 * HDIM :]
    x = x_b.astype(F32)
    mean = jnp.mean(x, axis=-1, keepdims=True)
    centred = x - mean
    spread = jnp.mean(centred * centred, axis=-1, keepdims=True)
    rstd = lax.rsqrt(spread + EPS)
    xhat = centred * rstd
    h_one = (xhat * gain1 + shift1).astype(BF16)
    h_two = (xhat * gain2 + shift2).astype(BF16)

    pre = plain(h_two, w_in) + b_in
    act, gelu_pull = jax.vjp(lambda u: jax.nn.gelu(u, approximate=False), pre)
    act_b = act.astype(BF16)
    d_pre = gelu_pull(plain(grad_b, w_out))[0].astype(BF16)

    partial_value = against(att_b, w_dense) + against(act_b, w_out)
    share = tp_scatter(partial_value, t, tps)
    share = half_of(share, i, 0) + swap(half_of(share, 1 - i, 0).astype(BF16)).astype(F32)
    part_w = width // tps
    offset = t * part_w
    cut = lambda vec: lax.dynamic_slice_in_dim(vec, offset, part_w, vec.ndim - 1)
    mixed = (cut(tokens).astype(F32) + share + cut(b_dense) + cut(b_out)).astype(BF16)

    g_out = reduce_planes(inner(grad_b, act_b), d, dp)
    g_in = reduce_planes(inner(h_two, d_pre), d, dp)
    g_att = reduce_planes(
        jnp.concatenate([inner(h_one, d_qkv), inner(grad_b, att_b)], axis=1), d, dp
    )
    e_two = against(d_pre, w_in)
    e_one = against(d_qkv, w_qkv)
    u = e_one * gain1 + e_two * gain2
    u_here = tp_scatter(u, t, tps)
    u_here = half_of(u_here, i, 0) + swap(half_of(u_here, 1 - i, 0).astype(BF16)).astype(F32)
    xhat_here = cut(half_of(xhat, i, 0))
    sums = jnp.stack([jnp.sum(u_here, axis=1), jnp.sum(u_here * xhat_here, axis=1)])
    sums = tp_sum(sums, tps) / width
    dx = half_of(rstd, i, 0) * (u_here - sums[0][:, None] - xhat_here * sums[1][:, None])
    tokens_grad = (cut(carried) + dx).astype(BF16)

    def pair_back(grad):
        own = half_of(grad, i, 0)
        got = swap(half_of(grad, 1 - i, 0).astype(BF16)).astype(F32)
        return jnp.where(i == 0, jnp.stack([own, got], 1), jnp.stack([got, own], 1))

    g_att, g_in, g_out = pair_back(g_att), pair_back(g_in), pair_back(g_out)
    qkv_weight_grad = (
        g_att[:, :, : 3 * HDIM].reshape(feats, 2, 3, HDIM).transpose(0, 2, 1, 3).reshape(feats, 3, head_cols)
    )
    dense_weight_grad = g_att[:, :, 3 * HDIM :].reshape(feats, head_cols).T
    fc_in_weight_grad = g_in.reshape(feats, units)
    fc_out_weight_grad = g_out.reshape(feats, units).T

    norms = jnp.stack(
        [
            jnp.sum(e_one * xhat, axis=0),
            jnp.sum(e_one, axis=0),
            jnp.sum(e_two * xhat, axis=0),
            jnp.sum(e_two, axis=0),
            jnp.sum(grad_here.astype(F32), axis=0),
        ]
    )
    norms = norms.reshape(5, shards, feats).transpose(1, 0, 2).reshape(shards, 5 * feats)
    in_b = jnp.where(jnp.arange(2)[:, None] == i, jnp.sum(d_pre.astype(F32), axis=0)[None], 0.0)
    in_b = in_b.reshape(ub[0], shards, ub[1]).transpose(1, 0, 2).reshape(shards, ub[0] * ub[1])
    qkv_b = jnp.sum(d_qkv.astype(F32), axis=0).reshape(3, 1, HDIM)
    qkv_b = jnp.where(jnp.arange(2)[None, :, None] == i, qkv_b, 0.0)
    qkv_b = qkv_b.reshape(3, 2, shards, hd).transpose(2, 0, 1, 3).reshape(shards, nq)
    small = jnp.concatenate([norms, in_b, qkv_b], axis=1)
    size = small.shape[1]
    lanes = -(-size // 1024) * 128
    small = jnp.pad(small, ((0, 0), (0, 8 * lanes - size))).reshape(shards, 8, lanes)
    small = jnp.sum(exchange(small, "fsdp", True, 2), axis=0).reshape(8 * lanes)
    norm_grads = small[: 4 * feats].reshape(8, feats // 2)
    norm_grads = jnp.sum(exchange(norm_grads, "tp", False, 3), axis=0).reshape(4, feats)
    bias_grad = small[4 * feats : 5 * feats]
    in_bias_grad = small[5 * feats : 5 * feats + ub[0] * ub[1]].reshape(ub)
    at = 5 * feats + ub[0] * ub[1]
    qkv_bias_grad = small[at : at + nq].reshape(3, heads_here, hd)
    return (
        mixed,
        tokens_grad,
        qkv_weight_grad,
        qkv_bias_grad,
        dense_weight_grad,
        bias_grad,
        fc_in_weight_grad,
        in_bias_grad,
        fc_out_weight_grad,
        bias_grad,
        norm_grads[0],
        norm_grads[1],
        norm_grads[2],
        norm_grads[3],
    )


def solution(mesh):
    in_specs = (
        P("fsdp", None),
        P("fsdp", None, "tp"),
        P(None, "tp", "fsdp"),
        P("tp", "fsdp"),
        P("fsdp"),
        P("fsdp", "tp"),
        P("tp", "fsdp"),
        P("tp", "fsdp"),
        P("fsdp"),
        P("fsdp"),
        P("fsdp"),
        P("fsdp"),
        P("fsdp"),
        P("fsdp", None),
        P("fsdp"),
        P(),
    )
    out_specs = (
        P("fsdp", "tp"),
        P("fsdp", "tp"),
        P("fsdp", None, "tp"),
        P(None, "tp", "fsdp"),
        P("tp", "fsdp"),
        P("fsdp"),
        P("fsdp", "tp"),
        P("tp", "fsdp"),
        P("tp", "fsdp"),
        P("fsdp"),
        P("fsdp"),
        P("fsdp"),
        P("fsdp"),
        P("fsdp"),
    )
    return jax.shard_map(
        on_device, mesh=mesh, in_specs=in_specs, out_specs=out_specs, check_vma=False
    )
```

```python
import functools
import math

import jax
import jax.numpy as jnp
from jax import lax
from jax.experimental import pallas as pl
from jax.experimental.pallas import tpu as pltpu
from jax.sharding import PartitionSpec as P

HDIM = 256
ROT = 64
SUBSETS = 22
SEQ_LEN = 2048
EPS = 1e-05
F32 = jnp.float32
BF16 = jnp.bfloat16
MESH = pl.DeviceIdType.MESH
ANY = pl.BlockSpec(memory_space=pl.ANY)
VMEM = pl.BlockSpec(memory_space=pltpu.VMEM)


def mm(left, right, dims):
    return lax.dot_general(left, right, (dims, ((), ())), preferred_element_type=F32)


def plain(left, right):
    return mm(left, right, ((1,), (0,)))


def inner(left, right):
    return mm(left, right, ((0,), (0,)))


def against(left, right):
    return mm(left, right, ((1,), (1,)))


def rotary_tables(positions):
    half = ROT // 2
    steps = jnp.arange(half, dtype=F32)
    freq = 1.0 / 10000.0 ** (steps * 2.0 / ROT)
    angle = positions[:, None] * freq[None, :]
    return jnp.cos(angle), jnp.sin(angle)


def locate(indices, starts):
    above = indices[:, None] >= starts[None, :]
    doc_ids = jnp.sum(above.astype(jnp.int32), axis=1) - 1
    pick = doc_ids[:, None] == jnp.arange(starts.shape[0], dtype=jnp.int32)[None, :]
    first = jnp.sum(jnp.where(pick, starts[None, :], 0), axis=1)
    return (doc_ids, (indices - first).astype(F32))


def half_of(value, which, axis):
    size = value.shape[axis] // 2
    return lax.dynamic_slice_in_dim(value, which * size, size, axis)


def exchange_kernel(axis, spread, v_ref, o_ref, ssem, rsem):
    count = o_ref.shape[0]
    me = lax.axis_index(axis)

    def peer(step):
        return lax.rem(me + step, count)

    barrier = pltpu.get_barrier_semaphore()
    for step in range(1, count):
        pl.semaphore_signal(barrier, 1, device_id={axis: peer(step)}, device_id_type=MESH)
    pl.semaphore_wait(barrier, count - 1)

    def copy(step):
        return pltpu.make_async_remote_copy(
            src_ref=v_ref.at[peer(step)] if spread else v_ref,
            dst_ref=o_ref.at[me],
            send_sem=ssem.at[step],
            recv_sem=rsem.at[step],
            device_id={axis: peer(step)},
            device_id_type=MESH,
        )

    for step in range(1, count):
        copy(step).start()
    o_ref[me] = v_ref[me] if spread else v_ref[...]
    for step in range(1, count):
        copy(step).wait()


def exchange(value, axis, spread, cid):
    count = lax.axis_size(axis)
    block = value.shape[1:] if spread else value.shape
    return pl.pallas_call(
        functools.partial(exchange_kernel, axis, spread),
        out_shape=jax.ShapeDtypeStruct((count,) + block, value.dtype),
        in_specs=[VMEM],
        out_specs=VMEM,
        scratch_shapes=[pltpu.SemaphoreType.DMA((count,)), pltpu.SemaphoreType.DMA((count,))],
        compiler_params=pltpu.CompilerParams(collective_id=cid, has_side_effects=True),
        name="exchange",
    )(value)


GROUPS = 3


def turn(u, tabs, at, sign):
    lo, hi = u[:, :128], u[:, 128:]
    a = pltpu.roll(lo, ROT // 2, 1) * tabs[1, at, :] + pltpu.roll(lo, 128 - ROT // 2, 1) * tabs[2, at, :]
    lo = lo * tabs[0, at, :] + (a if sign > 0 else -a)
    return jnp.concatenate([lo, hi], axis=1)


def attend_kernel(
    dims,
    tok, gh, w2, vecs, bq, tabs, first,
    x_o, g_o, wa_o, wi_o, wo_o, att_o, dq_o, dwin_o,
    xs, h1s, was, gs, win, qs, das, acc, lsem, tsem, psem, zsem, zrec, ksem,
):
    R, D, feats, dp, reach = dims
    f = lax.axis_index("fsdp")
    t = lax.axis_index("tp")
    d, i = f // 2, lax.rem(f, 2)
    core = lax.rem(t, 2)
    plane = 2 * R
    qb = min(256, plane)
    nb = plane // qb
    mate = (f + 1 - 2 * i, t)
    near = (f, t + 1 - 2 * core)
    dirs = ((f + 2, t), (f - 2, t))
    has = (d + 1 < dp, d >= 1)
    outs = (wa_o, wi_o, wo_o)
    gw = w2.shape[2] // GROUPS

    barrier = pltpu.get_barrier_semaphore()
    for who in (mate, near):
        pl.semaphore_signal(barrier, 1, device_id=who, device_id_type=MESH)
    for k in range(2):
        @pl.when(has[k])
        def _():
            pl.semaphore_signal(barrier, 1, device_id=dirs[k], device_id_type=MESH)
    pl.semaphore_wait(barrier, 2 + has[0].astype(jnp.int32) + has[1].astype(jnp.int32))

    def rc(src, dst, ssem, rsem, who):
        return pltpu.make_async_remote_copy(
            src_ref=src, dst_ref=dst, send_sem=ssem, recv_sem=rsem, device_id=who, device_id_type=MESH
        )

    def slot(g, s):
        return outs[g].at[pl.ds(s * feats, feats), :]

    def part(half, g):
        return w2.at[half, :, pl.ds(g * gw, gw)]

    def pair_copy(g):
        return rc(part(1 - i, g), slot(g, f), psem.at[0, g], psem.at[1, g], mate)

    def own_copy(g):
        return pltpu.make_async_copy(part(i, g), slot(g, f), lsem.at[g])

    def z_own(g, way):
        return rc(part(i, g), slot(g, f), zsem.at[g, 0, way, 0], zrec.at[g, f], dirs[way])

    def z_mate(g, way):
        s = f + 1 - 2 * i
        return rc(slot(g, s), slot(g, s), zsem.at[g, 0, way, 1], zrec.at[g, s], dirs[way])

    def z_fwd(g, k, way, j):
        s = (d - k) * 2 + j if way == 0 else (d + k) * 2 + j
        return rc(slot(g, s), slot(g, s), zsem.at[g, k, way, j], zrec.at[g, s], dirs[way])

    def send_own(g):
        for way in range(2):
            @pl.when(has[way])
            def _():
                z_own(g, way).start()

    def send_mate(g):
        pair_copy(g).wait_recv()
        for way in range(2):
            @pl.when(has[way])
            def _():
                z_mate(g, way).start()

    def from_dist(k, way):
        return d >= k if way == 0 else d + k < dp

    def arrive(g, k):
        for way in range(2):
            @pl.when(from_dist(k, way))
            def _():
                for j in range(2):
                    z_fwd(g, k, way, j).wait_recv()

                    @pl.when(has[way])
                    def _():
                        z_fwd(g, k, way, j).start()

    def finish(g):
        own_copy(g).wait()
        pair_copy(g).wait_send()
        for way in range(2):
            @pl.when(has[way])
            def _():
                z_own(g, way).wait_send()
                z_mate(g, way).wait_send()
            for k in range(1, dp - 1):
                @pl.when(from_dist(k, way) & has[way])
                def _():
                    for j in range(2):
                        z_fwd(g, k, way, j).wait_send()

    hr = R // 2

    def rows_x(a, ref, out):
        return rc(
            ref.at[pl.ds(core * hr, hr), :], out.at[pl.ds(i * R + core * hr, hr), :],
            tsem.at[a, 0], tsem.at[a, 1], mate,
        )

    def rows_c(a, out):
        at = out.at[pl.ds((1 - i) * R + core * hr, hr), :]
        return rc(at, at, tsem.at[a, 2], tsem.at[a, 3], near)

    def rows_own(a, ref, out):
        return pltpu.make_async_copy(ref, out.at[pl.ds(i * R, R), :], lsem.at[GROUPS + a])

    pair_copy(0).start()
    send_own(0)
    pair_copy(1).start()
    pair_copy(2).start()
    rows_x(0, tok, x_o).start()
    send_own(1)
    own_copy(0).start()
    rows_own(0, tok, x_o).start()
    rows_own(1, gh, g_o).start()
    own_copy(1).start()
    own_copy(2).start()
    send_mate(0)
    send_own(2)
    rows_x(1, gh, g_o).start()
    arrive(0, 1)
    send_mate(1)
    rows_x(0, tok, x_o).wait_recv()
    rows_c(0, x_o).start()
    rows_c(0, x_o).wait_recv()
    rows_own(0, tok, x_o).wait()
    load_x = pltpu.make_async_copy(x_o, xs, lsem.at[5])
    load_x.start()
    send_mate(2)
    load_x.wait()

    def norm_block(b, _):
        at = pl.ds(pl.multiple_of(b * qb, qb), qb)
        x = xs[at, :].astype(F32)
        mean = jnp.mean(x, axis=-1, keepdims=True)
        c = x - mean
        var = jnp.mean(c * c, axis=-1, keepdims=True)
        h1s[at, :] = (c * lax.rsqrt(var + EPS) * vecs[0:1, :] + vecs[1:2, :]).astype(BF16)
        return 0

    lax.fori_loop(0, nb // 2, norm_block, 0)
    arrive(0, 2)
    lax.fori_loop(nb // 2, nb, norm_block, 0)
    for k in range(3, dp):
        arrive(0, k)
    own_copy(0).wait()
    load_w = pltpu.make_async_copy(wa_o, was, lsem.at[5])
    load_w.start()
    arrive(1, 1)
    rows_x(1, gh, g_o).wait_recv()
    rows_c(1, g_o).start()
    rows_c(1, g_o).wait_recv()
    rows_own(1, gh, g_o).wait()
    load_g = pltpu.make_async_copy(g_o, gs, lsem.at[6])
    load_g.start()
    load_w.wait()
    load_g.wait()

    scale = 1.0 / math.sqrt(HDIM)

    def proj_block(b, _):
        at = pl.ds(pl.multiple_of(b * qb, qb), qb)
        y = plain(h1s[at, :], was[:, : 3 * HDIM]) + bq[...]
        qs[at, :] = (turn(y[:, :HDIM], tabs, at, 1).astype(BF16).astype(F32) * scale).astype(BF16)
        win[reach, at, :HDIM] = turn(y[:, HDIM : 2 * HDIM], tabs, at, 1).astype(BF16)
        win[reach, at, HDIM:] = y[:, 2 * HDIM :].astype(BF16)
        das[at, :] = plain(gs[at, :], was[:, 3 * HDIM :]).astype(BF16)
        return 0

    lax.fori_loop(0, nb, proj_block, 0)

    def kv_copy(k):
        return rc(win.at[reach - k], win.at[reach - k - 1], ksem.at[0, k], ksem.at[1, k + 1], dirs[0])

    def kv_recv(k):
        return rc(win.at[reach - k], win.at[reach - k], ksem.at[0, k - 1], ksem.at[1, k], dirs[0])

    @pl.when(has[0])
    def _():
        kv_copy(0).start()

    arrive(2, 1)
    arrive(1, 2)
    for k in range(1, reach + 1):
        @pl.when(d >= k)
        def _():
            kv_recv(k).wait_recv()
            if k < reach:
                @pl.when(has[0])
                def _():
                    kv_copy(k).start()

        @pl.when(d < k)
        def _():
            win[reach - k] = jnp.zeros((plane, 2 * HDIM), BF16)

    acc[...] = jnp.zeros_like(acc)
    span = SEQ_LEN + qb
    base = reach * plane - SEQ_LEN

    def attend_block(b, _):
        at = pl.ds(pl.multiple_of(b * qb, qb), qb)
        keys_at = pl.ds(pl.multiple_of(base + b * qb, qb), span)
        flat = win.reshape((reach + 1) * plane, 2 * HDIM)
        keys = flat[keys_at, :HDIM]
        vals = flat[keys_at, HDIM:]
        q = qs[at, :]
        s = against(q, keys)
        c = base + b * qb + lax.broadcasted_iota(jnp.int32, (qb, span), 1)
        r = reach * plane + b * qb + lax.broadcasted_iota(jnp.int32, (qb, span), 0)
        s = jnp.where((c >= first[at, :]) & (c <= r), s, -1e30)
        e = jnp.exp(s - jnp.max(s, axis=1, keepdims=True))
        p = e * (1.0 / jnp.sum(e, axis=1, keepdims=True))
        pb = p.astype(BF16)
        att_o[at, :] = plain(pb, vals).astype(BF16)
        da = das[at, :]
        dpr = against(da, vals)
        delta = jnp.sum(p * dpr, axis=1, keepdims=True)
        ds = (p * (dpr - delta)).astype(BF16)
        dq = plain(ds, keys) * scale
        dq_o[at, :] = turn(dq, tabs, at, -1).astype(BF16)
        acc[keys_at, :HDIM] += inner(ds, q)
        acc[keys_at, HDIM:] += inner(pb, da)
        return 0

    lax.fori_loop(0, nb // 2, attend_block, 0)
    arrive(2, 2)
    for k in range(3, dp):
        arrive(1, k)
    lax.fori_loop(nb // 2, nb, attend_block, 0)

    for r in range(reach + 1):
        dwin_o[r] = acc[pl.ds(r * plane, plane), :].astype(BF16)
    for k in range(3, dp):
        arrive(2, k)

    for k in range(reach):
        @pl.when((d >= k) & has[0])
        def _():
            kv_copy(k).wait_send()
    for g in range(GROUPS):
        if g == 0:
            pair_copy(g).wait_send()
            for way in range(2):
                @pl.when(has[way])
                def _():
                    z_own(g, way).wait_send()
                    z_mate(g, way).wait_send()
                for k in range(1, dp - 1):
                    @pl.when(from_dist(k, way) & has[way])
                    def _():
                        for j in range(2):
                            z_fwd(g, k, way, j).wait_send()
        else:
            finish(g)
    for a, (ref, out) in enumerate(((tok, x_o), (gh, g_o))):
        rows_x(a, ref, out).wait_send()
        rows_c(a, out).wait_send()


def attend(tok, gh, w2, vecs, bq, tabs, first, dims):
    R, D, feats, dp, reach = dims
    plane = 2 * R
    gw = w2.shape[2] // GROUPS
    sds = jax.ShapeDtypeStruct
    return pl.pallas_call(
        functools.partial(attend_kernel, dims),
        out_shape=[
            sds((plane, D), BF16), sds((plane, D), BF16),
            sds((D, gw), BF16), sds((D, gw), BF16), sds((D, gw), BF16),
            sds((plane, HDIM), BF16), sds((plane, HDIM), BF16),
            sds((reach + 1, plane, 2 * HDIM), BF16),
        ],
        in_specs=[ANY, ANY, ANY, VMEM, VMEM, VMEM, VMEM],
        out_specs=[ANY] * 5 + [VMEM] * 3,
        scratch_shapes=[
            pltpu.VMEM((plane, D), BF16),
            pltpu.VMEM((plane, D), BF16),
            pltpu.VMEM((D, gw), BF16),
            pltpu.VMEM((plane, D), BF16),
            pltpu.VMEM((reach + 1, plane, 2 * HDIM), BF16),
            pltpu.VMEM((plane, HDIM), BF16),
            pltpu.VMEM((plane, HDIM), BF16),
            pltpu.VMEM(((reach + 1) * plane, 2 * HDIM), F32),
            pltpu.SemaphoreType.DMA((8,)),
            pltpu.SemaphoreType.DMA((2, 4)),
            pltpu.SemaphoreType.DMA((2, GROUPS)),
            pltpu.SemaphoreType.DMA((GROUPS, dp, 2, 2)),
            pltpu.SemaphoreType.DMA((GROUPS, 2 * dp)),
            pltpu.SemaphoreType.DMA((2, reach + 1)),
        ],
        compiler_params=pltpu.CompilerParams(
            collective_id=4, has_side_effects=True, vmem_limit_bytes=62 << 20
        ),
        name="attend",
    )(tok, gh, w2, vecs, bq, tabs, first)


def branch_kernel(
    dims,
    x_i, g_i, wa_i, wi_i, wo_i, att, dq_i, dwin_i, vecs, bin_, tabs,
    mixed_o, u_o, sums_o, own_o, oth_o,
    xs, gs, wi, wo, wd, act, dpre, dqkv, rcv, dtmp, up, tpr0, tpr1, tpr2, rs, mean, rstd,
    lsem, dsem, ssem, rsem, fsem, osem, tsem, near_ok, far_ok, mate_ok,
):
    R, D, feats, dp, reach = dims
    f = lax.axis_index("fsdp")
    t = lax.axis_index("tp")
    d, i = f // 2, lax.rem(f, 2)
    plane, pf = 2 * R, 2 * feats
    qb = min(256, plane)
    nb = plane // qb
    fb = min(256, pf)
    gw = wi.shape[1]
    pw = up.shape[2]
    mate = (f + 1 - 2 * i, t)
    tn, tf = t + 1 - 2 * lax.rem(t, 2), lax.rem(t + 2, 4)
    near, far = (f, tn), (f, tf)
    dirs = ((f + 2, t), (f - 2, t))
    has = (d + 1 < dp, d >= 1)

    barrier = pltpu.get_barrier_semaphore()
    for who in (mate, near, far):
        pl.semaphore_signal(barrier, 1, device_id=who, device_id_type=MESH)
    for k in range(2):
        @pl.when(has[k])
        def _():
            pl.semaphore_signal(barrier, 1, device_id=dirs[k], device_id_type=MESH)
    pl.semaphore_wait(barrier, 3 + has[0].astype(jnp.int32) + has[1].astype(jnp.int32))

    def rc(src, dst, ss, rs_, who):
        return pltpu.make_async_remote_copy(
            src_ref=src, dst_ref=dst, send_sem=ss, recv_sem=rs_, device_id=who, device_id_type=MESH
        )

    def down_copy(r):
        src = dwin_i.at[0] if r == 0 else dtmp
        return rc(src, rcv.at[r], dsem.at[0, r], dsem.at[1, r], dirs[1])

    @pl.when(d >= reach)
    def _():
        down_copy(0).start()

    loads = [
        pltpu.make_async_copy(src, dst, lsem.at[n])
        for n, (src, dst) in enumerate(
            (
                (x_i, xs), (wi_i, wi), (g_i, gs), (wo_i, wo),
                (wa_i.at[:, pl.ds(3 * HDIM, HDIM)], wd),
                (dq_i, dqkv.at[:, pl.ds(0, HDIM)]),
                (dwin_i.at[1], dtmp),
            )
        )
    ]
    for c in loads:
        c.start()
    sums_o[...] = jnp.zeros_like(sums_o)

    def rows(b):
        return pl.ds(pl.multiple_of(b * qb, qb), qb)

    loads[0].wait()

    def stat_block(b, _):
        x = xs[rows(b), :].astype(F32)
        m = jnp.mean(x, axis=-1, keepdims=True)
        c = x - m
        mean[rows(b), :] = m
        rstd[rows(b), :] = lax.rsqrt(jnp.mean(c * c, axis=-1, keepdims=True) + EPS)
        return 0

    lax.fori_loop(0, nb, stat_block, 0)
    for c in loads[1:5]:
        c.wait()

    def hat(at):
        return (xs[at, :].astype(F32) - mean[at, :]) * rstd[at, :]

    def ffn_block(b, _):
        at = rows(b)
        h2 = (hat(at) * vecs[2:3, :] + vecs[3:4, :]).astype(BF16)
        pre = plain(h2, wi[...]) + bin_[...]
        cdf = 0.5 * (1.0 + lax.erf(pre * (1.0 / math.sqrt(2.0))))
        a = (pre * cdf).astype(BF16)
        act[at, :] = a
        slope = cdf + pre * jnp.exp(-0.5 * pre * pre) * (1.0 / math.sqrt(2.0 * math.pi))
        g = gs[at, :]
        dp_b = (plain(g, wo[...]) * slope).astype(BF16)
        dpre[at, :] = dp_b
        sums_o[5:6, :gw] += jnp.sum(dp_b.astype(F32), axis=0, keepdims=True)
        sums_o[4:5, :] += jnp.sum(g.astype(F32), axis=0, keepdims=True)
        for c in range(4):
            cols = slice(c * pw, (c + 1) * pw)
            y = against(att[at, :], wd[cols, :]) + against(a, wo[cols, :])
            up[c, at, :] = y.astype(BF16)
        return 0

    def down_add(r):
        def block(b, _):
            at = rows(b)
            dtmp[at, :] = (dtmp[at, :].astype(F32) + rcv[r - 1, at, :].astype(F32)).astype(BF16)
            return 0

        @pl.when(has[0] & (d >= reach - r))
        def _():
            down_copy(r - 1).wait_recv()
            lax.fori_loop(0, nb, block, 0)

    lax.fori_loop(0, nb // 2, ffn_block, 0)
    loads[5].wait()
    loads[6].wait()
    for r in range(1, reach):
        down_add(r)

        @pl.when(d >= reach - r)
        def _():
            down_copy(r).start()

        if r == 1:
            lax.fori_loop(nb // 2, nb, ffn_block, 0)

        @pl.when(d >= reach - r)
        def _():
            down_copy(r).wait_send()

        more = pltpu.make_async_copy(dwin_i.at[r + 1], dtmp, lsem.at[6])
        more.start()
        more.wait()

    def near_copy(j):
        return rc(up.at[tn if j == 0 else lax.rem(tn + 2, 4)], tpr0.at[j], tsem.at[0, j], tsem.at[1, j], near)

    def far_copy():
        return rc(up.at[tf], tpr1, tsem.at[0, 2], tsem.at[1, 2], far)

    def mate_copy():
        return rc(up.at[t, pl.ds((1 - i) * R, R), :], tpr2, tsem.at[0, 3], tsem.at[1, 3], mate)

    def tp_near(second):
        if second:
            pl.semaphore_wait(near_ok, 1)
        near_copy(0).start()
        near_copy(1).start()

    def tp_far(second):
        def block(b, _):
            at = rows(b)
            up[tf, at, :] = (up[tf, at, :].astype(F32) + tpr0[1, at, :].astype(F32)).astype(BF16)
            return 0

        near_copy(1).wait_recv()
        lax.fori_loop(0, nb, block, 0)
        if second:
            pl.semaphore_wait(far_ok, 1)
        far_copy().start()

    def tp_mate(second):
        def block(b, _):
            at = rows(b)
            v = up[t, at, :].astype(F32) + tpr0[0, at, :].astype(F32) + tpr1[at, :].astype(F32)
            up[t, at, :] = v.astype(BF16)
            return 0

        near_copy(0).wait_recv()
        far_copy().wait_recv()
        lax.fori_loop(0, nb, block, 0)
        if not second:
            pl.semaphore_signal(near_ok, 1, device_id=near, device_id_type=MESH)
            pl.semaphore_signal(far_ok, 1, device_id=far, device_id_type=MESH)
        if second:
            pl.semaphore_wait(mate_ok, 1)
        mate_copy().start()

    def tp_last(second, out):
        mate_copy().wait_recv()
        mine = up[t, pl.ds(pl.multiple_of(i * R, R), R), :].astype(F32)
        out[...] = mine + tpr2[...].astype(F32)
        if not second:
            pl.semaphore_signal(mate_ok, 1, device_id=mate, device_id_type=MESH)
        near_copy(0).wait_send()
        near_copy(1).wait_send()
        far_copy().wait_send()
        mate_copy().wait_send()

    def grad_part(g, p, c):
        cols = pl.ds(pl.multiple_of(p * pf + c * fb, fb), fb)
        if g == 2:
            return inner(gs[:, cols], act[...])
        z = (xs[:, cols].astype(F32) - mean[...]) * rstd[...]
        n = 2 if g == 1 else 0
        h = (z * vecs[n : n + 1, cols] + vecs[n + 1 : n + 2, cols]).astype(BF16)
        if g == 1:
            return inner(h, dpre[...])
        return jnp.concatenate([inner(h, dqkv[...]), inner(gs[:, cols], att[...])], axis=1)

    def rs_copy(g, k, way):
        p = d + k * (1 - 2 * way)
        to = jnp.where((way == 1) & (k == 1), dp, p)
        who = (f + 2 - 4 * way, t)
        return rc(rs.at[g, p], rs.at[g, to], ssem.at[g, k, way], rsem.at[g, to], who)

    def rs_wait(g, p):
        return rc(rs.at[g, p], rs.at[g, p], ssem.at[g, 0, 0], rsem.at[g, p], mate)

    def add_part(g, p):
        def block(c, _):
            at = pl.ds(pl.multiple_of(c * fb, fb), fb)
            rs[g, p, at, :] = (rs[g, p, at, :].astype(F32) + grad_part(g, p, c)).astype(BF16)
            return 0

        lax.fori_loop(0, pf // fb, block, 0)

    def stage(g, k):
        def go(way, _):
            p = d + k * (1 - 2 * way)
            came = jnp.where(way == 0, d >= 1, d + 1 < dp)

            @pl.when((p >= 0) & (p < dp))
            def _():
                @pl.when(came)
                def _():
                    rs_wait(g, p).wait_recv()

                @pl.when(jnp.logical_not(came))
                def _():
                    rs[g, p] = jnp.zeros((pf, gw), BF16)

                add_part(g, p)
                rs_copy(g, k, way).start()

            return 0

        lax.fori_loop(0, 2, go, 0)

    def own_copy(g):
        return pltpu.make_async_copy(rs.at[g, d, pl.ds(i * feats, feats), :], own_o.at[g], osem.at[g, 0])

    def oth_copy(g):
        return rc(rs.at[g, d, pl.ds((1 - i) * feats, feats), :], oth_o.at[g], osem.at[g, 1], osem.at[g, 2], mate)

    def final(g):
        @pl.when(d >= 1)
        def _():
            rs_wait(g, d).wait_recv()

        @pl.when(d < 1)
        def _():
            rs[g, d] = jnp.zeros((pf, gw), BF16)

        @pl.when(d + 1 < dp)
        def _():
            rs_wait(g, dp).wait_recv()

        @pl.when(d + 1 >= dp)
        def _():
            rs[g, dp] = jnp.zeros((pf, gw), BF16)

        def block(c, _):
            at = pl.ds(pl.multiple_of(c * fb, fb), fb)
            v = rs[g, d, at, :].astype(F32) + rs[g, dp, at, :].astype(F32)
            rs[g, d, at, :] = (v + grad_part(g, d, c)).astype(BF16)
            return 0

        lax.fori_loop(0, pf // fb, block, 0)
        own_copy(g).start()
        oth_copy(g).start()

    def e_block(b, _):
        at = rows(b)
        z = hat(at)
        e1 = against(dqkv[at, :], wo[:, : 3 * HDIM])
        sums_o[0:1, :] += jnp.sum(e1 * z, axis=0, keepdims=True)
        sums_o[1:2, :] += jnp.sum(e1, axis=0, keepdims=True)
        u = e1 * vecs[0:1, :]
        e2 = against(dpre[at, :], wi[...])
        sums_o[2:3, :] += jnp.sum(e2 * z, axis=0, keepdims=True)
        sums_o[3:4, :] += jnp.sum(e2, axis=0, keepdims=True)
        u = (u + e2 * vecs[2:3, :]).astype(BF16)
        for c in range(4):
            up[c, at, :] = u[:, c * pw : (c + 1) * pw]
        sums_o[6:7, : 3 * HDIM] += jnp.sum(dqkv[at, :].astype(F32), axis=0, keepdims=True)
        return 0

    def tail_block(b, _):
        at = rows(b)
        a = dtmp[at, :].astype(F32)
        dqkv[at, HDIM : 2 * HDIM] = turn(a[:, :HDIM], tabs, at, -1).astype(BF16)
        dqkv[at, 2 * HDIM :] = a[:, HDIM:].astype(BF16)
        return 0

    tp_near(False)
    load_a = pltpu.make_async_copy(wa_i, wo, lsem.at[3])
    load_a.start()
    for k in range(dp - 1, 2, -1):
        stage(2, k)
        stage(1, k)
    tp_far(False)
    down_add(reach)
    lax.fori_loop(0, nb, tail_block, 0)
    stage(2, 2)
    stage(1, 2)
    tp_mate(False)
    stage(2, 1)
    tp_last(False, mixed_o)
    load_a.wait()
    lax.fori_loop(0, nb, e_block, 0)
    tp_near(True)
    stage(1, 1)
    for k in range(dp - 1, 2, -1):
        stage(0, k)
    tp_far(True)
    stage(0, 2)
    tp_mate(True)
    final(2)
    stage(0, 1)
    final(1)
    tp_last(True, u_o)
    final(0)

    @pl.when(d >= reach)
    def _():
        down_copy(0).wait_send()
    for g in range(GROUPS):
        for k in range(1, dp):
            @pl.when(d + k < dp)
            def _():
                rs_copy(g, k, 0).wait_send()

            @pl.when(d >= k)
            def _():
                rs_copy(g, k, 1).wait_send()
        own_copy(g).wait()
        oth_copy(g).wait()


def branch(x, g, wa, wi, wo, att, dq, dwin, vecs, b_in, tabs, dims):
    R, D, feats, dp, reach = dims
    plane, pf = 2 * R, 2 * feats
    gw = wi.shape[1]
    pw = D // 4
    sds = jax.ShapeDtypeStruct
    vm = pltpu.VMEM
    dma = pltpu.SemaphoreType.DMA
    return pl.pallas_call(
        functools.partial(branch_kernel, dims),
        out_shape=[
            sds((R, pw), F32), sds((R, pw), F32), sds((8, D), F32),
            sds((GROUPS, feats, gw), BF16), sds((GROUPS, feats, gw), BF16),
        ],
        in_specs=[ANY] * 5 + [VMEM, ANY, ANY, VMEM, VMEM, VMEM],
        out_specs=[VMEM] * 3 + [ANY] * 2,
        scratch_shapes=[
            vm((plane, D), BF16), vm((plane, D), BF16), vm((D, gw), BF16), vm((D, gw), BF16),
            vm((D, HDIM), BF16), vm((plane, gw), BF16), vm((plane, gw), BF16),
            vm((plane, 3 * HDIM), BF16), vm((reach, plane, 2 * HDIM), BF16), vm((plane, 2 * HDIM), BF16),
            vm((4, plane, pw), BF16), vm((2, plane, pw), BF16), vm((plane, pw), BF16), vm((R, pw), BF16),
            vm((GROUPS, dp + 1, pf, gw), BF16), vm((plane, 1), F32), vm((plane, 1), F32),
            dma((7,)), dma((2, reach)), dma((GROUPS, dp, 2)), dma((GROUPS, dp + 1)),
            dma((1,)), dma((GROUPS, 3)), dma((2, 4)),
            pltpu.SemaphoreType.REGULAR, pltpu.SemaphoreType.REGULAR, pltpu.SemaphoreType.REGULAR,
        ],
        compiler_params=pltpu.CompilerParams(
            collective_id=5, has_side_effects=True, vmem_limit_bytes=63 << 20
        ),
        name="branch",
    )(x, g, wa, wi, wo, att, dq, dwin, vecs, b_in, tabs)


def on_device(
    tokens,
    qkv_weight,
    qkv_bias,
    dense_weight,
    dense_bias,
    fc_in_weight,
    fc_in_bias,
    fc_out_weight,
    fc_out_bias,
    norm1_gain,
    norm1_shift,
    norm2_gain,
    norm2_shift,
    cotangent,
    subset_ids,
    seq_starts,
):
    rows, width = tokens.shape
    shards = lax.axis_size("fsdp")
    tps = lax.axis_size("tp")
    dp = shards // 2
    f = lax.axis_index("fsdp")
    t = lax.axis_index("tp")
    i = lax.rem(f, 2)
    d = f // 2
    total = rows * shards
    scale = 1.0 / math.sqrt(HDIM)
    feats = qkv_weight.shape[0]
    units = fc_in_weight.shape[1]
    head_cols = qkv_weight.shape[2]
    heads_here = head_cols // HDIM
    hd = qkv_bias.shape[2]
    ub = fc_in_bias.shape

    match = subset_ids[:, None] == jnp.arange(SUBSETS, dtype=jnp.int32)[None, :]
    counts = jnp.sum(match.astype(F32), axis=0)
    vecs = [norm1_gain, norm1_shift, norm2_gain, norm2_shift, dense_bias, fc_out_bias]
    pack = jnp.concatenate(
        [v.astype(F32) for v in vecs]
        + [qkv_bias.astype(F32).reshape(-1), fc_in_bias.astype(F32).reshape(-1), counts]
    )
    size = pack.shape[0]
    lanes = -(-size // 1024) * 128
    got = exchange(jnp.pad(pack, (0, 8 * lanes - size)).reshape(8, lanes), "fsdp", False, 1)
    got = got.reshape(shards, 8 * lanes)
    gain1, shift1, gain2, shift2, b_dense, b_out = [
        got[:, k * feats : (k + 1) * feats].reshape(width) for k in range(6)
    ]
    at = 6 * feats
    nq = 3 * heads_here * hd
    b_qkv = got[:, at : at + nq].reshape(shards, 3, heads_here, hd)
    b_qkv = b_qkv.transpose(1, 2, 0, 3).reshape(3, heads_here, HDIM)
    b_qkv = lax.dynamic_index_in_dim(b_qkv, i, 1, keepdims=False).reshape(3 * HDIM)
    at += nq
    b_in = got[:, at : at + units // shards].reshape(shards, ub[0], ub[1])
    b_in = half_of(b_in.transpose(1, 0, 2).reshape(units), i, 0)
    at += units // shards
    counts = jnp.sum(got[:, at : at + SUBSETS], axis=0)
    table = total / (SUBSETS * counts)
    row_scale = jnp.sum(jnp.where(match, table[None, :], 0.0), axis=1)
    carried = cotangent.astype(F32) * row_scale[:, None]
    grad_here = carried.astype(BF16)

    w2 = jnp.concatenate(
        [
            qkv_weight.reshape(feats, 3, heads_here, HDIM).transpose(2, 0, 1, 3).reshape(2, feats, 3 * HDIM),
            dense_weight.reshape(heads_here, HDIM, feats).transpose(0, 2, 1),
            fc_in_weight.reshape(feats, 2, units // 2).transpose(1, 0, 2),
            fc_out_weight.reshape(2, units // 2, feats).transpose(0, 2, 1),
        ],
        axis=2,
    )
    plane = 2 * rows
    start_row = d * plane
    reach = min(dp - 1, -(-(SEQ_LEN - 1) // plane))
    here = start_row + jnp.arange(plane, dtype=jnp.int32)
    docs_here, pos_here = locate(here, seq_starts)
    first = (here - pos_here.astype(jnp.int32)) - (start_row - reach * plane)
    cosine, sine = rotary_tables(pos_here)
    ones = jnp.ones((plane, 128 - ROT), F32)
    none = jnp.zeros((plane, 128 - ROT), F32)
    zero = jnp.zeros_like(sine)
    tabs = jnp.stack(
        [
            jnp.concatenate([cosine, cosine, ones], 1),
            jnp.concatenate([zero, sine, none], 1),
            jnp.concatenate([-sine, zero, none], 1),
        ]
    )
    vecs = jnp.stack([gain1, shift1, gain2, shift2] + [jnp.zeros_like(gain1)] * 4)
    dims = (rows, width, feats, dp, reach)
    x_b, g_b, w_a, w_i, w_o, att, dq, dwin = attend(
        tokens, grad_here, w2, vecs, b_qkv.reshape(1, -1), tabs, first[:, None], dims
    )
    share, u_here, sums, own, other = branch(
        x_b, g_b, w_a, w_i, w_o, att, dq, dwin, vecs, b_in.reshape(1, -1), tabs, dims
    )
    part_w = width // tps
    offset = t * part_w
    cut = lambda vec: lax.dynamic_slice_in_dim(vec, offset, part_w, vec.ndim - 1)
    x_here = cut(tokens).astype(F32)
    mixed = (x_here + share + cut(b_dense) + cut(b_out)).astype(BF16)

    both = jnp.where(i == 0, jnp.stack([own, other], 2), jnp.stack([other, own], 2)).astype(F32)
    g_att, g_in, g_out = both[0], both[1], both[2]
    qkv_weight_grad = (
        g_att[:, :, : 3 * HDIM].reshape(feats, 2, 3, HDIM).transpose(0, 2, 1, 3).reshape(feats, 3, head_cols)
    )
    dense_weight_grad = g_att[:, :, 3 * HDIM :].reshape(feats, head_cols).T
    fc_in_weight_grad = g_in.reshape(feats, units)
    fc_out_weight_grad = g_out.reshape(feats, units).T

    norms = sums[:5]
    norms = norms.reshape(5, shards, feats).transpose(1, 0, 2).reshape(shards, 5 * feats)
    in_b = jnp.where(jnp.arange(2)[:, None] == i, sums[5, : units // 2][None], 0.0)
    in_b = in_b.reshape(ub[0], shards, ub[1]).transpose(1, 0, 2).reshape(shards, ub[0] * ub[1])
    qkv_b = sums[6, : 3 * HDIM].reshape(3, 1, HDIM)
    qkv_b = jnp.where(jnp.arange(2)[None, :, None] == i, qkv_b, 0.0)
    qkv_b = qkv_b.reshape(3, 2, shards, hd).transpose(2, 0, 1, 3).reshape(shards, nq)
    small = jnp.concatenate([norms, in_b, qkv_b], axis=1)
    size = small.shape[1]
    lanes = -(-size // 1024) * 128
    small = jnp.pad(small, ((0, 0), (0, 8 * lanes - size))).reshape(shards, 8, lanes)
    small = jnp.sum(exchange(small, "fsdp", True, 2), axis=0).reshape(8 * lanes)
    x_rows = tokens.astype(F32)
    mean = jnp.mean(x_rows, axis=-1, keepdims=True)
    spread = jnp.mean((x_rows - mean) ** 2, axis=-1, keepdims=True)
    rstd = lax.rsqrt(spread + EPS)
    xhat_here = (x_here - mean) * rstd
    mine = jnp.concatenate(
        [small[: 4 * feats], jnp.sum(u_here, axis=1), jnp.sum(u_here * xhat_here, axis=1)]
    )
    size = mine.shape[0]
    lanes = -(-size // 1024) * 128
    mine = jnp.pad(mine, (0, 8 * lanes - size)).reshape(8, lanes)
    mine = jnp.sum(exchange(mine, "tp", False, 3), axis=0).reshape(8 * lanes)
    norm_grads = mine[: 4 * feats].reshape(4, feats)
    at = 4 * feats
    mean_u = (mine[at : at + rows] / width)[:, None]
    mean_ux = (mine[at + rows : at + 2 * rows] / width)[:, None]
    dx = rstd * (u_here - mean_u - xhat_here * mean_ux)
    tokens_grad = (cut(cotangent).astype(F32) * row_scale[:, None] + dx).astype(BF16)
    bias_grad = small[4 * feats : 5 * feats] * 0.5
    in_bias_grad = small[5 * feats : 5 * feats + ub[0] * ub[1]].reshape(ub)
    at = 5 * feats + ub[0] * ub[1]
    qkv_bias_grad = small[at : at + nq].reshape(3, heads_here, hd)
    return (
        mixed,
        tokens_grad,
        qkv_weight_grad,
        qkv_bias_grad,
        dense_weight_grad,
        bias_grad,
        fc_in_weight_grad,
        in_bias_grad,
        fc_out_weight_grad,
        bias_grad,
        norm_grads[0],
        norm_grads[1],
        norm_grads[2],
        norm_grads[3],
    )


def solution(mesh):
    in_specs = (
        P("fsdp", None),
        P("fsdp", None, "tp"),
        P(None, "tp", "fsdp"),
        P("tp", "fsdp"),
        P("fsdp"),
        P("fsdp", "tp"),
        P("tp", "fsdp"),
        P("tp", "fsdp"),
        P("fsdp"),
        P("fsdp"),
        P("fsdp"),
        P("fsdp"),
        P("fsdp"),
        P("fsdp", None),
        P("fsdp"),
        P(),
    )
    out_specs = (
        P("fsdp", "tp"),
        P("fsdp", "tp"),
        P("fsdp", None, "tp"),
        P(None, "tp", "fsdp"),
        P("tp", "fsdp"),
        P("fsdp"),
        P("fsdp", "tp"),
        P("tp", "fsdp"),
        P("tp", "fsdp"),
        P("fsdp"),
        P("fsdp"),
        P("fsdp"),
        P("fsdp"),
        P("fsdp"),
    )
    return jax.shard_map(
        on_device, mesh=mesh, in_specs=in_specs, out_specs=out_specs, check_vma=False
    )
```

```python
import functools
import math

import jax
import jax.numpy as jnp
from jax import lax
from jax.experimental import pallas as pl
from jax.experimental.pallas import tpu as pltpu
from jax.sharding import PartitionSpec as P

HDIM = 256
ROT = 64
SUBSETS = 22
SEQ_LEN = 2048
EPS = 1e-05
F32 = jnp.float32
BF16 = jnp.bfloat16
MESH = pl.DeviceIdType.MESH
ANY = pl.BlockSpec(memory_space=pl.ANY)
VMEM = pl.BlockSpec(memory_space=pltpu.VMEM)


def mm(left, right, dims):
    return lax.dot_general(left, right, (dims, ((), ())), preferred_element_type=F32)


def plain(left, right):
    return mm(left, right, ((1,), (0,)))


def inner(left, right):
    return mm(left, right, ((0,), (0,)))


def against(left, right):
    return mm(left, right, ((1,), (1,)))


def rotary_tables(positions):
    half = ROT // 2
    steps = jnp.arange(half, dtype=F32)
    freq = 1.0 / 10000.0 ** (steps * 2.0 / ROT)
    angle = positions[:, None] * freq[None, :]
    return jnp.cos(angle), jnp.sin(angle)


def locate(indices, starts):
    above = indices[:, None] >= starts[None, :]
    doc_ids = jnp.sum(above.astype(jnp.int32), axis=1) - 1
    pick = doc_ids[:, None] == jnp.arange(starts.shape[0], dtype=jnp.int32)[None, :]
    first = jnp.sum(jnp.where(pick, starts[None, :], 0), axis=1)
    return (doc_ids, (indices - first).astype(F32))


def half_of(value, which, axis):
    size = value.shape[axis] // 2
    return lax.dynamic_slice_in_dim(value, which * size, size, axis)


def exchange_kernel(axis, spread, v_ref, o_ref, ssem, rsem):
    count = o_ref.shape[0]
    me = lax.axis_index(axis)

    def peer(step):
        return lax.rem(me + step, count)

    barrier = pltpu.get_barrier_semaphore()
    for step in range(1, count):
        pl.semaphore_signal(barrier, 1, device_id={axis: peer(step)}, device_id_type=MESH)
    pl.semaphore_wait(barrier, count - 1)

    def copy(step):
        return pltpu.make_async_remote_copy(
            src_ref=v_ref.at[peer(step)] if spread else v_ref,
            dst_ref=o_ref.at[me],
            send_sem=ssem.at[step],
            recv_sem=rsem.at[step],
            device_id={axis: peer(step)},
            device_id_type=MESH,
        )

    for step in range(1, count):
        copy(step).start()
    o_ref[me] = v_ref[me] if spread else v_ref[...]
    for step in range(1, count):
        copy(step).wait()


def exchange(value, axis, spread, cid):
    count = lax.axis_size(axis)
    block = value.shape[1:] if spread else value.shape
    return pl.pallas_call(
        functools.partial(exchange_kernel, axis, spread),
        out_shape=jax.ShapeDtypeStruct((count,) + block, value.dtype),
        in_specs=[VMEM],
        out_specs=VMEM,
        scratch_shapes=[pltpu.SemaphoreType.DMA((count,)), pltpu.SemaphoreType.DMA((count,))],
        compiler_params=pltpu.CompilerParams(collective_id=cid, has_side_effects=True),
        name="exchange",
    )(value)


GROUPS = 3


def turn(u, tabs, at, sign):
    lo, hi = u[:, :128], u[:, 128:]
    a = pltpu.roll(lo, ROT // 2, 1) * tabs[1, at, :] + pltpu.roll(lo, 128 - ROT // 2, 1) * tabs[2, at, :]
    lo = lo * tabs[0, at, :] + (a if sign > 0 else -a)
    return jnp.concatenate([lo, hi], axis=1)


def block_kernel(
    dims,
    tok, gh, w2, vecs, bq, bin_, bias, tabs, first,
    wa_o, w0_o, w1_o, mixed_o, u_o, sums_o, own_o, oth_o,
    xs, gs, wbuf, win, qs, das, act, dpre, dqkv, att, rcv, dtmp, dwin, tpr0, tpr1, tpr2, rs, mean, rstd,
    lsem, tsem, psem, zsem, zrec, ksem, dsem, ssem, rsem, osem, bsem, near_ok, far_ok, mate_ok,
):
    R, D, feats, dp, reach = dims
    f = lax.axis_index("fsdp")
    t = lax.axis_index("tp")
    d, i = f // 2, lax.rem(f, 2)
    core = lax.rem(t, 2)
    plane, pf = 2 * R, 2 * feats
    qb = min(256, plane)
    nb = plane // qb
    fb = min(256, pf)
    gw = w2.shape[2] // GROUPS
    hu = gw // 2
    pw = D // 4
    tn, tf = t + 1 - 2 * core, lax.rem(t + 2, 4)
    mate, near, far = (f + 1 - 2 * i, t), (f, tn), (f, tf)
    dirs = ((f + 2, t), (f - 2, t))
    has = (d + 1 < dp, d >= 1)
    outs = (wa_o, w0_o, w1_o)
    scale = 1.0 / math.sqrt(HDIM)

    barrier = pltpu.get_barrier_semaphore()
    for who in (mate, near, far):
        pl.semaphore_signal(barrier, 1, device_id=who, device_id_type=MESH)
    for k in range(2):
        @pl.when(has[k])
        def _():
            pl.semaphore_signal(barrier, 1, device_id=dirs[k], device_id_type=MESH)
    pl.semaphore_wait(barrier, 3 + has[0].astype(jnp.int32) + has[1].astype(jnp.int32))

    def rc(src, dst, ss, rv, who):
        return pltpu.make_async_remote_copy(
            src_ref=src, dst_ref=dst, send_sem=ss, recv_sem=rv, device_id=who, device_id_type=MESH
        )

    def rows(b):
        return pl.ds(pl.multiple_of(b * qb, qb), qb)

    def slot(g, s):
        return outs[g].at[pl.ds(s * feats, feats), :]

    def part(half, g):
        return w2.at[half, :, pl.ds(g * gw, gw)]

    def pair_copy(g):
        return rc(part(1 - i, g), slot(g, f), psem.at[0, g], psem.at[1, g], mate)

    def mine_copy(g):
        return pltpu.make_async_copy(part(i, g), slot(g, f), lsem.at[g])

    def z_own(g, way):
        return rc(part(i, g), slot(g, f), zsem.at[g, 0, way, 0], zrec.at[g, f], dirs[way])

    def z_mate(g, way):
        s = f + 1 - 2 * i
        return rc(slot(g, s), slot(g, s), zsem.at[g, 0, way, 1], zrec.at[g, s], dirs[way])

    def z_fwd(g, k, way, j):
        s = (d - k) * 2 + j if way == 0 else (d + k) * 2 + j
        return rc(slot(g, s), slot(g, s), zsem.at[g, k, way, j], zrec.at[g, s], dirs[way])

    def send_own(g):
        for way in range(2):
            @pl.when(has[way])
            def _():
                z_own(g, way).start()

    def send_mate(g):
        pair_copy(g).wait_recv()
        for way in range(2):
            @pl.when(has[way])
            def _():
                z_mate(g, way).start()

    def from_dist(k, way):
        return d >= k if way == 0 else d + k < dp

    def arrive(g, k):
        for way in range(2):
            @pl.when(from_dist(k, way))
            def _():
                for j in range(2):
                    z_fwd(g, k, way, j).wait_recv()

                    @pl.when(has[way])
                    def _():
                        z_fwd(g, k, way, j).start()

    def gather_sent(g):
        pair_copy(g).wait_send()
        for way in range(2):
            @pl.when(has[way])
            def _():
                z_own(g, way).wait_send()
                z_mate(g, way).wait_send()
            for k in range(1, dp - 1):
                @pl.when(from_dist(k, way) & has[way])
                def _():
                    for j in range(2):
                        z_fwd(g, k, way, j).wait_send()

    def load(src, dst, n):
        c = pltpu.make_async_copy(src, dst, bsem.at[n])
        c.start()
        return c

    hr = R // 2

    def rows_x(a, ref, out):
        return rc(
            ref.at[pl.ds(core * hr, hr), :], out.at[pl.ds(i * R + core * hr, hr), :],
            tsem.at[a, 0], tsem.at[a, 1], mate,
        )

    def rows_c(a, out):
        at = out.at[pl.ds((1 - i) * R + core * hr, hr), :]
        return rc(at, at, tsem.at[a, 2], tsem.at[a, 3], near)

    def rows_own(a, ref, out):
        return pltpu.make_async_copy(ref, out.at[pl.ds(i * R, R), :], lsem.at[GROUPS + a])

    def rows_done(a, ref, out):
        rows_x(a, ref, out).wait_recv()
        rows_c(a, out).start()
        rows_c(a, out).wait_recv()
        rows_own(a, ref, out).wait()

    def hat(at):
        return (xs[at, :].astype(F32) - mean[at, :]) * rstd[at, :]

    def stat_block(b, _):
        x = xs[rows(b), :].astype(F32)
        m = jnp.mean(x, axis=-1, keepdims=True)
        c = x - m
        mean[rows(b), :] = m
        rstd[rows(b), :] = lax.rsqrt(jnp.mean(c * c, axis=-1, keepdims=True) + EPS)
        return 0

    def proj_block(b, _):
        at = rows(b)
        h1 = (hat(at) * vecs[0:1, :] + vecs[1:2, :]).astype(BF16)
        y = plain(h1, wbuf[:, : 3 * HDIM]) + bq[...]
        qs[at, :] = (turn(y[:, :HDIM], tabs, at, 1).astype(BF16).astype(F32) * scale).astype(BF16)
        win[reach, at, :HDIM] = turn(y[:, HDIM : 2 * HDIM], tabs, at, 1).astype(BF16)
        win[reach, at, HDIM:] = y[:, 2 * HDIM :].astype(BF16)
        return 0

    def datt_block(b, _):
        at = rows(b)
        das[at, :] = plain(gs[at, :], wbuf[:, 3 * HDIM :]).astype(BF16)
        return 0

    def ffn(h):
        mine = slice(h * hu, (h + 1) * hu)

        def block(b, _):
            at = rows(b)
            h2 = (hat(at) * vecs[2:3, :] + vecs[3:4, :]).astype(BF16)
            pre = plain(h2, wbuf[:, :hu]) + bin_[:, mine]
            cdf = 0.5 * (1.0 + lax.erf(pre * (1.0 / math.sqrt(2.0))))
            act[at, mine] = (pre * cdf).astype(BF16)
            slope = cdf + pre * jnp.exp(-0.5 * pre * pre) * (1.0 / math.sqrt(2.0 * math.pi))
            dp_b = (plain(gs[at, :], wbuf[:, hu:]) * slope).astype(BF16)
            dpre[at, mine] = dp_b
            sums_o[5:6, mine] += jnp.sum(dp_b.astype(F32), axis=0, keepdims=True)
            return 0

        lax.fori_loop(0, nb, block, 0)

    def kv_copy(k):
        return rc(win.at[reach - k], win.at[reach - k - 1], ksem.at[0, k], ksem.at[1, k + 1], dirs[0])

    def kv_recv(k):
        return rc(win.at[reach - k], win.at[reach - k], ksem.at[0, k - 1], ksem.at[1, k], dirs[0])

    def kv_step(k):
        @pl.when(d >= k)
        def _():
            kv_recv(k).wait_recv()
            if k < reach:
                @pl.when(has[0])
                def _():
                    kv_copy(k).start()

        @pl.when(d < k)
        def _():
            win[reach - k] = jnp.zeros((plane, 2 * HDIM), BF16)

    span = SEQ_LEN + qb
    base = reach * plane - SEQ_LEN

    def attention(acc, lo, hi):
        def block(b, _):
            at = rows(b)
            keys_at = pl.ds(pl.multiple_of(base + b * qb, qb), span)
            flat = win.reshape((reach + 1) * plane, 2 * HDIM)
            keys = flat[keys_at, :HDIM]
            vals = flat[keys_at, HDIM:]
            q = qs[at, :]
            s = against(q, keys)
            c = base + b * qb + lax.broadcasted_iota(jnp.int32, (qb, span), 1)
            r = reach * plane + b * qb + lax.broadcasted_iota(jnp.int32, (qb, span), 0)
            s = jnp.where((c >= first[at, :]) & (c <= r), s, -1e30)
            e = jnp.exp(s - jnp.max(s, axis=1, keepdims=True))
            p = e * (1.0 / jnp.sum(e, axis=1, keepdims=True))
            pb = p.astype(BF16)
            att[at, :] = plain(pb, vals).astype(BF16)
            da = das[at, :]
            dpr = against(da, vals)
            delta = jnp.sum(p * dpr, axis=1, keepdims=True)
            ds = (p * (dpr - delta)).astype(BF16)
            dq = plain(ds, keys) * scale
            dqkv[at, :HDIM] = turn(dq, tabs, at, -1).astype(BF16)
            acc[keys_at, :HDIM] += inner(ds, q)
            acc[keys_at, HDIM:] += inner(pb, da)
            return 0

        lax.fori_loop(lo, hi, block, 0)

    def down_copy(r):
        src = dwin.at[0] if r == 0 else dtmp
        return rc(src, rcv.at[r], dsem.at[0, r], dsem.at[1, r], dirs[1])

    def down_step(r):
        def keep(b, _):
            at = rows(b)
            dtmp[at, :] = dwin[r, at, :]
            return 0

        def add(b, _):
            at = rows(b)
            dtmp[at, :] = (dwin[r, at, :].astype(F32) + rcv[r - 1, at, :].astype(F32)).astype(BF16)
            return 0

        came = has[0] & (d >= reach - r)
        if r > 1:
            @pl.when(d >= reach - r + 1)
            def _():
                down_copy(r - 1).wait_send()

        @pl.when(came)
        def _():
            down_copy(r - 1).wait_recv()
            lax.fori_loop(0, nb, add, 0)

        @pl.when(jnp.logical_not(came))
        def _():
            lax.fori_loop(0, nb, keep, 0)

        if r < reach:
            @pl.when(d >= reach - r)
            def _():
                down_copy(r).start()

    def tail_block(b, _):
        at = rows(b)
        a = dtmp[at, :].astype(F32)
        dqkv[at, HDIM : 2 * HDIM] = turn(a[:, :HDIM], tabs, at, -1).astype(BF16)
        dqkv[at, 2 * HDIM :] = a[:, HDIM:].astype(BF16)
        return 0

    def grad_part(g, p, c):
        cols = pl.ds(pl.multiple_of(p * pf + c * fb, fb), fb)
        z = (xs[:, cols].astype(F32) - mean[...]) * rstd[...]
        n = 0 if g == 0 else 2
        h = (z * vecs[n : n + 1, cols] + vecs[n + 1 : n + 2, cols]).astype(BF16)
        if g == 0:
            return inner(h, dqkv[...]), inner(gs[:, cols], att[...])
        mine = slice((g - 1) * hu, g * hu)
        return inner(h, dpre[:, mine]), inner(gs[:, cols], act[:, mine])

    def add_part(g, p, second=None):
        cut = 3 * HDIM if g == 0 else hu

        def block(c, _):
            at = pl.ds(pl.multiple_of(c * fb, fb), fb)
            left, right = grad_part(g, p, c)
            for cols, v in ((slice(0, cut), left), (slice(cut, gw), right)):
                v = rs[g, p, at, cols].astype(F32) + v
                if second is not None:
                    v = v + rs[g, second, at, cols].astype(F32)
                rs[g, p, at, cols] = v.astype(BF16)
            return 0

        lax.fori_loop(0, pf // fb, block, 0)

    def rs_copy(g, k, way):
        p = d + k * (1 - 2 * way)
        to = jnp.where((way == 1) & (k == 1), dp, p)
        who = (f + 2 - 4 * way, t)
        return rc(rs.at[g, p], rs.at[g, to], ssem.at[g, k, way], rsem.at[g, to], who)

    def rs_wait(g, p):
        return rc(rs.at[g, p], rs.at[g, p], ssem.at[g, 0, 0], rsem.at[g, p], mate)

    def stage(g, k):
        def go(way, _):
            p = d + k * (1 - 2 * way)
            came = jnp.where(way == 0, d >= 1, d + 1 < dp)

            @pl.when((p >= 0) & (p < dp))
            def _():
                @pl.when(came)
                def _():
                    rs_wait(g, p).wait_recv()

                @pl.when(jnp.logical_not(came))
                def _():
                    rs[g, p] = jnp.zeros((pf, gw), BF16)

                add_part(g, p)
                rs_copy(g, k, way).start()

            return 0

        lax.fori_loop(0, 2, go, 0)

    def own_copy(g):
        return pltpu.make_async_copy(rs.at[g, d, pl.ds(i * feats, feats), :], own_o.at[g], osem.at[g, 0])

    def oth_copy(g):
        return rc(rs.at[g, d, pl.ds((1 - i) * feats, feats), :], oth_o.at[g], osem.at[g, 1], osem.at[g, 2], mate)

    def final(g):
        @pl.when(d >= 1)
        def _():
            rs_wait(g, d).wait_recv()

        @pl.when(d < 1)
        def _():
            rs[g, d] = jnp.zeros((pf, gw), BF16)

        @pl.when(d + 1 < dp)
        def _():
            rs_wait(g, dp).wait_recv()

        @pl.when(d + 1 >= dp)
        def _():
            rs[g, dp] = jnp.zeros((pf, gw), BF16)

        add_part(g, d, dp)
        own_copy(g).start()
        oth_copy(g).start()

    pair_copy(0).start()
    send_own(0)
    pair_copy(1).start()
    pair_copy(2).start()
    rows_x(0, tok, xs).start()
    send_own(1)
    mine_copy(0).start()
    rows_own(0, tok, xs).start()
    rows_own(1, gh, gs).start()
    mine_copy(1).start()
    mine_copy(2).start()
    sums_o[...] = jnp.zeros_like(sums_o)
    send_mate(0)
    send_own(2)
    rows_x(1, gh, gs).start()
    arrive(0, 1)
    send_mate(1)
    rows_done(0, tok, xs)
    send_mate(2)
    lax.fori_loop(0, nb, stat_block, 0)
    for k in range(2, dp):
        arrive(0, k)
    mine_copy(0).wait()
    weights = load(wa_o, wbuf, 0)
    arrive(1, 1)
    weights.wait()
    lax.fori_loop(0, nb, proj_block, 0)

    @pl.when(has[0])
    def _():
        kv_copy(0).start()

    rows_done(1, gh, gs)
    lax.fori_loop(0, nb, datt_block, 0)
    arrive(2, 1)
    arrive(1, 2)
    for k in range(1, reach):
        kv_step(k)
    for k in range(3, dp):
        arrive(1, k)
    mine_copy(1).wait()
    load(w0_o, wbuf, 0).wait()
    arrive(2, 2)
    ffn(0)
    for k in range(dp - 1, 2, -1):
        stage(1, k)
    kv_step(reach)

    def attend(acc):
        acc[...] = jnp.zeros_like(acc)
        attention(acc, 0, nb // 2)
        stage(1, 2)
        for k in range(3, dp):
            arrive(2, k)
        attention(acc, nb // 2, nb)
        for r in range(reach + 1):
            dwin[r] = acc[pl.ds(r * plane, plane), :].astype(BF16)

    pl.run_scoped(attend, pltpu.VMEM(((reach + 1) * plane, 2 * HDIM), F32))

    @pl.when(d >= reach)
    def _():
        down_copy(0).start()

    mine_copy(2).wait()
    weights = load(w1_o, wbuf, 0)
    stage(1, 1)
    weights.wait()
    ffn(1)
    for r in range(1, reach):
        down_step(r)
    for k in range(dp - 1, 2, -1):
        stage(2, k)

    def finish(up, wd):
        def out_block(b, _):
            at = rows(b)
            sums_o[4:5, :] += jnp.sum(gs[at, :].astype(F32), axis=0, keepdims=True)
            for c in range(4):
                cols = slice(c * pw, (c + 1) * pw)
                y = against(att[at, :], wd[cols, :]) + against(act[at, :], wbuf[cols, :])
                up[c, at, :] = y.astype(BF16)
            return 0

        def hidden_block(b, _):
            at = rows(b)
            e2 = against(dpre[at, :], wbuf[...])
            z = hat(at)
            sums_o[2:3, :] += jnp.sum(e2 * z, axis=0, keepdims=True)
            sums_o[3:4, :] += jnp.sum(e2, axis=0, keepdims=True)
            u = (e2 * vecs[2:3, :]).astype(BF16)
            for c in range(4):
                up[c, at, :] = u[:, c * pw : (c + 1) * pw]
            return 0

        def qkv_block(b, _):
            at = rows(b)
            e1 = against(dqkv[at, :], wbuf[:, : 3 * HDIM])
            z = hat(at)
            sums_o[0:1, :] += jnp.sum(e1 * z, axis=0, keepdims=True)
            sums_o[1:2, :] += jnp.sum(e1, axis=0, keepdims=True)
            sums_o[6:7, : 3 * HDIM] += jnp.sum(dqkv[at, :].astype(F32), axis=0, keepdims=True)
            u = e1 * vecs[0:1, :]
            for c in range(4):
                up[c, at, :] = (up[c, at, :].astype(F32) + u[:, c * pw : (c + 1) * pw]).astype(BF16)
            return 0

        def near_copy(j):
            return rc(up.at[tn if j == 0 else lax.rem(tn + 2, 4)], tpr0.at[j], tsem.at[2, j], tsem.at[3, j], near)

        def far_copy():
            return rc(up.at[tf], tpr1, tsem.at[2, 2], tsem.at[3, 2], far)

        def mate_copy():
            return rc(up.at[t, pl.ds((1 - i) * R, R), :], tpr2, tsem.at[2, 3], tsem.at[3, 3], mate)

        def tp_near(second):
            if second:
                pl.semaphore_wait(near_ok, 1)
            near_copy(0).start()
            near_copy(1).start()

        def tp_far(second):
            def block(b, _):
                at = rows(b)
                up[tf, at, :] = (up[tf, at, :].astype(F32) + tpr0[1, at, :].astype(F32)).astype(BF16)
                return 0

            near_copy(1).wait_recv()
            lax.fori_loop(0, nb, block, 0)
            if second:
                pl.semaphore_wait(far_ok, 1)
            far_copy().start()

        def tp_mate(second):
            def block(b, _):
                at = rows(b)
                v = up[t, at, :].astype(F32) + tpr0[0, at, :].astype(F32) + tpr1[at, :].astype(F32)
                up[t, at, :] = v.astype(BF16)
                return 0

            near_copy(0).wait_recv()
            far_copy().wait_recv()
            lax.fori_loop(0, nb, block, 0)
            if second:
                pl.semaphore_wait(mate_ok, 1)
            else:
                pl.semaphore_signal(near_ok, 1, device_id=near, device_id_type=MESH)
                pl.semaphore_signal(far_ok, 1, device_id=far, device_id_type=MESH)
            mate_copy().start()

        def tp_last(second):
            mate_copy().wait_recv()
            here = pl.ds(pl.multiple_of(i * R, R), R)
            v = up[t, here, :].astype(F32) + tpr2[...].astype(F32)
            if second:
                u_o[...] = v
            else:
                x = xs[here, pl.ds(pl.multiple_of(t * pw, pw), pw)].astype(F32)
                mixed_o[...] = (x + v + bias[...]).astype(BF16)
                pl.semaphore_signal(mate_ok, 1, device_id=mate, device_id_type=MESH)
            near_copy(0).wait_send()
            near_copy(1).wait_send()
            far_copy().wait_send()
            mate_copy().wait_send()

        loads = [
            load(w0_o.at[:, pl.ds(hu, hu)], wbuf.at[:, pl.ds(0, hu)], 0),
            load(w1_o.at[:, pl.ds(hu, hu)], wbuf.at[:, pl.ds(hu, hu)], 1),
            load(wa_o.at[:, pl.ds(3 * HDIM, HDIM)], wd, 2),
        ]
        final(1)
        for c in loads:
            c.wait()
        lax.fori_loop(0, nb, out_block, 0)
        tp_near(False)
        loads = [
            load(w0_o.at[:, pl.ds(0, hu)], wbuf.at[:, pl.ds(0, hu)], 0),
            load(w1_o.at[:, pl.ds(0, hu)], wbuf.at[:, pl.ds(hu, hu)], 1),
        ]
        stage(2, 2)
        tp_far(False)
        down_step(reach)
        lax.fori_loop(0, nb, tail_block, 0)
        for k in range(dp - 1, 2, -1):
            stage(0, k)
        stage(2, 1)
        tp_mate(False)
        stage(0, 2)
        tp_last(False)
        for c in loads:
            c.wait()
        lax.fori_loop(0, nb, hidden_block, 0)
        load(wa_o, wbuf, 0).wait()
        lax.fori_loop(0, nb, qkv_block, 0)
        tp_near(True)
        stage(0, 1)
        final(2)
        tp_far(True)
        tp_mate(True)
        tp_last(True)
        final(0)

    pl.run_scoped(finish, pltpu.VMEM((4, plane, pw), BF16), pltpu.VMEM((D, HDIM), BF16))

    @pl.when(d >= reach)
    def _():
        down_copy(0).wait_send()
    for k in range(reach):
        @pl.when((d >= k) & has[0])
        def _():
            kv_copy(k).wait_send()
    for a, (ref, out) in enumerate(((tok, xs), (gh, gs))):
        rows_x(a, ref, out).wait_send()
        rows_c(a, out).wait_send()
    for g in range(GROUPS):
        gather_sent(g)
        for k in range(1, dp):
            @pl.when(d + k < dp)
            def _():
                rs_copy(g, k, 0).wait_send()

            @pl.when(d >= k)
            def _():
                rs_copy(g, k, 1).wait_send()
        own_copy(g).wait()
        oth_copy(g).wait()


def block(tok, gh, w2, vecs, bq, b_in, bias, tabs, first, dims):
    R, D, feats, dp, reach = dims
    plane, pf = 2 * R, 2 * feats
    gw = w2.shape[2] // GROUPS
    pw = D // 4
    sds = jax.ShapeDtypeStruct
    vm = pltpu.VMEM
    dma = pltpu.SemaphoreType.DMA
    reg = pltpu.SemaphoreType.REGULAR
    return pl.pallas_call(
        functools.partial(block_kernel, dims),
        out_shape=[sds((D, gw), BF16)] * GROUPS
        + [sds((R, pw), BF16), sds((R, pw), F32), sds((8, D), F32)]
        + [sds((GROUPS, feats, gw), BF16)] * 2,
        in_specs=[ANY] * 3 + [VMEM] * 6,
        out_specs=[ANY] * GROUPS + [VMEM] * 3 + [ANY] * 2,
        scratch_shapes=[
            vm((plane, D), BF16), vm((plane, D), BF16), vm((D, gw), BF16),
            vm((reach + 1, plane, 2 * HDIM), BF16), vm((plane, HDIM), BF16), vm((plane, HDIM), BF16),
            vm((plane, gw), BF16), vm((plane, gw), BF16), vm((plane, 3 * HDIM), BF16), vm((plane, HDIM), BF16),
            vm((reach, plane, 2 * HDIM), BF16), vm((plane, 2 * HDIM), BF16),
            vm((reach + 1, plane, 2 * HDIM), BF16),
            vm((2, plane, pw), BF16), vm((plane, pw), BF16), vm((R, pw), BF16),
            vm((GROUPS, dp + 1, pf, gw), BF16), vm((plane, 1), F32), vm((plane, 1), F32),
            dma((GROUPS + 2,)), dma((4, 4)), dma((2, GROUPS)), dma((GROUPS, dp, 2, 2)), dma((GROUPS, 2 * dp)),
            dma((2, reach + 1)), dma((2, reach)), dma((GROUPS, dp, 2)), dma((GROUPS, dp + 1)), dma((GROUPS, 3)),
            dma((3,)), reg, reg, reg,
        ],
        compiler_params=pltpu.CompilerParams(
            collective_id=4, has_side_effects=True, vmem_limit_bytes=63 << 20
        ),
        name="block",
    )(tok, gh, w2, vecs, bq, b_in, bias, tabs, first)


def on_device(
    tokens,
    qkv_weight,
    qkv_bias,
    dense_weight,
    dense_bias,
    fc_in_weight,
    fc_in_bias,
    fc_out_weight,
    fc_out_bias,
    norm1_gain,
    norm1_shift,
    norm2_gain,
    norm2_shift,
    cotangent,
    subset_ids,
    seq_starts,
):
    rows, width = tokens.shape
    shards = lax.axis_size("fsdp")
    tps = lax.axis_size("tp")
    dp = shards // 2
    f = lax.axis_index("fsdp")
    t = lax.axis_index("tp")
    i = lax.rem(f, 2)
    d = f // 2
    total = rows * shards
    scale = 1.0 / math.sqrt(HDIM)
    feats = qkv_weight.shape[0]
    units = fc_in_weight.shape[1]
    head_cols = qkv_weight.shape[2]
    heads_here = head_cols // HDIM
    hd = qkv_bias.shape[2]
    ub = fc_in_bias.shape

    match = subset_ids[:, None] == jnp.arange(SUBSETS, dtype=jnp.int32)[None, :]
    counts = jnp.sum(match.astype(F32), axis=0)
    vecs = [norm1_gain, norm1_shift, norm2_gain, norm2_shift, dense_bias, fc_out_bias]
    pack = jnp.concatenate(
        [v.astype(F32) for v in vecs]
        + [qkv_bias.astype(F32).reshape(-1), fc_in_bias.astype(F32).reshape(-1), counts]
    )
    size = pack.shape[0]
    lanes = -(-size // 1024) * 128
    got = exchange(jnp.pad(pack, (0, 8 * lanes - size)).reshape(8, lanes), "fsdp", False, 1)
    got = got.reshape(shards, 8 * lanes)
    gain1, shift1, gain2, shift2, b_dense, b_out = [
        got[:, k * feats : (k + 1) * feats].reshape(width) for k in range(6)
    ]
    at = 6 * feats
    nq = 3 * heads_here * hd
    b_qkv = got[:, at : at + nq].reshape(shards, 3, heads_here, hd)
    b_qkv = b_qkv.transpose(1, 2, 0, 3).reshape(3, heads_here, HDIM)
    b_qkv = lax.dynamic_index_in_dim(b_qkv, i, 1, keepdims=False).reshape(3 * HDIM)
    at += nq
    b_in = got[:, at : at + units // shards].reshape(shards, ub[0], ub[1])
    b_in = half_of(b_in.transpose(1, 0, 2).reshape(units), i, 0)
    at += units // shards
    counts = jnp.sum(got[:, at : at + SUBSETS], axis=0)
    table = total / (SUBSETS * counts)
    row_scale = jnp.sum(jnp.where(match, table[None, :], 0.0), axis=1)
    carried = cotangent.astype(F32) * row_scale[:, None]
    grad_here = carried.astype(BF16)

    wi = fc_in_weight.reshape(feats, 2, 2, units // 4).transpose(1, 0, 2, 3)
    wo = fc_out_weight.reshape(2, 2, units // 4, feats).transpose(0, 3, 1, 2)
    w2 = jnp.concatenate(
        [
            qkv_weight.reshape(feats, 3, heads_here, HDIM).transpose(2, 0, 1, 3).reshape(2, feats, 3 * HDIM),
            dense_weight.reshape(heads_here, HDIM, feats).transpose(0, 2, 1),
            wi[:, :, 0], wo[:, :, 0], wi[:, :, 1], wo[:, :, 1],
        ],
        axis=2,
    )
    plane = 2 * rows
    start_row = d * plane
    reach = min(dp - 1, -(-(SEQ_LEN - 1) // plane))
    here = start_row + jnp.arange(plane, dtype=jnp.int32)
    docs_here, pos_here = locate(here, seq_starts)
    first = (here - pos_here.astype(jnp.int32)) - (start_row - reach * plane)
    cosine, sine = rotary_tables(pos_here)
    ones = jnp.ones((plane, 128 - ROT), F32)
    none = jnp.zeros((plane, 128 - ROT), F32)
    zero = jnp.zeros_like(sine)
    tabs = jnp.stack(
        [
            jnp.concatenate([cosine, cosine, ones], 1),
            jnp.concatenate([zero, sine, none], 1),
            jnp.concatenate([-sine, zero, none], 1),
        ]
    )
    vecs = jnp.stack([gain1, shift1, gain2, shift2] + [jnp.zeros_like(gain1)] * 4)
    dims = (rows, width, feats, dp, reach)
    part_w = width // tps
    offset = t * part_w
    cut = lambda vec: lax.dynamic_slice_in_dim(vec, offset, part_w, vec.ndim - 1)
    bias = (cut(b_dense) + cut(b_out)).reshape(1, -1)
    _, _, _, mixed, u_here, sums, own, other = block(
        tokens, grad_here, w2, vecs, b_qkv.reshape(1, -1), b_in.reshape(1, -1), bias, tabs, first[:, None], dims
    )
    x_here = cut(tokens).astype(F32)

    both = jnp.where(i == 0, jnp.stack([own, other], 2), jnp.stack([other, own], 2)).astype(F32)
    g_att = both[0]
    g_fc = both[1:].reshape(2, feats, 2, 2, units // 4)
    qkv_weight_grad = (
        g_att[:, :, : 3 * HDIM].reshape(feats, 2, 3, HDIM).transpose(0, 2, 1, 3).reshape(feats, 3, head_cols)
    )
    dense_weight_grad = g_att[:, :, 3 * HDIM :].reshape(feats, head_cols).T
    fc_in_weight_grad = g_fc[:, :, :, 0].transpose(1, 2, 0, 3).reshape(feats, units)
    fc_out_weight_grad = g_fc[:, :, :, 1].transpose(2, 0, 3, 1).reshape(units, feats)

    norms = sums[:5]
    norms = norms.reshape(5, shards, feats).transpose(1, 0, 2).reshape(shards, 5 * feats)
    in_b = jnp.where(jnp.arange(2)[:, None] == i, sums[5, : units // 2][None], 0.0)
    in_b = in_b.reshape(ub[0], shards, ub[1]).transpose(1, 0, 2).reshape(shards, ub[0] * ub[1])
    qkv_b = sums[6, : 3 * HDIM].reshape(3, 1, HDIM)
    qkv_b = jnp.where(jnp.arange(2)[None, :, None] == i, qkv_b, 0.0)
    qkv_b = qkv_b.reshape(3, 2, shards, hd).transpose(2, 0, 1, 3).reshape(shards, nq)
    small = jnp.concatenate([norms, in_b, qkv_b], axis=1)
    size = small.shape[1]
    lanes = -(-size // 1024) * 128
    small = jnp.pad(small, ((0, 0), (0, 8 * lanes - size))).reshape(shards, 8, lanes)
    small = jnp.sum(exchange(small, "fsdp", True, 2), axis=0).reshape(8 * lanes)
    x_rows = tokens.astype(F32)
    mean = jnp.mean(x_rows, axis=-1, keepdims=True)
    spread = jnp.mean((x_rows - mean) ** 2, axis=-1, keepdims=True)
    rstd = lax.rsqrt(spread + EPS)
    xhat_here = (x_here - mean) * rstd
    mine = jnp.concatenate(
        [small[: 4 * feats], jnp.sum(u_here, axis=1), jnp.sum(u_here * xhat_here, axis=1)]
    )
    size = mine.shape[0]
    lanes = -(-size // 1024) * 128
    mine = jnp.pad(mine, (0, 8 * lanes - size)).reshape(8, lanes)
    mine = jnp.sum(exchange(mine, "tp", False, 3), axis=0).reshape(8 * lanes)
    norm_grads = mine[: 4 * feats].reshape(4, feats)
    at = 4 * feats
    mean_u = (mine[at : at + rows] / width)[:, None]
    mean_ux = (mine[at + rows : at + 2 * rows] / width)[:, None]
    dx = rstd * (u_here - mean_u - xhat_here * mean_ux)
    tokens_grad = (cut(cotangent).astype(F32) * row_scale[:, None] + dx).astype(BF16)
    bias_grad = small[4 * feats : 5 * feats] * 0.5
    in_bias_grad = small[5 * feats : 5 * feats + ub[0] * ub[1]].reshape(ub)
    at = 5 * feats + ub[0] * ub[1]
    qkv_bias_grad = small[at : at + nq].reshape(3, heads_here, hd)
    return (
        mixed,
        tokens_grad,
        qkv_weight_grad,
        qkv_bias_grad,
        dense_weight_grad,
        bias_grad,
        fc_in_weight_grad,
        in_bias_grad,
        fc_out_weight_grad,
        bias_grad,
        norm_grads[0],
        norm_grads[1],
        norm_grads[2],
        norm_grads[3],
    )


def solution(mesh):
    in_specs = (
        P("fsdp", None),
        P("fsdp", None, "tp"),
        P(None, "tp", "fsdp"),
        P("tp", "fsdp"),
        P("fsdp"),
        P("fsdp", "tp"),
        P("tp", "fsdp"),
        P("tp", "fsdp"),
        P("fsdp"),
        P("fsdp"),
        P("fsdp"),
        P("fsdp"),
        P("fsdp"),
        P("fsdp", None),
        P("fsdp"),
        P(),
    )
    out_specs = (
        P("fsdp", "tp"),
        P("fsdp", "tp"),
        P("fsdp", None, "tp"),
        P(None, "tp", "fsdp"),
        P("tp", "fsdp"),
        P("fsdp"),
        P("fsdp", "tp"),
        P("tp", "fsdp"),
        P("tp", "fsdp"),
        P("fsdp"),
        P("fsdp"),
        P("fsdp"),
        P("fsdp"),
        P("fsdp"),
    )
    return jax.shard_map(
        on_device, mesh=mesh, in_specs=in_specs, out_specs=out_specs, check_vma=False
    )
```

```python
import functools
import math

import jax
import jax.numpy as jnp
from jax import lax
from jax.experimental import pallas as pl
from jax.experimental.pallas import tpu as pltpu
from jax.sharding import PartitionSpec as P

HDIM = 256
ROT = 64
SUBSETS = 22
SEQ_LEN = 2048
EPS = 1e-05
F32 = jnp.float32
BF16 = jnp.bfloat16
MESH = pl.DeviceIdType.MESH
ANY = pl.BlockSpec(memory_space=pl.ANY)
VMEM = pl.BlockSpec(memory_space=pltpu.VMEM)


def mm(left, right, dims):
    return lax.dot_general(left, right, (dims, ((), ())), preferred_element_type=F32)


def plain(left, right):
    return mm(left, right, ((1,), (0,)))


def inner(left, right):
    return mm(left, right, ((0,), (0,)))


def against(left, right):
    return mm(left, right, ((1,), (1,)))


def rotary_tables(positions):
    half = ROT // 2
    steps = jnp.arange(half, dtype=F32)
    freq = 1.0 / 10000.0 ** (steps * 2.0 / ROT)
    angle = positions[:, None] * freq[None, :]
    return jnp.cos(angle), jnp.sin(angle)


def locate(indices, starts):
    above = indices[:, None] >= starts[None, :]
    doc_ids = jnp.sum(above.astype(jnp.int32), axis=1) - 1
    pick = doc_ids[:, None] == jnp.arange(starts.shape[0], dtype=jnp.int32)[None, :]
    first = jnp.sum(jnp.where(pick, starts[None, :], 0), axis=1)
    return (doc_ids, (indices - first).astype(F32))


def half_of(value, which, axis):
    size = value.shape[axis] // 2
    return lax.dynamic_slice_in_dim(value, which * size, size, axis)


def exchange_kernel(axis, spread, v_ref, o_ref, ssem, rsem):
    count = o_ref.shape[0]
    me = lax.axis_index(axis)

    def peer(step):
        return lax.rem(me + step, count)

    barrier = pltpu.get_barrier_semaphore()
    for step in range(1, count):
        pl.semaphore_signal(barrier, 1, device_id={axis: peer(step)}, device_id_type=MESH)
    pl.semaphore_wait(barrier, count - 1)

    def copy(step):
        return pltpu.make_async_remote_copy(
            src_ref=v_ref.at[peer(step)] if spread else v_ref,
            dst_ref=o_ref.at[me],
            send_sem=ssem.at[step],
            recv_sem=rsem.at[step],
            device_id={axis: peer(step)},
            device_id_type=MESH,
        )

    for step in range(1, count):
        copy(step).start()
    o_ref[me] = v_ref[me] if spread else v_ref[...]
    for step in range(1, count):
        copy(step).wait()


def exchange(value, axis, spread, cid):
    count = lax.axis_size(axis)
    block = value.shape[1:] if spread else value.shape
    return pl.pallas_call(
        functools.partial(exchange_kernel, axis, spread),
        out_shape=jax.ShapeDtypeStruct((count,) + block, value.dtype),
        in_specs=[VMEM],
        out_specs=VMEM,
        scratch_shapes=[pltpu.SemaphoreType.DMA((count,)), pltpu.SemaphoreType.DMA((count,))],
        compiler_params=pltpu.CompilerParams(collective_id=cid, has_side_effects=True),
        name="exchange",
    )(value)


GROUPS = 3
ORDER = (
    "pair0", "own0i", "pair1", "own1o", "own0o", "own1i", "mate0o", "mate0i", "rx0", "mate1i", "mate1o",
    "arr01", "arr11", "pair2", "own2i", "rc0", "rx1", "arr02", "rc1", "stats", "arr03", "arr12", "proj",
    "datt", "arr13", "mate2i", "ffn0", "kv1k", "st13i", "kv1v", "st12o", "st12i", "mate2o", "kv2v", "own2o",
    "kv2k", "att0", "att1", "arr21", "st11i", "att2", "att3", "arr22", "st11o", "dn0", "sta3i", "arr23",
    "sta2i", "dn1k", "ffn1", "sta2o", "out", "st23i", "dn1v", "far0", "st22i", "mt0", "dn2v", "st22o", "dn2k",
    "stb3i", "last0", "st21o", "hid", "st21i", "qk", "stb2o", "far1", "stb2i", "fin1", "sta1i", "fin2",
    "sta1o", "stb1o", "mt1", "stb1i", "fina", "finb", "small", "last1",
)


def turn(u, tabs, at, sign):
    lo, hi = u[:, :128], u[:, 128:]
    lane = lax.broadcasted_iota(jnp.int32, lo.shape, 1)
    other = jnp.where(lane < ROT // 2, pltpu.roll(lo, 128 - ROT // 2, 1), pltpu.roll(lo, ROT // 2, 1))
    a = other * tabs[1, at, :]
    lo = lo * tabs[0, at, :] + (a if sign > 0 else -a)
    return jnp.concatenate([lo, hi], axis=1)


def block_kernel(
    dims,
    tok, gh, w2, vecs, bq, bin_, bias, carried, tabs, first,
    wa_o, w0_o, w1_o, mixed_o, dtok_o, norm_o, bias_o, dq_o, dd_o, di_o, do_o,
    xs, gs, wbuf, wk, wv, qs, das, act, dpre, dqkv, att, rcv, dtmp, tpr0, tpr1, tpr2,
    rs_a, rs_f, mean, rstd, tra, trf, sums, bsum, sum_s, sum_r, row_r, nrm_r,
    lsem, tsem, psem, zsem, zrec, ksem, dsem, ssem, rsem, fsem, bsem, xsem, near_ok, far_ok, mate_ok,
):
    R, D, feats, dp, reach = dims
    F, T = 2 * dp, tpr0.shape[0] * 2
    f = lax.axis_index("fsdp")
    t = lax.axis_index("tp")
    d, i = f // 2, lax.rem(f, 2)
    core = lax.rem(t, 2)
    plane, pf = 2 * R, 2 * feats
    qb = min(256, plane)
    nb = plane // qb
    fb = min(256, pf)
    gw = w2.shape[2] // GROUPS
    hu = gw // 2
    pw = D // T
    tn, tf = t + 1 - 2 * core, lax.rem(t + 2, T)
    mate, near, far = (f + 1 - 2 * i, t), (f, tn), (f, tf)
    has = (d + 1 < dp, d >= 1)
    inward = jnp.where(d < dp // 2, 0, 1)
    ways = {"i": inward, "o": 1 - inward}
    outs = (wa_o, w0_o, w1_o)
    scale = 1.0 / math.sqrt(HDIM)

    barrier = pltpu.get_barrier_semaphore()
    for s in range(1, F):
        pl.semaphore_signal(barrier, 1, device_id=(lax.rem(f + s, F), t), device_id_type=MESH)
    for s in range(1, T):
        pl.semaphore_signal(barrier, 1, device_id=(f, lax.rem(t + s, T)), device_id_type=MESH)
    pl.semaphore_wait(barrier, F + T - 2)

    def rc(src, dst, ss, rv, who):
        return pltpu.make_async_remote_copy(
            src_ref=src, dst_ref=dst, send_sem=ss, recv_sem=rv, device_id=who, device_id_type=MESH
        )

    def rows(b):
        return pl.ds(pl.multiple_of(b * qb, qb), qb)

    def toward(way):
        return (f + 2 - 4 * way, t)

    def open_way(way):
        return jnp.where(way == 0, d + 1 < dp, d >= 1)

    def slot(g, s):
        return outs[g].at[pl.ds(s * feats, feats), :]

    def part(half, g):
        return w2.at[half, :, pl.ds(g * gw, gw)]

    def pair_copy(g):
        return rc(part(1 - i, g), slot(g, f), psem.at[0, g], psem.at[1, g], mate)

    def mine_copy(g):
        return pltpu.make_async_copy(part(i, g), slot(g, f), lsem.at[g])

    def z_own(g, way):
        return rc(part(i, g), slot(g, f), zsem.at[g, 0, way, 0], zrec.at[g, f], toward(way))

    def z_mate(g, way):
        s = f + 1 - 2 * i
        return rc(slot(g, s), slot(g, s), zsem.at[g, 0, way, 1], zrec.at[g, s], toward(way))

    def z_fwd(g, k, way, j):
        s = (d - k) * 2 + j if way == 0 else (d + k) * 2 + j
        return rc(slot(g, s), slot(g, s), zsem.at[g, k, way, j], zrec.at[g, s], toward(way))

    def send_own(g, io):
        @pl.when(open_way(ways[io]))
        def _():
            z_own(g, ways[io]).start()

    def send_mate(g, io, wait):
        if wait:
            pair_copy(g).wait_recv()

        @pl.when(open_way(ways[io]))
        def _():
            z_mate(g, ways[io]).start()

    def from_dist(k, way):
        return d >= k if way == 0 else d + k < dp

    def arrive(g, k):
        for way in range(2):
            @pl.when(from_dist(k, way))
            def _():
                for j in range(2):
                    z_fwd(g, k, way, j).wait_recv()

                    @pl.when(has[way])
                    def _():
                        z_fwd(g, k, way, j).start()

    def gather_sent(g):
        pair_copy(g).wait_send()
        for way in range(2):
            @pl.when(has[way])
            def _():
                z_own(g, way).wait_send()
                z_mate(g, way).wait_send()
            for k in range(1, dp - 1):
                @pl.when(from_dist(k, way) & has[way])
                def _():
                    for j in range(2):
                        z_fwd(g, k, way, j).wait_send()

    def load(*pairs):
        copies = [pltpu.make_async_copy(src, dst, bsem.at[n]) for n, (src, dst) in enumerate(pairs)]
        for c in copies:
            c.start()
        for c in copies:
            c.wait()

    hr = R // 2
    given = ((tok, xs), (gh, gs))

    def rows_x(a):
        ref, out = given[a]
        return rc(
            ref.at[pl.ds(core * hr, hr), :], out.at[pl.ds(i * R + core * hr, hr), :],
            tsem.at[a, 0], tsem.at[a, 1], mate,
        )

    def rows_c(a):
        at = given[a][1].at[pl.ds((1 - i) * R + core * hr, hr), :]
        return rc(at, at, tsem.at[a, 2], tsem.at[a, 3], near)

    def rows_own(a):
        ref, out = given[a]
        return pltpu.make_async_copy(ref, out.at[pl.ds(i * R, R), :], lsem.at[GROUPS + a])

    def rows_on(a):
        rows_x(a).wait_recv()
        rows_c(a).start()

    def rows_done(a):
        rows_c(a).wait_recv()
        rows_own(a).wait()

    def hat(at):
        return (xs[at, :].astype(F32) - mean[at, :]) * rstd[at, :]

    def stats():
        def block(b, _):
            x = xs[rows(b), :].astype(F32)
            m = jnp.mean(x, axis=-1, keepdims=True)
            c = x - m
            mean[rows(b), :] = m
            rstd[rows(b), :] = lax.rsqrt(jnp.mean(c * c, axis=-1, keepdims=True) + EPS)
            return 0

        rows_done(0)
        lax.fori_loop(0, nb, block, 0)

    def proj():
        def block(b, _):
            at = rows(b)
            h1 = (hat(at) * vecs[0:1, :] + vecs[1:2, :]).astype(BF16)
            y = plain(h1, wbuf[:, : 3 * HDIM]) + bq[...]
            qs[at, :] = (turn(y[:, :HDIM], tabs, at, 1).astype(BF16).astype(F32) * scale).astype(BF16)
            wk[reach, at, :] = turn(y[:, HDIM : 2 * HDIM], tabs, at, 1).astype(BF16)
            wv[reach, at, :] = y[:, 2 * HDIM :].astype(BF16)
            return 0

        mine_copy(0).wait()
        load((wa_o, wbuf))
        lax.fori_loop(0, nb, block, 0)

        @pl.when(has[0])
        def _():
            kv_copy(0, 0).start()
            kv_copy(1, 0).start()

    def datt():
        def block(b, _):
            at = rows(b)
            das[at, :] = plain(gs[at, :], wbuf[:, 3 * HDIM :]).astype(BF16)
            return 0

        rows_done(1)
        lax.fori_loop(0, nb, block, 0)

    def ffn(h):
        mine = slice(h * hu, (h + 1) * hu)

        def block(b, _):
            at = rows(b)
            h2 = (hat(at) * vecs[2:3, :] + vecs[3:4, :]).astype(BF16)
            pre = plain(h2, wbuf[:, :hu]) + bin_[:, mine]
            cdf = 0.5 * (1.0 + lax.erf(pre * (1.0 / math.sqrt(2.0))))
            act[at, mine] = (pre * cdf).astype(BF16)
            slope = cdf + pre * jnp.exp(-0.5 * pre * pre) * (1.0 / math.sqrt(2.0 * math.pi))
            dp_b = (plain(gs[at, :], wbuf[:, hu:]) * slope).astype(BF16)
            dpre[at, mine] = dp_b
            bsum[0:1, mine] += jnp.sum(dp_b.astype(F32), axis=0, keepdims=True)
            return 0

        mine_copy(1 + h).wait()
        load((outs[1 + h], wbuf))
        lax.fori_loop(0, nb, block, 0)

    def kv_copy(h, k):
        w = (wk, wv)[h]
        return rc(w.at[reach - k], w.at[reach - k - 1], ksem.at[h, 0, k], ksem.at[h, 1, k + 1], toward(0))

    def kv_recv(h, k):
        w = (wk, wv)[h]
        return rc(w.at[reach - k], w.at[reach - k], ksem.at[h, 0, k - 1], ksem.at[h, 1, k], toward(0))

    def kv_step(h, k):
        @pl.when(d >= k)
        def _():
            kv_recv(h, k).wait_recv()
            if k < reach:
                @pl.when(has[0])
                def _():
                    kv_copy(h, k).start()

        @pl.when(d < k)
        def _():
            (wk, wv)[h][reach - k] = jnp.zeros((plane, HDIM), BF16)

    span = SEQ_LEN + qb
    base = reach * plane - SEQ_LEN
    parts = 4

    def attention(acc, n):
        def block(b, _):
            at = rows(b)
            keys_at = pl.ds(pl.multiple_of(base + b * qb, qb), span)
            keys = wk.reshape((reach + 1) * plane, HDIM)[keys_at, :]
            vals = wv.reshape((reach + 1) * plane, HDIM)[keys_at, :]
            q = qs[at, :]
            s = against(q, keys)
            c = base + b * qb + lax.broadcasted_iota(jnp.int32, (qb, span), 1)
            r = reach * plane + b * qb + lax.broadcasted_iota(jnp.int32, (qb, span), 0)
            s = jnp.where((c >= first[at, :]) & (c <= r), s, -1e30)
            e = jnp.exp(s - jnp.max(s, axis=1, keepdims=True))
            p = e * (1.0 / jnp.sum(e, axis=1, keepdims=True))
            pb = p.astype(BF16)
            att[at, :] = plain(pb, vals).astype(BF16)
            da = das[at, :]
            dpr = against(da, vals)
            delta = jnp.sum(p * dpr, axis=1, keepdims=True)
            ds = (p * (dpr - delta)).astype(BF16)
            dq = plain(ds, keys) * scale
            dqkv[at, :HDIM] = turn(dq, tabs, at, -1).astype(BF16)
            acc[keys_at, :HDIM] += inner(ds, q)
            acc[keys_at, HDIM:] += inner(pb, da)
            return 0

        if n == 0:
            acc[...] = jnp.zeros_like(acc)
        lax.fori_loop(n * nb // parts, (n + 1) * nb // parts, block, 0)

    dwin = (wk, wv)

    def down_copy(h, r):
        src = dwin[h].at[0] if r == 0 else dtmp.at[h]
        return rc(src, rcv.at[h, r], dsem.at[h, 0, r], dsem.at[h, 1, r], toward(1))

    def down_first(acc):
        for k in range(reach):
            @pl.when((d >= k) & has[0])
            def _():
                kv_copy(0, k).wait_send()
                kv_copy(1, k).wait_send()

        for r in range(reach + 1):
            for h in range(2):
                dwin[h][r] = acc[pl.ds(r * plane, plane), h * HDIM : (h + 1) * HDIM].astype(BF16)
            if r == 0:
                @pl.when(d >= reach)
                def _():
                    down_copy(0, 0).start()
                    down_copy(1, 0).start()

    def down_step(h, r):
        def keep(b, _):
            dtmp[h, rows(b), :] = dwin[h][r, rows(b), :]
            return 0

        def add(b, _):
            at = rows(b)
            v = dwin[h][r, at, :].astype(F32) + rcv[h, r - 1, at, :].astype(F32)
            dtmp[h, at, :] = v.astype(BF16)
            return 0

        def turned(b, _):
            at = rows(b)
            v = dtmp[h, at, :]
            dqkv[at, (h + 1) * HDIM : (h + 2) * HDIM] = (
                turn(v.astype(F32), tabs, at, -1).astype(BF16) if h == 0 else v
            )
            return 0

        came = has[0] & (d >= reach - r)
        if r > 1:
            @pl.when(d >= reach - r + 1)
            def _():
                down_copy(h, r - 1).wait_send()

        @pl.when(came)
        def _():
            down_copy(h, r - 1).wait_recv()
            lax.fori_loop(0, nb, add, 0)

        @pl.when(jnp.logical_not(came))
        def _():
            lax.fori_loop(0, nb, keep, 0)

        if r < reach:
            @pl.when(d >= reach - r)
            def _():
                down_copy(h, r).start()
        else:
            lax.fori_loop(0, nb, turned, 0)

    def rs(g):
        return rs_a.at[g] if g < 2 else rs_f.at[g - 2]

    def grad_part(g, p, c):
        cols = pl.ds(pl.multiple_of(p * pf + c * fb, fb), fb)
        z = (xs[:, cols].astype(F32) - mean[...]) * rstd[...]
        n = 0 if g < 2 else 2
        h = (z * vecs[n : n + 1, cols] + vecs[n + 1 : n + 2, cols]).astype(BF16)
        if g == 0:
            return inner(h, dqkv[:, :HDIM]), inner(gs[:, cols], att[...])
        if g == 1:
            return (inner(h, dqkv[:, HDIM:]),)
        mine = slice((g - 2) * hu, (g - 1) * hu)
        return inner(h, dpre[:, mine]), inner(gs[:, cols], act[:, mine])

    def add_part(g, p, second=None):
        def block(c, _):
            at = pl.ds(pl.multiple_of(c * fb, fb), fb)
            left = 0
            for v in grad_part(g, p, c):
                cols = slice(left, left + v.shape[1])
                left += v.shape[1]
                v = rs(g)[p, at, cols].astype(F32) + v
                if second is not None:
                    v = v + rs(g)[second, at, cols].astype(F32)
                rs(g)[p, at, cols] = v.astype(BF16)
            return 0

        lax.fori_loop(0, pf // fb, block, 0)

    def rs_copy(g, k, way):
        p = d + k * (1 - 2 * way)
        to = jnp.where((way == 1) & (k == 1), dp, p)
        return rc(rs(g).at[p], rs(g).at[to], ssem.at[g, k, way], rsem.at[g, to], toward(way))

    def rs_wait(g, p):
        return rc(rs(g).at[p], rs(g).at[p], ssem.at[g, 0, 0], rsem.at[g, p], mate)

    def clear(g, p):
        rs(g)[p] = jnp.zeros(rs(g).shape[1:], BF16)

    def stage(g, k, io):
        way = ways[io]
        p = d + k * (1 - 2 * way)
        came = open_way(1 - way)

        @pl.when((p >= 0) & (p < dp))
        def _():
            @pl.when(came)
            def _():
                rs_wait(g, p).wait_recv()

            @pl.when(jnp.logical_not(came))
            def _():
                clear(g, p)

            add_part(g, p)
            rs_copy(g, k, way).start()

    def final_copies(g):
        lo = pl.multiple_of(i * HDIM, HDIM)
        pieces = []
        for j in range(2):
            at = pl.ds((i if j == 0 else 1 - i) * feats, feats)
            src = rs(g).at[d, at]
            if g == 0:
                dst = (dq_o.at[0, :, pl.ds(lo, HDIM)], dd_o.at[pl.ds(lo, HDIM), :])
                src = (src.at[:, pl.ds(0, HDIM)], tra.at[j])
            elif g == 1:
                dst = tuple(dq_o.at[n, :, pl.ds(lo, HDIM)] for n in (1, 2))
                src = tuple(src.at[:, pl.ds(n * HDIM, HDIM)] for n in (0, 1))
            else:
                u = pl.multiple_of(i * gw + (g - 2) * hu, hu)
                dst = (di_o.at[:, pl.ds(u, hu)], do_o.at[pl.ds(u, hu), :])
                src = (src.at[:, pl.ds(0, hu)], trf.at[g - 2, j])
            for n in range(2):
                if j == 0:
                    pieces.append(pltpu.make_async_copy(src[n], dst[n], fsem.at[g, n, 0]))
                else:
                    pieces.append(rc(src[n], dst[n], fsem.at[g, n, 1], fsem.at[g, n, 2], mate))
        return pieces

    def final(g):
        for p, came in ((d, has[1]), (dp, has[0])):
            @pl.when(came)
            def _():
                rs_wait(g, p).wait_recv()

            @pl.when(jnp.logical_not(came))
            def _():
                clear(g, p)

        add_part(g, d, dp)
        if g != 1:
            cut = HDIM if g == 0 else hu
            for j in range(2):
                at = pl.ds(pl.multiple_of((i if j == 0 else 1 - i) * feats, feats), feats)
                turned = rs(g)[d, at, cut:].astype(F32).T.astype(BF16)
                if g == 0:
                    tra[j] = turned
                else:
                    trf[g - 2, j] = turned
        for c in final_copies(g):
            c.start()

    def out_step(up, wd):
        def block(b, _):
            at = rows(b)
            sums[4:5, :] += jnp.sum(gs[at, :].astype(F32), axis=0, keepdims=True)
            for c in range(T):
                cols = slice(c * pw, (c + 1) * pw)
                y = against(att[at, :], wd[cols, :]) + against(act[at, :], wbuf[cols, :])
                up[c, at, :] = y.astype(BF16)
            return 0

        load(
            (w0_o.at[:, pl.ds(hu, hu)], wbuf.at[:, pl.ds(0, hu)]),
            (w1_o.at[:, pl.ds(hu, hu)], wbuf.at[:, pl.ds(hu, hu)]),
            (wa_o.at[:, pl.ds(3 * HDIM, HDIM)], wd),
            (carried, env["kept"]),
        )
        lax.fori_loop(0, nb, block, 0)
        tp_near(up, False)

    def hidden_step(up):
        def block(b, _):
            at = rows(b)
            e2 = against(dpre[at, :], wbuf[...])
            z = hat(at)
            sums[2:3, :] += jnp.sum(e2 * z, axis=0, keepdims=True)
            sums[3:4, :] += jnp.sum(e2, axis=0, keepdims=True)
            u = (e2 * vecs[2:3, :]).astype(BF16)
            for c in range(T):
                up[c, at, :] = u[:, c * pw : (c + 1) * pw]
            return 0

        load(
            (w0_o.at[:, pl.ds(0, hu)], wbuf.at[:, pl.ds(0, hu)]),
            (w1_o.at[:, pl.ds(0, hu)], wbuf.at[:, pl.ds(hu, hu)]),
        )
        lax.fori_loop(0, nb, block, 0)

    def qkv_step(up):
        def block(b, _):
            at = rows(b)
            e1 = against(dqkv[at, :], wbuf[:, : 3 * HDIM])
            z = hat(at)
            sums[0:1, :] += jnp.sum(e1 * z, axis=0, keepdims=True)
            sums[1:2, :] += jnp.sum(e1, axis=0, keepdims=True)
            bsum[1:2, : 3 * HDIM] += jnp.sum(dqkv[at, :].astype(F32), axis=0, keepdims=True)
            u = e1 * vecs[0:1, :]
            for c in range(T):
                up[c, at, :] = (up[c, at, :].astype(F32) + u[:, c * pw : (c + 1) * pw]).astype(BF16)
            return 0

        load((wa_o, wbuf))
        lax.fori_loop(0, nb, block, 0)
        tp_near(up, True)
        for s in range(F):
            sum_s[s] = sums[:, s * feats : (s + 1) * feats]
        for s in range(1, F):
            sum_copy(s).start()
            bias_copy(s).start()
        sum_r[f] = sum_s[f]
        bias_o[f] = bsum[...]

    def near_copy(up, j):
        return rc(up.at[tn if j == 0 else lax.rem(tn + 2, T)], tpr0.at[j], tsem.at[2, j], tsem.at[3, j], near)

    def far_copy(up):
        return rc(up.at[tf], tpr1, tsem.at[2, 2], tsem.at[3, 2], far)

    def mate_copy(up):
        return rc(up.at[t, pl.ds((1 - i) * R, R), :], tpr2, tsem.at[2, 3], tsem.at[3, 3], mate)

    def tp_near(up, second):
        if second:
            pl.semaphore_wait(near_ok, 1)
        near_copy(up, 0).start()
        near_copy(up, 1).start()

    def tp_far(up, second):
        def block(b, _):
            at = rows(b)
            up[tf, at, :] = (up[tf, at, :].astype(F32) + tpr0[1, at, :].astype(F32)).astype(BF16)
            return 0

        near_copy(up, 1).wait_recv()
        lax.fori_loop(0, nb, block, 0)
        if second:
            pl.semaphore_wait(far_ok, 1)
        far_copy(up).start()

    def tp_mate(up, second):
        def block(b, _):
            at = rows(b)
            v = up[t, at, :].astype(F32) + tpr0[0, at, :].astype(F32) + tpr1[at, :].astype(F32)
            up[t, at, :] = v.astype(BF16)
            return 0

        near_copy(up, 0).wait_recv()
        far_copy(up).wait_recv()
        lax.fori_loop(0, nb, block, 0)
        if second:
            pl.semaphore_wait(mate_ok, 1)
        else:
            pl.semaphore_signal(near_ok, 1, device_id=near, device_id_type=MESH)
            pl.semaphore_signal(far_ok, 1, device_id=far, device_id_type=MESH)
        mate_copy(up).start()

    def tp_last(up, second):
        mate_copy(up).wait_recv()
        here = pl.ds(pl.multiple_of(i * R, R), R)
        x = xs[here, pl.ds(pl.multiple_of(t * pw, pw), pw)].astype(F32)
        if second:
            u = up[t, here, :].astype(F32) + tpr2[...].astype(F32)
            z = (x - mean[here, :]) * rstd[here, :]
            lane = lax.broadcasted_iota(jnp.int32, (R, 128), 1)
            one, two = jnp.sum(u, axis=1, keepdims=True), jnp.sum(u * z, axis=1, keepdims=True)
            row_r[t] = jnp.where(lane == 0, one, jnp.where(lane == 1, two, 0.0)).T[:8]
            for s in range(1, T):
                row_copy(s).start()
            for s in range(1, T):
                row_copy(s).wait()
            both = row_r[0]
            for s in range(1, T):
                both = both + row_r[s]
            both = jnp.concatenate([both, jnp.zeros((120, R), F32)], axis=0).T * (1.0 / D)
            dx = rstd[here, :] * (u - both[:, 0:1] - z * both[:, 1:2])
            dtok_o[...] = (env["kept"][...] + dx).astype(BF16)
        else:
            v = up[t, here, :].astype(F32) + tpr2[...].astype(F32)
            mixed_o[...] = (x + v + bias[...]).astype(BF16)
            pl.semaphore_signal(mate_ok, 1, device_id=mate, device_id_type=MESH)
        near_copy(up, 0).wait_send()
        near_copy(up, 1).wait_send()
        far_copy(up).wait_send()
        mate_copy(up).wait_send()

    def row_copy(s):
        return rc(row_r.at[t], row_r.at[t], xsem.at[0, 0, s], xsem.at[0, 1, s], (f, lax.rem(t + s, T)))

    def norm_copy(s):
        return rc(nrm_r.at[t], nrm_r.at[t], xsem.at[1, 0, s], xsem.at[1, 1, s], (f, lax.rem(t + s, T)))

    def sum_copy(s):
        to = lax.rem(f + s, F)
        return rc(sum_s.at[to], sum_r.at[f], xsem.at[2, 0, s], xsem.at[2, 1, s], (to, t))

    def bias_copy(s):
        return rc(bsum, bias_o.at[f], xsem.at[3, 0, s], xsem.at[3, 1, s], (lax.rem(f + s, F), t))

    def small_sums():
        for s in range(1, F):
            sum_copy(s).wait()
            bias_copy(s).wait()
        v = sum_r[0]
        for s in range(1, F):
            v = v + sum_r[s]
        nrm_r[t] = v
        for s in range(1, T):
            norm_copy(s).start()
        for s in range(1, T):
            norm_copy(s).wait()
        both = nrm_r[0]
        for s in range(1, T):
            both = both + nrm_r[s]
        row = lax.broadcasted_iota(jnp.int32, both.shape, 0)
        norm_o[...] = jnp.where(row == 4, v * 0.5, both)

    env = {}
    far_out = tuple(range(dp - 1, 2, -1))
    groups = {"a": 0, "b": 1, "1": 2, "2": 3}
    paired = set()

    def step(name):
        kind, rest = name.rstrip("0123456789abiokv"), ""
        rest = name[len(kind):]
        if kind == "pair":
            pair_copy(int(rest)).start()
            mine_copy(int(rest)).start()
        elif kind == "own":
            send_own(int(rest[0]), rest[1])
        elif kind == "mate":
            send_mate(int(rest[0]), rest[1], rest[0] not in paired)
            paired.add(rest[0])
        elif kind == "arr":
            g, k = int(rest[0]), int(rest[1])
            for n in range(k, dp if k == 3 else k + 1):
                arrive(g, n)
        elif kind == "rx":
            rows_x(int(rest)).start()
            rows_own(int(rest)).start()
        elif kind == "rc":
            rows_on(int(rest))
        elif kind == "stats":
            stats()
        elif kind == "proj":
            proj()
        elif kind == "datt":
            datt()
        elif kind == "ffn":
            ffn(int(rest))
        elif kind == "att":
            attention(env["acc"], int(rest))
        elif kind == "dn" and rest == "0":
            down_first(env["acc"])
        elif kind == "dn":
            for r in range(1, reach) if rest[0] == "1" else (reach,):
                down_step("kv".index(rest[1]), r)
        elif kind == "st":
            g, k, io = groups[rest[0]], int(rest[1]), rest[2]
            if k == 3:
                for n in far_out:
                    stage(g, n, io)
            elif k == 2 and io == "o":
                for n in far_out + (2,):
                    stage(g, n, io)
            else:
                stage(g, k, io)
        elif kind == "fin":
            final(groups[rest])
        elif kind == "out":
            out_step(env["up"], env["wd"])
        elif kind == "far":
            tp_far(env["up"], rest == "1")
        elif kind == "mt":
            tp_mate(env["up"], rest == "1")
        elif kind == "last":
            tp_last(env["up"], rest == "1")
        elif kind == "hid":
            hidden_step(env["up"])
        elif kind == "q":
            qkv_step(env["up"])
        elif kind == "small":
            small_sums()
        else:
            hop = int(rest[-2])
            for k in range(1, reach) if hop == 1 else (reach,):
                kv_step("kv".index(rest[-1]), k)

    def attend_scope(acc):
        env["acc"] = acc
        for name in ORDER[ORDER.index("att0") : ORDER.index("dn0") + 1]:
            step(name)

    def finish_scope(up, wd, kept):
        env["up"], env["wd"], env["kept"] = up, wd, kept
        for name in ORDER[ORDER.index("out") :]:
            step(name)

    sums[...] = jnp.zeros_like(sums)
    bsum[...] = jnp.zeros_like(bsum)
    for name in ORDER[: ORDER.index("att0")]:
        step(name)
    pl.run_scoped(attend_scope, pltpu.VMEM(((reach + 1) * plane, 2 * HDIM), F32))
    for name in ORDER[ORDER.index("dn0") + 1 : ORDER.index("out")]:
        step(name)
    pl.run_scoped(
        finish_scope, pltpu.VMEM((T, plane, pw), BF16), pltpu.VMEM((D, HDIM), BF16), pltpu.VMEM((R, pw), F32)
    )

    for h in range(2):
        @pl.when(d >= reach)
        def _():
            down_copy(h, 0).wait_send()
    for a in range(2):
        rows_x(a).wait_send()
        rows_c(a).wait_send()
    for g in range(GROUPS):
        gather_sent(g)
    for g in range(4):
        for k in range(1, dp):
            for way in range(2):
                @pl.when(from_dist(k, 1 - way))
                def _():
                    rs_copy(g, k, way).wait_send()
        for c in final_copies(g):
            c.wait()


def block(tok, gh, w2, vecs, bq, b_in, bias, carried, tabs, first, dims):
    R, D, feats, dp, reach = dims
    plane, pf, F, T = 2 * R, 2 * feats, 2 * dp, lax.axis_size("tp")
    gw = w2.shape[2] // GROUPS
    pw = D // T
    sds = jax.ShapeDtypeStruct
    vm = pltpu.VMEM
    dma = pltpu.SemaphoreType.DMA
    reg = pltpu.SemaphoreType.REGULAR
    win = vm((reach + 1, plane, HDIM), BF16)
    return pl.pallas_call(
        functools.partial(block_kernel, dims),
        out_shape=[sds((D, gw), BF16)] * GROUPS
        + [sds((R, pw), BF16), sds((R, pw), BF16), sds((8, feats), F32), sds((F, 8, gw), F32)]
        + [sds((3, feats, 2 * HDIM), BF16), sds((2 * HDIM, feats), BF16)]
        + [sds((feats, 2 * gw), BF16), sds((2 * gw, feats), BF16)],
        in_specs=[ANY] * 3 + [VMEM] * 4 + [ANY] + [VMEM] * 2,
        out_specs=[ANY] * GROUPS + [VMEM] * 4 + [ANY] * 4,
        scratch_shapes=[
            vm((plane, D), BF16), vm((plane, D), BF16), vm((D, gw), BF16),
            win, win, vm((plane, HDIM), BF16), vm((plane, HDIM), BF16),
            vm((plane, gw), BF16), vm((plane, gw), BF16), vm((plane, 3 * HDIM), BF16), vm((plane, HDIM), BF16),
            vm((2, reach, plane, HDIM), BF16), vm((2, plane, HDIM), BF16),
            vm((T // 2, plane, pw), BF16), vm((plane, pw), BF16), vm((R, pw), BF16),
            vm((2, dp + 1, pf, 2 * HDIM), BF16), vm((2, dp + 1, pf, gw), BF16),
            vm((plane, 1), F32), vm((plane, 1), F32),
            vm((2, HDIM, feats), BF16), vm((2, 2, gw // 2, feats), BF16),
            vm((8, D), F32), vm((8, gw), F32), vm((F, 8, feats), F32), vm((F, 8, feats), F32),
            vm((T, 8, R), F32), vm((T, 8, feats), F32),
            dma((GROUPS + 2,)), dma((4, 4)), dma((2, GROUPS)), dma((GROUPS, dp, 2, 2)), dma((GROUPS, F)),
            dma((2, 2, reach + 1)), dma((2, 2, reach)), dma((4, dp, 2)), dma((4, dp + 1)), dma((4, 2, 3)),
            dma((4,)), dma((4, 2, F)), reg, reg, reg,
        ],
        compiler_params=pltpu.CompilerParams(
            collective_id=4, has_side_effects=True, vmem_limit_bytes=63 << 20
        ),
        name="block",
    )(tok, gh, w2, vecs, bq, b_in, bias, carried, tabs, first)


def on_device(
    tokens,
    qkv_weight,
    qkv_bias,
    dense_weight,
    dense_bias,
    fc_in_weight,
    fc_in_bias,
    fc_out_weight,
    fc_out_bias,
    norm1_gain,
    norm1_shift,
    norm2_gain,
    norm2_shift,
    cotangent,
    subset_ids,
    seq_starts,
):
    rows, width = tokens.shape
    shards = lax.axis_size("fsdp")
    tps = lax.axis_size("tp")
    dp = shards // 2
    f = lax.axis_index("fsdp")
    t = lax.axis_index("tp")
    i = lax.rem(f, 2)
    d = f // 2
    total = rows * shards
    scale = 1.0 / math.sqrt(HDIM)
    feats = qkv_weight.shape[0]
    units = fc_in_weight.shape[1]
    head_cols = qkv_weight.shape[2]
    heads_here = head_cols // HDIM
    hd = qkv_bias.shape[2]
    ub = fc_in_bias.shape

    match = subset_ids[:, None] == jnp.arange(SUBSETS, dtype=jnp.int32)[None, :]
    counts = jnp.sum(match.astype(F32), axis=0)
    vecs = [norm1_gain, norm1_shift, norm2_gain, norm2_shift, dense_bias, fc_out_bias]
    pack = jnp.concatenate(
        [v.astype(F32) for v in vecs]
        + [qkv_bias.astype(F32).reshape(-1), fc_in_bias.astype(F32).reshape(-1), counts]
    )
    size = pack.shape[0]
    lanes = -(-size // 1024) * 128
    got = exchange(jnp.pad(pack, (0, 8 * lanes - size)).reshape(8, lanes), "fsdp", False, 1)
    got = got.reshape(shards, 8 * lanes)
    gain1, shift1, gain2, shift2, b_dense, b_out = [
        got[:, k * feats : (k + 1) * feats].reshape(width) for k in range(6)
    ]
    at = 6 * feats
    nq = 3 * heads_here * hd
    b_qkv = got[:, at : at + nq].reshape(shards, 3, heads_here, hd)
    b_qkv = b_qkv.transpose(1, 2, 0, 3).reshape(3, heads_here, HDIM)
    b_qkv = lax.dynamic_index_in_dim(b_qkv, i, 1, keepdims=False).reshape(3 * HDIM)
    at += nq
    b_in = got[:, at : at + units // shards].reshape(shards, ub[0], ub[1])
    b_in = half_of(b_in.transpose(1, 0, 2).reshape(units), i, 0)
    at += units // shards
    counts = jnp.sum(got[:, at : at + SUBSETS], axis=0)
    table = total / (SUBSETS * counts)
    row_scale = jnp.sum(jnp.where(match, table[None, :], 0.0), axis=1)
    carried = cotangent.astype(F32) * row_scale[:, None]
    grad_here = carried.astype(BF16)

    wi = fc_in_weight.reshape(feats, 2, 2, units // 4).transpose(1, 0, 2, 3)
    wo = fc_out_weight.reshape(2, 2, units // 4, feats).transpose(0, 3, 1, 2)
    w2 = jnp.concatenate(
        [
            qkv_weight.reshape(feats, 3, heads_here, HDIM).transpose(2, 0, 1, 3).reshape(2, feats, 3 * HDIM),
            dense_weight.reshape(heads_here, HDIM, feats).transpose(0, 2, 1),
            wi[:, :, 0], wo[:, :, 0], wi[:, :, 1], wo[:, :, 1],
        ],
        axis=2,
    )
    plane = 2 * rows
    start_row = d * plane
    reach = min(dp - 1, -(-(SEQ_LEN - 1) // plane))
    here = start_row + jnp.arange(plane, dtype=jnp.int32)
    docs_here, pos_here = locate(here, seq_starts)
    first = (here - pos_here.astype(jnp.int32)) - (start_row - reach * plane)
    cosine, sine = rotary_tables(pos_here)
    ones = jnp.ones((plane, 128 - ROT), F32)
    none = jnp.zeros((plane, 128 - ROT), F32)
    tabs = jnp.stack(
        [
            jnp.concatenate([cosine, cosine, ones], 1),
            jnp.concatenate([-sine, sine, none], 1),
        ]
    )
    vecs = jnp.stack([gain1, shift1, gain2, shift2] + [jnp.zeros_like(gain1)] * 4)
    dims = (rows, width, feats, dp, reach)
    part_w = width // tps
    offset = t * part_w
    cut = lambda vec: lax.dynamic_slice_in_dim(vec, offset, part_w, vec.ndim - 1)
    bias = (cut(b_dense) + cut(b_out)).reshape(1, -1)
    carried_here = cut(cotangent).astype(F32) * row_scale[:, None]
    _, _, _, mixed, tokens_grad, norm_grads, bias_sums, g_qkv, g_dense, g_in, g_out = block(
        tokens, grad_here, w2, vecs, b_qkv.reshape(1, -1), b_in.reshape(1, -1), bias, carried_here, tabs,
        first[:, None], dims,
    )
    qkv_weight_grad = g_qkv.transpose(1, 0, 2).astype(F32)
    dense_weight_grad = g_dense.astype(F32)
    fc_in_weight_grad = g_in.astype(F32)
    fc_out_weight_grad = g_out.astype(F32)
    bias_grad = norm_grads[4]

    bias_sums = jnp.sum(bias_sums.reshape(dp, 2, 8, units // 2), axis=0)
    in_bias_grad = bias_sums[:, 0].reshape(ub[0], shards * ub[1])
    in_bias_grad = lax.dynamic_slice_in_dim(in_bias_grad, f * ub[1], ub[1], 1)
    qkv_bias_grad = bias_sums[:, 1, : 3 * HDIM].reshape(2, 3, HDIM).transpose(1, 0, 2)
    qkv_bias_grad = lax.dynamic_slice_in_dim(qkv_bias_grad, f * hd, hd, 2)
    return (
        mixed,
        tokens_grad,
        qkv_weight_grad,
        qkv_bias_grad,
        dense_weight_grad,
        bias_grad,
        fc_in_weight_grad,
        in_bias_grad,
        fc_out_weight_grad,
        bias_grad,
        norm_grads[0],
        norm_grads[1],
        norm_grads[2],
        norm_grads[3],
    )


def solution(mesh):
    in_specs = (
        P("fsdp", None),
        P("fsdp", None, "tp"),
        P(None, "tp", "fsdp"),
        P("tp", "fsdp"),
        P("fsdp"),
        P("fsdp", "tp"),
        P("tp", "fsdp"),
        P("tp", "fsdp"),
        P("fsdp"),
        P("fsdp"),
        P("fsdp"),
        P("fsdp"),
        P("fsdp"),
        P("fsdp", None),
        P("fsdp"),
        P(),
    )
    out_specs = (
        P("fsdp", "tp"),
        P("fsdp", "tp"),
        P("fsdp", None, "tp"),
        P(None, "tp", "fsdp"),
        P("tp", "fsdp"),
        P("fsdp"),
        P("fsdp", "tp"),
        P("tp", "fsdp"),
        P("tp", "fsdp"),
        P("fsdp"),
        P("fsdp"),
        P("fsdp"),
        P("fsdp"),
        P("fsdp"),
    )
    return jax.shard_map(
        on_device, mesh=mesh, in_specs=in_specs, out_specs=out_specs, check_vma=False
    )
```

```python
import functools
import math

import jax
import jax.numpy as jnp
from jax import lax
from jax.experimental import pallas as pl
from jax.experimental.pallas import tpu as pltpu
from jax.sharding import PartitionSpec as P

HDIM = 256
ROT = 64
SUBSETS = 22
SEQ_LEN = 2048
EPS = 1e-05
F32 = jnp.float32
BF16 = jnp.bfloat16
MESH = pl.DeviceIdType.MESH
ANY = pl.BlockSpec(memory_space=pl.ANY)
VMEM = pl.BlockSpec(memory_space=pltpu.VMEM)


def mm(left, right, dims):
    return lax.dot_general(left, right, (dims, ((), ())), preferred_element_type=F32)


def plain(left, right):
    return mm(left, right, ((1,), (0,)))


def inner(left, right):
    return mm(left, right, ((0,), (0,)))


def against(left, right):
    return mm(left, right, ((1,), (1,)))


def rotary_tables(positions):
    half = ROT // 2
    steps = jnp.arange(half, dtype=F32)
    freq = 1.0 / 10000.0 ** (steps * 2.0 / ROT)
    angle = positions[:, None] * freq[None, :]
    return jnp.cos(angle), jnp.sin(angle)


def locate(indices, starts):
    above = indices[:, None] >= starts[None, :]
    doc_ids = jnp.sum(above.astype(jnp.int32), axis=1) - 1
    pick = doc_ids[:, None] == jnp.arange(starts.shape[0], dtype=jnp.int32)[None, :]
    first = jnp.sum(jnp.where(pick, starts[None, :], 0), axis=1)
    return (doc_ids, (indices - first).astype(F32))


def half_of(value, which, axis):
    size = value.shape[axis] // 2
    return lax.dynamic_slice_in_dim(value, which * size, size, axis)


def exchange_kernel(axis, spread, v_ref, o_ref, ssem, rsem):
    count = o_ref.shape[0]
    me = lax.axis_index(axis)

    def peer(step):
        return lax.rem(me + step, count)

    barrier = pltpu.get_barrier_semaphore()
    for step in range(1, count):
        pl.semaphore_signal(barrier, 1, device_id={axis: peer(step)}, device_id_type=MESH)
    pl.semaphore_wait(barrier, count - 1)

    def copy(step):
        return pltpu.make_async_remote_copy(
            src_ref=v_ref.at[peer(step)] if spread else v_ref,
            dst_ref=o_ref.at[me],
            send_sem=ssem.at[step],
            recv_sem=rsem.at[step],
            device_id={axis: peer(step)},
            device_id_type=MESH,
        )

    for step in range(1, count):
        copy(step).start()
    o_ref[me] = v_ref[me] if spread else v_ref[...]
    for step in range(1, count):
        copy(step).wait()


def exchange(value, axis, spread, cid):
    count = lax.axis_size(axis)
    block = value.shape[1:] if spread else value.shape
    return pl.pallas_call(
        functools.partial(exchange_kernel, axis, spread),
        out_shape=jax.ShapeDtypeStruct((count,) + block, value.dtype),
        in_specs=[VMEM],
        out_specs=VMEM,
        scratch_shapes=[pltpu.SemaphoreType.DMA((count,)), pltpu.SemaphoreType.DMA((count,))],
        compiler_params=pltpu.CompilerParams(collective_id=cid, has_side_effects=True),
        name="exchange",
    )(value)


GROUPS = 3
ORDER = (
    "own1o", "pair0", "pair2", "own0i", "pair1", "rx0", "own0o", "mate0i", "own1i", "mate0o", "arr01",
    "own2i", "arr02", "mate1i", "mate1o", "rx1", "rc0", "arr03", "rc1", "stats", "arr11", "mate2i", "arr12",
    "proj", "datt", "arr13", "ffn0", "kv1k", "st13i", "kv1v", "qd1", "kv2k", "mate2o", "st12i", "kv2v",
    "own2o", "att0", "att1", "arr21", "st12o", "st11i", "att2", "att3", "arr22", "qd2", "sta3i", "st11o",
    "sta2i", "sta2o", "ls0", "sta1i", "arr23", "ffn1", "st23i", "sta1o", "out", "ls1", "dkv0", "fin1",
    "far00", "far01", "st22i", "st22o", "fina", "dkv1", "mt0", "dkv2", "st21i", "dkv3", "st21o", "last0",
    "stb3i", "hid", "qk", "stb2i", "stb2o", "far10", "fin2", "far11", "stb1i", "stb1o", "small", "mt1",
    "finb", "last1",
)


def turn(u, tabs, at, sign):
    lo, hi = u[:, :128], u[:, 128:]
    lane = lax.broadcasted_iota(jnp.int32, lo.shape, 1)
    other = jnp.where(lane < ROT // 2, pltpu.roll(lo, 128 - ROT // 2, 1), pltpu.roll(lo, ROT // 2, 1))
    a = other * tabs[1, at, :]
    lo = lo * tabs[0, at, :] + (a if sign > 0 else -a)
    return jnp.concatenate([lo, hi], axis=1)


def block_kernel(
    dims,
    tok, gh, w2, vecs, bq, bin_, bias, carried, tabs, firstq,
    wa_o, w0_o, w1_o, mixed_o, dtok_o, norm_o, bias_o, dq_o, dd_o, di_o, do_o,
    xs, gs, wbuf, wk, wv, wq, wd, st, act, dpre, dqkv, att, tpr0, tpr1, tpr2,
    rs_a, rs_f, norms, tra, trf, sums, bsum, sum_s, sum_r, row_r, nrm_r,
    lsem, tsem, psem, zsem, zrec, ksem, qsem, lssem, ssem, rsem, fsem, bsem, xsem, usem, near_ok, far_ok, mate_ok,
):
    R, D, feats, dp, reach = dims
    F, T = 2 * dp, tpr0.shape[0] * 2
    f = lax.axis_index("fsdp")
    t = lax.axis_index("tp")
    d, i = f // 2, lax.rem(f, 2)
    core = lax.rem(t, 2)
    plane, pf = 2 * R, 2 * feats
    qb = min(256, plane)
    nb = plane // qb
    fb = min(256, pf)
    gw = w2.shape[2] // GROUPS
    hu = gw // 2
    pw = D // T
    tn, tf = t + 1 - 2 * core, lax.rem(t + 2, T)
    mate, near, far = (f + 1 - 2 * i, t), (f, tn), (f, tf)
    has = (d + 1 < dp, d >= 1)
    inward = jnp.where(d < dp // 2, 0, 1)
    ways = {"i": inward, "o": 1 - inward}
    outs = (wa_o, w0_o, w1_o)
    scale = 1.0 / math.sqrt(HDIM)

    barrier = pltpu.get_barrier_semaphore()
    for s in range(1, F):
        pl.semaphore_signal(barrier, 1, device_id=(lax.rem(f + s, F), t), device_id_type=MESH)
    for s in range(1, T):
        pl.semaphore_signal(barrier, 1, device_id=(f, lax.rem(t + s, T)), device_id_type=MESH)
    pl.semaphore_wait(barrier, F + T - 2)

    def rc(src, dst, ss, rv, who):
        return pltpu.make_async_remote_copy(
            src_ref=src, dst_ref=dst, send_sem=ss, recv_sem=rv, device_id=who, device_id_type=MESH
        )

    def rows(b):
        return pl.ds(pl.multiple_of(b * qb, qb), qb)

    def toward(way):
        return (f + 2 - 4 * way, t)

    def open_way(way):
        return jnp.where(way == 0, d + 1 < dp, d >= 1)

    def slot(g, s):
        return outs[g].at[pl.ds(s * feats, feats), :]

    def part(half, g):
        return w2.at[half, :, pl.ds(g * gw, gw)]

    def pair_copy(g):
        return rc(part(1 - i, g), slot(g, f), psem.at[0, g], psem.at[1, g], mate)

    def mine_copy(g):
        return pltpu.make_async_copy(part(i, g), slot(g, f), lsem.at[g])

    def z_own(g, way):
        return rc(part(i, g), slot(g, f), zsem.at[g, 0, way, 0], zrec.at[g, f], toward(way))

    def z_mate(g, way):
        s = f + 1 - 2 * i
        return rc(slot(g, s), slot(g, s), zsem.at[g, 0, way, 1], zrec.at[g, s], toward(way))

    def z_fwd(g, k, way, j):
        s = (d - k) * 2 + j if way == 0 else (d + k) * 2 + j
        return rc(slot(g, s), slot(g, s), zsem.at[g, k, way, j], zrec.at[g, s], toward(way))

    def send_own(g, io):
        @pl.when(open_way(ways[io]))
        def _():
            z_own(g, ways[io]).start()

    def send_mate(g, io, wait):
        if wait:
            pair_copy(g).wait_recv()

        @pl.when(open_way(ways[io]))
        def _():
            z_mate(g, ways[io]).start()

    def from_dist(k, way):
        return d >= k if way == 0 else d + k < dp

    def arrive(g, k):
        for way in range(2):
            @pl.when(from_dist(k, way))
            def _():
                for j in range(2):
                    z_fwd(g, k, way, j).wait_recv()

                    @pl.when(has[way])
                    def _():
                        z_fwd(g, k, way, j).start()

    def gather_sent(g):
        pair_copy(g).wait_send()
        for way in range(2):
            @pl.when(has[way])
            def _():
                z_own(g, way).wait_send()
                z_mate(g, way).wait_send()
            for k in range(1, dp - 1):
                @pl.when(from_dist(k, way) & has[way])
                def _():
                    for j in range(2):
                        z_fwd(g, k, way, j).wait_send()

    def load(*pairs):
        copies = [pltpu.make_async_copy(src, dst, bsem.at[n]) for n, (src, dst) in enumerate(pairs)]
        for c in copies:
            c.start()
        for c in copies:
            c.wait()

    hr = R // 2
    given = ((tok, xs), (gh, gs))

    def rows_x(a):
        ref, out = given[a]
        return rc(
            ref.at[pl.ds(core * hr, hr), :], out.at[pl.ds(i * R + core * hr, hr), :],
            tsem.at[a, 0], tsem.at[a, 1], mate,
        )

    def rows_c(a):
        at = given[a][1].at[pl.ds((1 - i) * R + core * hr, hr), :]
        return rc(at, at, tsem.at[a, 2], tsem.at[a, 3], near)

    def rows_own(a):
        ref, out = given[a]
        return pltpu.make_async_copy(ref, out.at[pl.ds(i * R, R), :], lsem.at[GROUPS + a])

    def rows_on(a):
        rows_x(a).wait_recv()
        rows_c(a).start()

    def rows_done(a):
        rows_c(a).wait_recv()
        rows_own(a).wait()

    def hat(at):
        return (xs[at, :].astype(F32) - norms[at, 0:1]) * norms[at, 1:2]

    def stats():
        def block(b, _):
            x = xs[rows(b), :].astype(F32)
            m = jnp.mean(x, axis=-1, keepdims=True)
            c = x - m
            norms[rows(b), 0:1] = m
            norms[rows(b), 1:2] = lax.rsqrt(jnp.mean(c * c, axis=-1, keepdims=True) + EPS)
            return 0

        rows_done(0)
        lax.fori_loop(0, nb, block, 0)

    def proj():
        def block(b, _):
            at = rows(b)
            h1 = (hat(at) * vecs[0:1, :] + vecs[1:2, :]).astype(BF16)
            y = plain(h1, wbuf[:, : 3 * HDIM]) + bq[...]
            wq[0, at, :] = (turn(y[:, :HDIM], tabs, at, 1).astype(BF16).astype(F32) * scale).astype(BF16)
            wk[reach, at, :] = turn(y[:, HDIM : 2 * HDIM], tabs, at, 1).astype(BF16)
            wv[reach, at, :] = y[:, 2 * HDIM :].astype(BF16)
            return 0

        mine_copy(0).wait()
        load((wa_o, wbuf))
        lax.fori_loop(0, nb, block, 0)

        @pl.when(has[0])
        def _():
            kv_copy(0, 0).start()
            kv_copy(1, 0).start()

    def datt():
        def block(b, _):
            at = rows(b)
            wd[0, at, :] = plain(gs[at, :], wbuf[:, 3 * HDIM :]).astype(BF16)
            return 0

        rows_done(1)
        lax.fori_loop(0, nb, block, 0)

        @pl.when(has[1])
        def _():
            qd_copy(0, 0).start()
            qd_copy(1, 0).start()

    def ffn(h):
        mine = slice(h * hu, (h + 1) * hu)

        def block(b, _):
            at = rows(b)
            h2 = (hat(at) * vecs[2:3, :] + vecs[3:4, :]).astype(BF16)
            pre = plain(h2, wbuf[:, :hu]) + bin_[:, mine]
            cdf = 0.5 * (1.0 + lax.erf(pre * (1.0 / math.sqrt(2.0))))
            act[at, mine] = (pre * cdf).astype(BF16)
            slope = cdf + pre * jnp.exp(-0.5 * pre * pre) * (1.0 / math.sqrt(2.0 * math.pi))
            dp_b = (plain(gs[at, :], wbuf[:, hu:]) * slope).astype(BF16)
            dpre[at, mine] = dp_b
            bsum[0:1, mine] += jnp.sum(dp_b.astype(F32), axis=0, keepdims=True)
            return 0

        mine_copy(1 + h).wait()
        load((outs[1 + h], wbuf))
        lax.fori_loop(0, nb, block, 0)

    def kv_copy(h, k):
        w = (wk, wv)[h]
        return rc(w.at[reach - k], w.at[reach - k - 1], ksem.at[h, 0, k], ksem.at[h, 1, k + 1], toward(0))

    def kv_recv(h, k):
        w = (wk, wv)[h]
        return rc(w.at[reach - k], w.at[reach - k], ksem.at[h, 0, k - 1], ksem.at[h, 1, k], toward(0))

    def kv_step(h, k):
        @pl.when(d >= k)
        def _():
            kv_recv(h, k).wait_recv()
            if k < reach:
                @pl.when(has[0])
                def _():
                    kv_copy(h, k).start()

        @pl.when(d < k)
        def _():
            (wk, wv)[h][reach - k] = jnp.zeros((plane, HDIM), BF16)

    def qd_copy(h, k):
        w = (wq, wd)[h]
        return rc(w.at[k], w.at[k + 1], qsem.at[h, 0, k], qsem.at[h, 1, k + 1], toward(1))

    def qd_recv(h, k):
        w = (wq, wd)[h]
        return rc(w.at[k], w.at[k], qsem.at[h, 0, k - 1], qsem.at[h, 1, k], toward(1))

    def qd_step(k):
        @pl.when(d + k < dp)
        def _():
            for h in range(2):
                qd_recv(h, k).wait_recv()
                if k < reach:
                    @pl.when(has[1])
                    def _():
                        qd_copy(h, k).start()

        @pl.when(d + k >= dp)
        def _():
            for h in range(2):
                (wq, wd)[h][k] = jnp.zeros((plane, HDIM), BF16)

    def stat_at(k):
        return st.at[:, pl.ds(k * plane, plane)]

    def stat_copy(k):
        return rc(stat_at(0), stat_at(k), lssem.at[0, k], lssem.at[1, k], (f - 2 * k, t))

    def stat_send():
        for k in range(1, reach + 1):
            @pl.when(d >= k)
            def _():
                stat_copy(k).start()

    def stat_wait():
        for k in range(1, reach + 1):
            @pl.when(d + k < dp)
            def _():
                stat_copy(k).wait_recv()

            @pl.when(d + k >= dp)
            def _():
                st[:, k * plane : (k + 1) * plane] = jnp.zeros((8, plane), F32)

    span = SEQ_LEN + qb
    base = reach * plane - SEQ_LEN
    parts = 4

    def attention(n):
        def block(b, _):
            at = rows(b)
            keys_at = pl.ds(pl.multiple_of(base + b * qb, qb), span)
            keys = wk.reshape((reach + 1) * plane, HDIM)[keys_at, :]
            vals = wv.reshape((reach + 1) * plane, HDIM)[keys_at, :]
            s = against(wq[0, at, :], keys)
            c = base + b * qb + lax.broadcasted_iota(jnp.int32, (qb, span), 1)
            r = reach * plane + b * qb + lax.broadcasted_iota(jnp.int32, (qb, span), 0)
            low = jnp.broadcast_to(firstq[:, at].astype(F32), (128, qb)).T[:, 0:1] + float(reach * plane)
            s = jnp.where((c.astype(F32) >= low) & (c <= r), s, -1e30)
            top = jnp.max(s, axis=1, keepdims=True)
            e = jnp.exp(s - top)
            total = jnp.sum(e, axis=1, keepdims=True)
            p = e * (1.0 / total)
            att[at, :] = plain(p.astype(BF16), vals).astype(BF16)
            dpr = against(wd[0, at, :], vals)
            delta = jnp.sum(p * dpr, axis=1, keepdims=True)
            ds = (p * (dpr - delta)).astype(BF16)
            dq = plain(ds, keys) * scale
            dqkv[at, :HDIM] = turn(dq, tabs, at, -1).astype(BF16)
            lane = lax.broadcasted_iota(jnp.int32, (qb, 128), 1)
            both = jnp.where(lane == 0, top + jnp.log(total), jnp.where(lane == 1, delta, 0.0))
            st[:, at] = both.T[:8]
            return 0

        lax.fori_loop(n * nb // parts, (n + 1) * nb // parts, block, 0)

    def key_grads(n):
        def block(b, _):
            at = rows(b)
            rows_at = pl.ds(pl.multiple_of(b * qb, qb), span)
            q = wq.reshape((reach + 1) * plane, HDIM)[rows_at, :]
            da = wd.reshape((reach + 1) * plane, HDIM)[rows_at, :]
            s = against(wk[reach, at, :], q)
            c = b * qb + lax.broadcasted_iota(jnp.int32, (qb, span), 0)
            r = b * qb + lax.broadcasted_iota(jnp.int32, (qb, span), 1)
            s = jnp.where((c >= firstq[:, rows_at]) & (c <= r), s - st[0:1, rows_at], -1e30)
            p = jnp.exp(s)
            dqkv[at, 2 * HDIM :] = plain(p.astype(BF16), da).astype(BF16)
            dpr = against(wv[reach, at, :], da)
            ds = (p * (dpr - st[1:2, rows_at])).astype(BF16)
            dqkv[at, HDIM : 2 * HDIM] = turn(plain(ds, q), tabs, at, -1).astype(BF16)
            return 0

        lax.fori_loop(n * nb // parts, (n + 1) * nb // parts, block, 0)

    def rs(g):
        return rs_a.at[g] if g < 2 else rs_f.at[g - 2]

    def grad_part(g, p, c):
        cols = pl.ds(pl.multiple_of(p * pf + c * fb, fb), fb)
        z = (xs[:, cols].astype(F32) - norms[:, 0:1]) * norms[:, 1:2]
        n = 0 if g < 2 else 2
        h = (z * vecs[n : n + 1, cols] + vecs[n + 1 : n + 2, cols]).astype(BF16)
        if g == 0:
            return inner(h, dqkv[:, :HDIM]), inner(gs[:, cols], att[...])
        if g == 1:
            return (inner(h, dqkv[:, HDIM:]),)
        mine = slice((g - 2) * hu, (g - 1) * hu)
        return inner(h, dpre[:, mine]), inner(gs[:, cols], act[:, mine])

    def add_part(g, p, second=None):
        def block(c, _):
            at = pl.ds(pl.multiple_of(c * fb, fb), fb)
            left = 0
            for v in grad_part(g, p, c):
                cols = slice(left, left + v.shape[1])
                left += v.shape[1]
                v = rs(g)[p, at, cols].astype(F32) + v
                if second is not None:
                    v = v + rs(g)[second, at, cols].astype(F32)
                rs(g)[p, at, cols] = v.astype(BF16)
            return 0

        lax.fori_loop(0, pf // fb, block, 0)

    def rs_copy(g, k, way):
        p = d + k * (1 - 2 * way)
        to = jnp.where((way == 1) & (k == 1), dp, p)
        return rc(rs(g).at[p], rs(g).at[to], ssem.at[g, k, way], rsem.at[g, to], toward(way))

    def rs_wait(g, p):
        return rc(rs(g).at[p], rs(g).at[p], ssem.at[g, 0, 0], rsem.at[g, p], mate)

    def clear(g, p):
        rs(g)[p] = jnp.zeros(rs(g).shape[1:], BF16)

    def stage(g, k, io):
        way = ways[io]
        p = d + k * (1 - 2 * way)
        came = open_way(1 - way)

        @pl.when((p >= 0) & (p < dp))
        def _():
            @pl.when(came)
            def _():
                rs_wait(g, p).wait_recv()

            @pl.when(jnp.logical_not(came))
            def _():
                clear(g, p)

            add_part(g, p)
            rs_copy(g, k, way).start()

    def final_copies(g):
        lo = pl.multiple_of(i * HDIM, HDIM)
        pieces = []
        for j in range(2):
            at = pl.ds((i if j == 0 else 1 - i) * feats, feats)
            src = rs(g).at[d, at]
            if g == 0:
                dst = (dq_o.at[0, :, pl.ds(lo, HDIM)], dd_o.at[pl.ds(lo, HDIM), :])
                src = (src.at[:, pl.ds(0, HDIM)], tra.at[j])
            elif g == 1:
                dst = tuple(dq_o.at[n, :, pl.ds(lo, HDIM)] for n in (1, 2))
                src = tuple(src.at[:, pl.ds(n * HDIM, HDIM)] for n in (0, 1))
            else:
                u = pl.multiple_of(i * gw + (g - 2) * hu, hu)
                dst = (di_o.at[:, pl.ds(u, hu)], do_o.at[pl.ds(u, hu), :])
                src = (src.at[:, pl.ds(0, hu)], trf.at[g - 2, j])
            for n in range(2):
                if j == 0:
                    pieces.append(pltpu.make_async_copy(src[n], dst[n], fsem.at[g, n, 0]))
                else:
                    pieces.append(rc(src[n], dst[n], fsem.at[g, n, 1], fsem.at[g, n, 2], mate))
        return pieces

    def final(g):
        for p, came in ((d, has[1]), (dp, has[0])):
            @pl.when(came)
            def _():
                rs_wait(g, p).wait_recv()

            @pl.when(jnp.logical_not(came))
            def _():
                clear(g, p)

        add_part(g, d, dp)
        if g != 1:
            cut = HDIM if g == 0 else hu
            for j in range(2):
                at = pl.ds(pl.multiple_of((i if j == 0 else 1 - i) * feats, feats), feats)
                turned = rs(g)[d, at, cut:].astype(F32).T.astype(BF16)
                if g == 0:
                    tra[j] = turned
                else:
                    trf[g - 2, j] = turned
        for c in final_copies(g):
            c.start()

    def out_step(up, wdense):
        def block(b, _):
            at = rows(b)
            sums[4:5, :] += jnp.sum(gs[at, :].astype(F32), axis=0, keepdims=True)
            for c in range(T):
                cols = slice(c * pw, (c + 1) * pw)
                y = against(att[at, :], wdense[cols, :]) + against(act[at, :], wbuf[cols, :])
                up[c, at, :] = y.astype(BF16)
            return 0

        load(
            (w0_o.at[:, pl.ds(hu, hu)], wbuf.at[:, pl.ds(0, hu)]),
            (w1_o.at[:, pl.ds(hu, hu)], wbuf.at[:, pl.ds(hu, hu)]),
            (wa_o.at[:, pl.ds(3 * HDIM, HDIM)], wdense),
            (carried, env["kept"]),
        )
        lax.fori_loop(0, nb, block, 0)
        tp_near(up, False)

    def hidden_step(up):
        def block(b, _):
            at = rows(b)
            e2 = against(dpre[at, :], wbuf[...])
            z = hat(at)
            sums[2:3, :] += jnp.sum(e2 * z, axis=0, keepdims=True)
            sums[3:4, :] += jnp.sum(e2, axis=0, keepdims=True)
            u = (e2 * vecs[2:3, :]).astype(BF16)
            for c in range(T):
                up[c, at, :] = u[:, c * pw : (c + 1) * pw]
            return 0

        load(
            (w0_o.at[:, pl.ds(0, hu)], wbuf.at[:, pl.ds(0, hu)]),
            (w1_o.at[:, pl.ds(0, hu)], wbuf.at[:, pl.ds(hu, hu)]),
        )
        lax.fori_loop(0, nb, block, 0)

    def qkv_step(up):
        def block(b, _):
            at = rows(b)
            e1 = against(dqkv[at, :], wbuf[:, : 3 * HDIM])
            z = hat(at)
            sums[0:1, :] += jnp.sum(e1 * z, axis=0, keepdims=True)
            sums[1:2, :] += jnp.sum(e1, axis=0, keepdims=True)
            bsum[1:2, : 3 * HDIM] += jnp.sum(dqkv[at, :].astype(F32), axis=0, keepdims=True)
            u = e1 * vecs[0:1, :]
            for c in range(T):
                up[c, at, :] = (up[c, at, :].astype(F32) + u[:, c * pw : (c + 1) * pw]).astype(BF16)
            return 0

        load((wa_o, wbuf))
        lax.fori_loop(0, nb, block, 0)
        tp_near(up, True)
        for s in range(F):
            sum_s[s] = sums[:, s * feats : (s + 1) * feats]
        for s in range(1, F):
            sum_copy(s).start()
            bias_copy(s).start()
        sum_r[f] = sum_s[f]
        bias_o[f] = bsum[...]

    def half(h):
        return pl.ds(pl.multiple_of((1 - i if h == 0 else i) * R, R), R)

    def half_block(h, b):
        return pl.ds(pl.multiple_of((1 - i if h == 0 else i) * R + b * qb, qb), qb)

    def near_copy(up, h, j):
        blk = tn if j == 0 else lax.rem(tn + 2, T)
        n = 2 * h + j
        return rc(up.at[blk, half(h)], tpr0.at[j, half(h)], usem.at[0, n], usem.at[1, n], near)

    def far_copy(up, h):
        return rc(up.at[tf, half(h)], tpr1.at[half(h)], usem.at[0, 4 + h], usem.at[1, 4 + h], far)

    def mate_copy(up):
        return rc(up.at[t, half(0)], tpr2, usem.at[0, 6], usem.at[1, 6], mate)

    def tp_near(up, second):
        if second:
            pl.semaphore_wait(near_ok, 1)
        for h in range(2):
            for j in (1, 0):
                near_copy(up, h, j).start()

    def tp_far(up, second, h):
        def block(b, _):
            at = half_block(h, b)
            up[tf, at, :] = (up[tf, at, :].astype(F32) + tpr0[1, at, :].astype(F32)).astype(BF16)
            return 0

        near_copy(up, h, 1).wait_recv()
        lax.fori_loop(0, R // qb, block, 0)
        if second and h == 0:
            pl.semaphore_wait(far_ok, 1)
        far_copy(up, h).start()

    def tp_mate(up, second):
        def block(b, _):
            at = half_block(0, b)
            v = up[t, at, :].astype(F32) + tpr0[0, at, :].astype(F32) + tpr1[at, :].astype(F32)
            up[t, at, :] = v.astype(BF16)
            return 0

        near_copy(up, 0, 0).wait_recv()
        far_copy(up, 0).wait_recv()
        lax.fori_loop(0, R // qb, block, 0)
        if second:
            pl.semaphore_wait(mate_ok, 1)
        mate_copy(up).start()

    def tp_last(up, second):
        near_copy(up, 1, 0).wait_recv()
        far_copy(up, 1).wait_recv()
        mate_copy(up).wait_recv()
        here = half(1)
        v = up[t, here, :].astype(F32) + tpr0[0, here, :].astype(F32) + tpr1[here, :].astype(F32)
        v = v + tpr2[...].astype(F32)
        x = xs[here, pl.ds(pl.multiple_of(t * pw, pw), pw)].astype(F32)
        if second:
            u = v
            z = (x - norms[here, 0:1]) * norms[here, 1:2]
            lane = lax.broadcasted_iota(jnp.int32, (R, 128), 1)
            one, two = jnp.sum(u, axis=1, keepdims=True), jnp.sum(u * z, axis=1, keepdims=True)
            row_r[t] = jnp.where(lane == 0, one, jnp.where(lane == 1, two, 0.0)).T[:8]
            for s in range(1, T):
                row_copy(s).start()
            for s in range(1, T):
                row_copy(s).wait()
            both = row_r[0]
            for s in range(1, T):
                both = both + row_r[s]
            both = jnp.concatenate([both, jnp.zeros((120, R), F32)], axis=0).T * (1.0 / D)
            dx = norms[here, 1:2] * (u - both[:, 0:1] - z * both[:, 1:2])
            dtok_o[...] = (env["kept"][...] + dx).astype(BF16)
        else:
            mixed_o[...] = (x + v + bias[...]).astype(BF16)
            pl.semaphore_signal(near_ok, 1, device_id=near, device_id_type=MESH)
            pl.semaphore_signal(far_ok, 1, device_id=far, device_id_type=MESH)
            pl.semaphore_signal(mate_ok, 1, device_id=mate, device_id_type=MESH)
        for h in range(2):
            near_copy(up, h, 0).wait_send()
            near_copy(up, h, 1).wait_send()
            far_copy(up, h).wait_send()
        mate_copy(up).wait_send()

    def row_copy(s):
        return rc(row_r.at[t], row_r.at[t], xsem.at[0, 0, s], xsem.at[0, 1, s], (f, lax.rem(t + s, T)))

    def norm_copy(s):
        return rc(nrm_r.at[t], nrm_r.at[t], xsem.at[1, 0, s], xsem.at[1, 1, s], (f, lax.rem(t + s, T)))

    def sum_copy(s):
        to = lax.rem(f + s, F)
        return rc(sum_s.at[to], sum_r.at[f], xsem.at[2, 0, s], xsem.at[2, 1, s], (to, t))

    def bias_copy(s):
        return rc(bsum, bias_o.at[f], xsem.at[3, 0, s], xsem.at[3, 1, s], (lax.rem(f + s, F), t))

    def small_sums():
        for s in range(1, F):
            sum_copy(s).wait()
            bias_copy(s).wait()
        v = sum_r[0]
        for s in range(1, F):
            v = v + sum_r[s]
        nrm_r[t] = v
        for s in range(1, T):
            norm_copy(s).start()
        for s in range(1, T):
            norm_copy(s).wait()
        both = nrm_r[0]
        for s in range(1, T):
            both = both + nrm_r[s]
        row = lax.broadcasted_iota(jnp.int32, both.shape, 0)
        norm_o[...] = jnp.where(row == 4, v * 0.5, both)

    env = {}
    far_out = tuple(range(dp - 1, 2, -1))
    groups = {"a": 0, "b": 1, "1": 2, "2": 3}
    paired = set()

    def step(name):
        kind, rest = name.rstrip("0123456789abiokv"), ""
        rest = name[len(kind):]
        if kind == "pair":
            pair_copy(int(rest)).start()
            mine_copy(int(rest)).start()
        elif kind == "own":
            send_own(int(rest[0]), rest[1])
        elif kind == "mate":
            send_mate(int(rest[0]), rest[1], rest[0] not in paired)
            paired.add(rest[0])
        elif kind == "arr":
            g, k = int(rest[0]), int(rest[1])
            for n in range(k, dp if k == 3 else k + 1):
                arrive(g, n)
        elif kind == "rx":
            rows_x(int(rest)).start()
            rows_own(int(rest)).start()
        elif kind == "rc":
            rows_on(int(rest))
        elif kind == "stats":
            stats()
        elif kind == "proj":
            proj()
        elif kind == "datt":
            datt()
        elif kind == "ffn":
            ffn(int(rest))
        elif kind == "att":
            attention(int(rest))
        elif kind == "qd":
            for k in range(1, reach) if rest == "1" else (reach,):
                qd_step(k)
        elif kind == "ls":
            stat_send() if rest == "0" else stat_wait()
        elif kind == "d":
            key_grads(int(rest[-1]))
        elif kind == "st":
            g, k, io = groups[rest[0]], int(rest[1]), rest[2]
            if k == 3:
                for n in far_out:
                    stage(g, n, io)
            elif k == 2 and io == "o":
                for n in far_out + (2,):
                    stage(g, n, io)
            else:
                stage(g, k, io)
        elif kind == "fin":
            final(groups[rest])
        elif kind == "out":
            out_step(env["up"], env["wd"])
        elif kind == "far":
            tp_far(env["up"], rest[0] == "1", int(rest[1]))
        elif kind == "mt":
            tp_mate(env["up"], rest == "1")
        elif kind == "last":
            tp_last(env["up"], rest == "1")
        elif kind == "hid":
            hidden_step(env["up"])
        elif kind == "q":
            qkv_step(env["up"])
        elif kind == "small":
            small_sums()
        else:
            hop = int(rest[-2])
            for k in range(1, reach) if hop == 1 else (reach,):
                kv_step("kv".index(rest[-1]), k)

    def finish_scope(up, wd, kept):
        env["up"], env["wd"], env["kept"] = up, wd, kept
        for name in ORDER[ORDER.index("out") :]:
            step(name)

    sums[...] = jnp.zeros_like(sums)
    bsum[...] = jnp.zeros_like(bsum)
    for name in ORDER[: ORDER.index("out")]:
        step(name)
    pl.run_scoped(
        finish_scope, pltpu.VMEM((T, plane, pw), BF16), pltpu.VMEM((D, HDIM), BF16), pltpu.VMEM((R, pw), F32)
    )

    for k in range(reach):
        for h in range(2):
            @pl.when((d >= k) & has[0])
            def _():
                kv_copy(h, k).wait_send()

            @pl.when((d + k < dp) & has[1])
            def _():
                qd_copy(h, k).wait_send()

        @pl.when(d >= k + 1)
        def _():
            stat_copy(k + 1).wait_send()
    for a in range(2):
        rows_x(a).wait_send()
        rows_c(a).wait_send()
    for g in range(GROUPS):
        gather_sent(g)
    for g in range(4):
        for k in range(1, dp):
            for way in range(2):
                @pl.when(from_dist(k, 1 - way))
                def _():
                    rs_copy(g, k, way).wait_send()
        for c in final_copies(g):
            c.wait()


def block(tok, gh, w2, vecs, bq, b_in, bias, carried, tabs, firstq, dims):
    R, D, feats, dp, reach = dims
    plane, pf, F, T = 2 * R, 2 * feats, 2 * dp, lax.axis_size("tp")
    gw = w2.shape[2] // GROUPS
    pw = D // T
    sds = jax.ShapeDtypeStruct
    vm = pltpu.VMEM
    dma = pltpu.SemaphoreType.DMA
    reg = pltpu.SemaphoreType.REGULAR
    win = vm((reach + 1, plane, HDIM), BF16)
    return pl.pallas_call(
        functools.partial(block_kernel, dims),
        out_shape=[sds((D, gw), BF16)] * GROUPS
        + [sds((R, pw), BF16), sds((R, pw), BF16), sds((8, feats), F32), sds((F, 8, gw), F32)]
        + [sds((3, feats, 2 * HDIM), BF16), sds((2 * HDIM, feats), BF16)]
        + [sds((feats, 2 * gw), BF16), sds((2 * gw, feats), BF16)],
        in_specs=[ANY] * 3 + [VMEM] * 4 + [ANY] + [VMEM] * 2,
        out_specs=[ANY] * GROUPS + [VMEM] * 4 + [ANY] * 4,
        scratch_shapes=[
            vm((plane, D), BF16), vm((plane, D), BF16), vm((D, gw), BF16),
            win, win, win, win, vm((8, (reach + 1) * plane), F32),
            vm((plane, gw), BF16), vm((plane, gw), BF16), vm((plane, 3 * HDIM), BF16), vm((plane, HDIM), BF16),
            vm((T // 2, plane, pw), BF16), vm((plane, pw), BF16), vm((R, pw), BF16),
            vm((2, dp + 1, pf, 2 * HDIM), BF16), vm((2, dp + 1, pf, gw), BF16),
            vm((plane, 2), F32),
            vm((2, HDIM, feats), BF16), vm((2, 2, gw // 2, feats), BF16),
            vm((8, D), F32), vm((8, gw), F32), vm((F, 8, feats), F32), vm((F, 8, feats), F32),
            vm((T, 8, R), F32), vm((T, 8, feats), F32),
            dma((GROUPS + 2,)), dma((4, 4)), dma((2, GROUPS)), dma((GROUPS, dp, 2, 2)), dma((GROUPS, F)),
            dma((2, 2, reach + 1)), dma((2, 2, reach + 1)), dma((2, reach + 1)), dma((4, dp, 2)), dma((4, dp + 1)), dma((4, 2, 3)),
            dma((4,)), dma((4, 2, F)), dma((2, 7)), reg, reg, reg,
        ],
        compiler_params=pltpu.CompilerParams(
            collective_id=4, has_side_effects=True, vmem_limit_bytes=63 << 20
        ),
        name="block",
    )(tok, gh, w2, vecs, bq, b_in, bias, carried, tabs, firstq)


def on_device(
    tokens,
    qkv_weight,
    qkv_bias,
    dense_weight,
    dense_bias,
    fc_in_weight,
    fc_in_bias,
    fc_out_weight,
    fc_out_bias,
    norm1_gain,
    norm1_shift,
    norm2_gain,
    norm2_shift,
    cotangent,
    subset_ids,
    seq_starts,
):
    rows, width = tokens.shape
    shards = lax.axis_size("fsdp")
    tps = lax.axis_size("tp")
    dp = shards // 2
    f = lax.axis_index("fsdp")
    t = lax.axis_index("tp")
    i = lax.rem(f, 2)
    d = f // 2
    total = rows * shards
    scale = 1.0 / math.sqrt(HDIM)
    feats = qkv_weight.shape[0]
    units = fc_in_weight.shape[1]
    head_cols = qkv_weight.shape[2]
    heads_here = head_cols // HDIM
    hd = qkv_bias.shape[2]
    ub = fc_in_bias.shape

    match = subset_ids[:, None] == jnp.arange(SUBSETS, dtype=jnp.int32)[None, :]
    counts = jnp.sum(match.astype(F32), axis=0)
    vecs = [norm1_gain, norm1_shift, norm2_gain, norm2_shift, dense_bias, fc_out_bias]
    pack = jnp.concatenate(
        [v.astype(F32) for v in vecs]
        + [qkv_bias.astype(F32).reshape(-1), fc_in_bias.astype(F32).reshape(-1), counts]
    )
    size = pack.shape[0]
    lanes = -(-size // 1024) * 128
    got = exchange(jnp.pad(pack, (0, 8 * lanes - size)).reshape(8, lanes), "fsdp", False, 1)
    got = got.reshape(shards, 8 * lanes)
    gain1, shift1, gain2, shift2, b_dense, b_out = [
        got[:, k * feats : (k + 1) * feats].reshape(width) for k in range(6)
    ]
    at = 6 * feats
    nq = 3 * heads_here * hd
    b_qkv = got[:, at : at + nq].reshape(shards, 3, heads_here, hd)
    b_qkv = b_qkv.transpose(1, 2, 0, 3).reshape(3, heads_here, HDIM)
    b_qkv = lax.dynamic_index_in_dim(b_qkv, i, 1, keepdims=False).reshape(3 * HDIM)
    at += nq
    b_in = got[:, at : at + units // shards].reshape(shards, ub[0], ub[1])
    b_in = half_of(b_in.transpose(1, 0, 2).reshape(units), i, 0)
    at += units // shards
    counts = jnp.sum(got[:, at : at + SUBSETS], axis=0)
    table = total / (SUBSETS * counts)
    row_scale = jnp.sum(jnp.where(match, table[None, :], 0.0), axis=1)
    carried = cotangent.astype(F32) * row_scale[:, None]
    grad_here = carried.astype(BF16)

    wi = fc_in_weight.reshape(feats, 2, 2, units // 4).transpose(1, 0, 2, 3)
    wo = fc_out_weight.reshape(2, 2, units // 4, feats).transpose(0, 3, 1, 2)
    w2 = jnp.concatenate(
        [
            qkv_weight.reshape(feats, 3, heads_here, HDIM).transpose(2, 0, 1, 3).reshape(2, feats, 3 * HDIM),
            dense_weight.reshape(heads_here, HDIM, feats).transpose(0, 2, 1),
            wi[:, :, 0], wo[:, :, 0], wi[:, :, 1], wo[:, :, 1],
        ],
        axis=2,
    )
    plane = 2 * rows
    start_row = d * plane
    reach = min(dp - 1, -(-(SEQ_LEN - 1) // plane))
    here = start_row + jnp.arange(plane, dtype=jnp.int32)
    docs_here, pos_here = locate(here, seq_starts)
    later = start_row + jnp.arange((reach + 1) * plane, dtype=jnp.int32)
    _, pos_later = locate(later, seq_starts)
    first_later = later - pos_later.astype(jnp.int32) - start_row
    first_later = jnp.where(later < total, first_later, 1 << 30)[None, :]
    cosine, sine = rotary_tables(pos_here)
    ones = jnp.ones((plane, 128 - ROT), F32)
    none = jnp.zeros((plane, 128 - ROT), F32)
    tabs = jnp.stack(
        [
            jnp.concatenate([cosine, cosine, ones], 1),
            jnp.concatenate([-sine, sine, none], 1),
        ]
    )
    vecs = jnp.stack([gain1, shift1, gain2, shift2] + [jnp.zeros_like(gain1)] * 4)
    dims = (rows, width, feats, dp, reach)
    part_w = width // tps
    offset = t * part_w
    cut = lambda vec: lax.dynamic_slice_in_dim(vec, offset, part_w, vec.ndim - 1)
    bias = (cut(b_dense) + cut(b_out)).reshape(1, -1)
    carried_here = cut(cotangent).astype(F32) * row_scale[:, None]
    _, _, _, mixed, tokens_grad, norm_grads, bias_sums, g_qkv, g_dense, g_in, g_out = block(
        tokens, grad_here, w2, vecs, b_qkv.reshape(1, -1), b_in.reshape(1, -1), bias, carried_here, tabs,
        first_later, dims,
    )
    qkv_weight_grad = g_qkv.transpose(1, 0, 2).astype(F32)
    dense_weight_grad = g_dense.astype(F32)
    fc_in_weight_grad = g_in.astype(F32)
    fc_out_weight_grad = g_out.astype(F32)
    bias_grad = norm_grads[4]

    bias_sums = jnp.sum(bias_sums.reshape(dp, 2, 8, units // 2), axis=0)
    in_bias_grad = bias_sums[:, 0].reshape(ub[0], shards * ub[1])
    in_bias_grad = lax.dynamic_slice_in_dim(in_bias_grad, f * ub[1], ub[1], 1)
    qkv_bias_grad = bias_sums[:, 1, : 3 * HDIM].reshape(2, 3, HDIM).transpose(1, 0, 2)
    qkv_bias_grad = lax.dynamic_slice_in_dim(qkv_bias_grad, f * hd, hd, 2)
    return (
        mixed,
        tokens_grad,
        qkv_weight_grad,
        qkv_bias_grad,
        dense_weight_grad,
        bias_grad,
        fc_in_weight_grad,
        in_bias_grad,
        fc_out_weight_grad,
        bias_grad,
        norm_grads[0],
        norm_grads[1],
        norm_grads[2],
        norm_grads[3],
    )


def solution(mesh):
    in_specs = (
        P("fsdp", None),
        P("fsdp", None, "tp"),
        P(None, "tp", "fsdp"),
        P("tp", "fsdp"),
        P("fsdp"),
        P("fsdp", "tp"),
        P("tp", "fsdp"),
        P("tp", "fsdp"),
        P("fsdp"),
        P("fsdp"),
        P("fsdp"),
        P("fsdp"),
        P("fsdp"),
        P("fsdp", None),
        P("fsdp"),
        P(),
    )
    out_specs = (
        P("fsdp", "tp"),
        P("fsdp", "tp"),
        P("fsdp", None, "tp"),
        P(None, "tp", "fsdp"),
        P("tp", "fsdp"),
        P("fsdp"),
        P("fsdp", "tp"),
        P("tp", "fsdp"),
        P("tp", "fsdp"),
        P("fsdp"),
        P("fsdp"),
        P("fsdp"),
        P("fsdp"),
        P("fsdp"),
    )
    return jax.shard_map(
        on_device, mesh=mesh, in_specs=in_specs, out_specs=out_specs, check_vma=False
    )
```

```python
import functools
import math

import jax
import jax.numpy as jnp
from jax import lax
from jax.experimental import pallas as pl
from jax.experimental.pallas import tpu as pltpu
from jax.sharding import PartitionSpec as P

HDIM = 256
ROT = 64
SUBSETS = 22
SEQ_LEN = 2048
EPS = 1e-05
F32 = jnp.float32
BF16 = jnp.bfloat16
MESH = pl.DeviceIdType.MESH
ANY = pl.BlockSpec(memory_space=pl.ANY)
VMEM = pl.BlockSpec(memory_space=pltpu.VMEM)


def mm(left, right, dims):
    return lax.dot_general(left, right, (dims, ((), ())), preferred_element_type=F32)


def plain(left, right):
    return mm(left, right, ((1,), (0,)))


def inner(left, right):
    return mm(left, right, ((0,), (0,)))


def against(left, right):
    return mm(left, right, ((1,), (1,)))


def rotary_tables(positions):
    half = ROT // 2
    steps = jnp.arange(half, dtype=F32)
    freq = 1.0 / 10000.0 ** (steps * 2.0 / ROT)
    angle = positions[:, None] * freq[None, :]
    return jnp.cos(angle), jnp.sin(angle)


def locate(indices, starts):
    above = indices[:, None] >= starts[None, :]
    doc_ids = jnp.sum(above.astype(jnp.int32), axis=1) - 1
    pick = doc_ids[:, None] == jnp.arange(starts.shape[0], dtype=jnp.int32)[None, :]
    first = jnp.sum(jnp.where(pick, starts[None, :], 0), axis=1)
    return (doc_ids, (indices - first).astype(F32))


def half_of(value, which, axis):
    size = value.shape[axis] // 2
    return lax.dynamic_slice_in_dim(value, which * size, size, axis)


def exchange_kernel(axis, spread, v_ref, o_ref, ssem, rsem):
    count = o_ref.shape[0]
    me = lax.axis_index(axis)

    def peer(step):
        return lax.rem(me + step, count)

    barrier = pltpu.get_barrier_semaphore()
    for step in range(1, count):
        pl.semaphore_signal(barrier, 1, device_id={axis: peer(step)}, device_id_type=MESH)
    pl.semaphore_wait(barrier, count - 1)

    def copy(step):
        return pltpu.make_async_remote_copy(
            src_ref=v_ref.at[peer(step)] if spread else v_ref,
            dst_ref=o_ref.at[me],
            send_sem=ssem.at[step],
            recv_sem=rsem.at[step],
            device_id={axis: peer(step)},
            device_id_type=MESH,
        )

    for step in range(1, count):
        copy(step).start()
    o_ref[me] = v_ref[me] if spread else v_ref[...]
    for step in range(1, count):
        copy(step).wait()


def exchange(value, axis, spread, cid):
    count = lax.axis_size(axis)
    block = value.shape[1:] if spread else value.shape
    return pl.pallas_call(
        functools.partial(exchange_kernel, axis, spread),
        out_shape=jax.ShapeDtypeStruct((count,) + block, value.dtype),
        in_specs=[VMEM],
        out_specs=VMEM,
        scratch_shapes=[pltpu.SemaphoreType.DMA((count,)), pltpu.SemaphoreType.DMA((count,))],
        compiler_params=pltpu.CompilerParams(collective_id=cid, has_side_effects=True),
        name="exchange",
    )(value)


NB = 4
GROUPS = 1 + NB
ORDER = (
    "pair0", "own0i", "own0o", "own1o", "mate0o", "pair1", "pair4", "rx0", "pair3", "mate0i", "mate1i",
    "mate1o", "own3i", "arr01", "own1i", "rc0", "pair2", "mate3i", "arr02", "own2i", "rx1", "arr11", "arr03",
    "mate2i", "rc1", "stats", "arr12", "own4i", "proj", "mate4i", "datt", "arr13", "ffn0", "kv1k", "kv1v",
    "qd1", "mate2o", "st13i", "st12o", "st12i", "own2o", "st11i", "mate3o", "kv2v", "own4o", "kv2k", "att0",
    "att1", "att2", "att3", "ls0", "sta3i", "arr21", "sta2i", "qd2", "ls1", "dkv0", "mate4o", "sta2o", "dkv1",
    "dkv2", "arr22", "dkv3", "sta1i", "arr41", "stb3i", "arr23", "own3o", "ffn1", "st23i", "arr31", "st22o",
    "st22i", "arr32", "stb2i", "arr33", "stb2o", "arr42", "st21i", "ffn2", "st33i", "st11o", "arr43", "ffn3",
    "out", "stb1i", "st43i", "st32o", "hid", "stb1o", "far00", "far01", "qk", "sta1o", "st21o", "st32i",
    "far10", "finb", "st42o", "mt0", "far11", "fina", "fin1", "st42i", "st31i", "st31o", "last0", "small",
    "mt1", "st41i", "fin2", "st41o", "fin3", "last1", "fin4",
)


def turn(u, tabs, at, sign):
    lo, hi = u[:, :128], u[:, 128:]
    lane = lax.broadcasted_iota(jnp.int32, lo.shape, 1)
    other = jnp.where(lane < ROT // 2, pltpu.roll(lo, 128 - ROT // 2, 1), pltpu.roll(lo, ROT // 2, 1))
    a = other * tabs[1, at, :]
    lo = lo * tabs[0, at, :] + (a if sign > 0 else -a)
    return jnp.concatenate([lo, hi], axis=1)


def block_kernel(
    dims,
    tok, gh, w2, vecs, bq, bin_, bias, cot, row_scale, tabs, firstq,
    *refs,
):
    outs, refs = refs[:GROUPS], refs[GROUPS:]
    (
        mixed_o, dtok_o, norm_o, bias_o, dq_o, dd_o, di_o, do_o, xs, gs, wbuf, wins, st,
        act, dpre, dqkv, att, tpr0, tpr1, tpr2, rs_a, rs_f, norms, tra, trf, sums, bsum, sum_s, sum_r, row_r, nrm_r,
        lsem, tsem, psem, zsem, zrec, ksem, qsem, lssem, ssem, rsem, fsem, bsem, xsem, usem, near_ok, far_ok, mate_ok,
    ) = refs
    R, D, feats, dp, reach = dims
    F, T = 2 * dp, row_r.shape[0]
    f = lax.axis_index("fsdp")
    t = lax.axis_index("tp")
    d, i = f // 2, lax.rem(f, 2)
    core = lax.rem(t, 2)
    plane, pf = 2 * R, 2 * feats
    qb = min(256, plane)
    nb = plane // qb
    fb = min(256, pf)
    aw = 4 * HDIM
    gw = act.shape[1]
    hu = gw // NB
    pw = D // T
    slots = reach + 1
    tn, tf = t + 1 - 2 * core, lax.rem(t + 2, T)
    mate, near, far = (f + 1 - 2 * i, t), (f, tn), (f, tf)
    has = (d + 1 < dp, d >= 1)
    inward = jnp.where(d < dp // 2, 0, 1)
    ways = {"i": inward, "o": 1 - inward}
    scale = 1.0 / math.sqrt(HDIM)

    barrier = pltpu.get_barrier_semaphore()
    for s in range(1, F):
        pl.semaphore_signal(barrier, 1, device_id=(lax.rem(f + s, F), t), device_id_type=MESH)
    for s in range(1, T):
        pl.semaphore_signal(barrier, 1, device_id=(f, lax.rem(t + s, T)), device_id_type=MESH)
    pl.semaphore_wait(barrier, F + T - 2)

    def rc(src, dst, ss, rv, who):
        return pltpu.make_async_remote_copy(
            src_ref=src, dst_ref=dst, send_sem=ss, recv_sem=rv, device_id=who, device_id_type=MESH
        )

    def rows(b):
        return pl.ds(pl.multiple_of(b * qb, qb), qb)

    def toward(way):
        return (f + 2 - 4 * way, t)

    def open_way(way):
        return jnp.where(way == 0, d + 1 < dp, d >= 1)

    def slot(g, s):
        return outs[g].at[pl.ds(s * feats, feats), :]

    def part(half, g):
        cols = pl.ds(0, aw) if g == 0 else pl.ds(aw + (g - 1) * 2 * hu, 2 * hu)
        return w2.at[half, :, cols]

    def pair_copy(g):
        return rc(part(1 - i, g), slot(g, f), psem.at[0, g], psem.at[1, g], mate)

    def mine_copy(g):
        return pltpu.make_async_copy(part(i, g), slot(g, f), lsem.at[g])

    def z_own(g, way):
        return rc(part(i, g), slot(g, f), zsem.at[g, 0, way, 0], zrec.at[g, f], toward(way))

    def z_mate(g, way):
        s = f + 1 - 2 * i
        return rc(slot(g, s), slot(g, s), zsem.at[g, 0, way, 1], zrec.at[g, s], toward(way))

    def z_fwd(g, k, way, j):
        s = (d - k) * 2 + j if way == 0 else (d + k) * 2 + j
        return rc(slot(g, s), slot(g, s), zsem.at[g, k, way, j], zrec.at[g, s], toward(way))

    def send_own(g, io):
        @pl.when(open_way(ways[io]))
        def _():
            z_own(g, ways[io]).start()

    def send_mate(g, io, wait):
        if wait:
            pair_copy(g).wait_recv()

        @pl.when(open_way(ways[io]))
        def _():
            z_mate(g, ways[io]).start()

    def from_dist(k, way):
        return d >= k if way == 0 else d + k < dp

    def arrive(g, k):
        for way in range(2):
            @pl.when(from_dist(k, way))
            def _():
                for j in range(2):
                    z_fwd(g, k, way, j).wait_recv()

                    @pl.when(has[way])
                    def _():
                        z_fwd(g, k, way, j).start()

    def gather_sent(g):
        pair_copy(g).wait_send()
        for way in range(2):
            @pl.when(has[way])
            def _():
                z_own(g, way).wait_send()
                z_mate(g, way).wait_send()
            for k in range(1, dp - 1):
                @pl.when(from_dist(k, way) & has[way])
                def _():
                    for j in range(2):
                        z_fwd(g, k, way, j).wait_send()

    def load(*pairs):
        copies = [pltpu.make_async_copy(src, dst, bsem.at[n]) for n, (src, dst) in enumerate(pairs)]
        for c in copies:
            c.start()
        for c in copies:
            c.wait()

    hr = R // 2
    given = ((tok, xs), (gh, gs))

    def rows_x(a):
        ref, out = given[a]
        return rc(
            ref.at[pl.ds(core * hr, hr), :], out.at[pl.ds(i * R + core * hr, hr), :],
            tsem.at[a, 0], tsem.at[a, 1], mate,
        )

    def rows_c(a):
        at = given[a][1].at[pl.ds((1 - i) * R + core * hr, hr), :]
        return rc(at, at, tsem.at[a, 2], tsem.at[a, 3], near)

    def rows_own(a):
        ref, out = given[a]
        return pltpu.make_async_copy(ref, out.at[pl.ds(i * R, R), :], lsem.at[GROUPS + a])

    def rows_on(a):
        rows_x(a).wait_recv()
        rows_c(a).start()

    def rows_done(a):
        rows_c(a).wait_recv()
        rows_own(a).wait()

    def hat(at):
        return (xs[at, :].astype(F32) - norms[at, 0:1]) * norms[at, 1:2]

    def stats():
        def block(b, _):
            x = xs[rows(b), :].astype(F32)
            m = jnp.mean(x, axis=-1, keepdims=True)
            c = x - m
            norms[rows(b), 0:1] = m
            norms[rows(b), 1:2] = lax.rsqrt(jnp.mean(c * c, axis=-1, keepdims=True) + EPS)
            return 0

        rows_done(0)
        lax.fori_loop(0, nb, block, 0)

    def proj():
        def block(b, _):
            at = rows(b)
            h1 = (hat(at) * vecs[0:1, :] + vecs[1:2, :]).astype(BF16)
            y = plain(h1, wbuf[:, : 3 * HDIM]) + bq[...]
            wins[2 * slots, at, :] = (turn(y[:, :HDIM], tabs, at, 1).astype(BF16).astype(F32) * scale).astype(BF16)
            wins[reach, at, :] = turn(y[:, HDIM : 2 * HDIM], tabs, at, 1).astype(BF16)
            wins[slots + reach, at, :] = y[:, 2 * HDIM :].astype(BF16)
            return 0

        mine_copy(0).wait()
        load((outs[0], wbuf))
        lax.fori_loop(0, nb, block, 0)

        @pl.when(has[0])
        def _():
            kv_copy(0, 0).start()
            kv_copy(1, 0).start()

    def datt():
        def block(b, _):
            at = rows(b)
            wins[3 * slots, at, :] = plain(gs[at, :], wbuf[:, 3 * HDIM :]).astype(BF16)
            return 0

        rows_done(1)
        lax.fori_loop(0, nb, block, 0)

        @pl.when(has[1])
        def _():
            qd_copy(0, 0).start()
            qd_copy(1, 0).start()

    def ffn(h):
        mine = slice(h * hu, (h + 1) * hu)

        def block(b, _):
            at = rows(b)
            h2 = (hat(at) * vecs[2:3, :] + vecs[3:4, :]).astype(BF16)
            pre = plain(h2, wbuf[:, :hu]) + bin_[:, mine]
            cdf = 0.5 * (1.0 + lax.erf(pre * (1.0 / math.sqrt(2.0))))
            act[at, mine] = (pre * cdf).astype(BF16)
            slope = cdf + pre * jnp.exp(-0.5 * pre * pre) * (1.0 / math.sqrt(2.0 * math.pi))
            dp_b = (plain(gs[at, :], wbuf[:, hu : 2 * hu]) * slope).astype(BF16)
            dpre[at, mine] = dp_b
            bsum[0:1, mine] += jnp.sum(dp_b.astype(F32), axis=0, keepdims=True)
            return 0

        mine_copy(1 + h).wait()
        load((outs[1 + h], wbuf.at[:, pl.ds(0, 2 * hu)]))
        lax.fori_loop(0, nb, block, 0)

    def kv_copy(h, k):
        w = wins.at[h * slots + reach - k]
        return rc(w, wins.at[h * slots + reach - k - 1], ksem.at[h, 0, k], ksem.at[h, 1, k + 1], toward(0))

    def kv_recv(h, k):
        w = wins.at[h * slots + reach - k]
        return rc(w, w, ksem.at[h, 0, k - 1], ksem.at[h, 1, k], toward(0))

    def kv_step(h, k):
        @pl.when(d >= k)
        def _():
            kv_recv(h, k).wait_recv()
            if k < reach:
                @pl.when(has[0])
                def _():
                    kv_copy(h, k).start()

        @pl.when(d < k)
        def _():
            wins[h * slots + reach - k] = jnp.zeros((plane, HDIM), BF16)

    def qd_copy(h, k):
        w = wins.at[(2 + h) * slots + k]
        return rc(w, wins.at[(2 + h) * slots + k + 1], qsem.at[h, 0, k], qsem.at[h, 1, k + 1], toward(1))

    def qd_recv(h, k):
        w = wins.at[(2 + h) * slots + k]
        return rc(w, w, qsem.at[h, 0, k - 1], qsem.at[h, 1, k], toward(1))

    def qd_step(k):
        @pl.when(d + k < dp)
        def _():
            for h in range(2):
                qd_recv(h, k).wait_recv()
                if k < reach:
                    @pl.when(has[1])
                    def _():
                        qd_copy(h, k).start()

        @pl.when(d + k >= dp)
        def _():
            for h in range(2):
                wins[(2 + h) * slots + k] = jnp.zeros((plane, HDIM), BF16)

    def stat_at(k):
        return st.at[:, pl.ds(k * plane, plane)]

    def stat_copy(k):
        return rc(stat_at(0), stat_at(k), lssem.at[0, k], lssem.at[1, k], (f - 2 * k, t))

    def stat_send():
        for k in range(1, reach + 1):
            @pl.when(d >= k)
            def _():
                stat_copy(k).start()

    def stat_wait():
        for k in range(1, reach + 1):
            @pl.when(d + k < dp)
            def _():
                stat_copy(k).wait_recv()

            @pl.when(d + k >= dp)
            def _():
                st[:, k * plane : (k + 1) * plane] = jnp.zeros((8, plane), F32)

    span = SEQ_LEN + qb
    base = reach * plane - SEQ_LEN
    parts = 4

    def wide(n, start):
        flat = wins.reshape(wins.shape[0] * plane, HDIM)
        return flat[pl.ds(pl.multiple_of(n * slots * plane + start, qb), span), :]

    def attention(n):
        def block(b, _):
            at = rows(b)
            keys_at = base + b * qb
            keys = wide(0, keys_at)
            vals = wide(1, keys_at)
            s = against(wins[2 * slots, at, :], keys)
            c = base + b * qb + lax.broadcasted_iota(jnp.int32, (qb, span), 1)
            r = reach * plane + b * qb + lax.broadcasted_iota(jnp.int32, (qb, span), 0)
            low = jnp.broadcast_to(firstq[:, at].astype(F32), (128, qb)).T[:, 0:1] + float(reach * plane)
            s = jnp.where((c.astype(F32) >= low) & (c <= r), s, -1e30)
            top = jnp.max(s, axis=1, keepdims=True)
            e = jnp.exp(s - top)
            total = jnp.sum(e, axis=1, keepdims=True)
            p = e * (1.0 / total)
            att[at, :] = plain(p.astype(BF16), vals).astype(BF16)
            dpr = against(wins[3 * slots, at, :], vals)
            delta = jnp.sum(p * dpr, axis=1, keepdims=True)
            ds = (p * (dpr - delta)).astype(BF16)
            dq = plain(ds, keys) * scale
            dqkv[at, :HDIM] = turn(dq, tabs, at, -1).astype(BF16)
            lane = lax.broadcasted_iota(jnp.int32, (qb, 128), 1)
            both = jnp.where(lane == 0, top + jnp.log(total), jnp.where(lane == 1, delta, 0.0))
            st[:, at] = both.T[:8]
            return 0

        lax.fori_loop(n * nb // parts, (n + 1) * nb // parts, block, 0)

    def key_grads(n):
        def block(b, _):
            at = rows(b)
            rows_at = pl.ds(pl.multiple_of(b * qb, qb), span)
            q = wide(2, b * qb)
            da = wide(3, b * qb)
            s = against(wins[reach, at, :], q)
            c = b * qb + lax.broadcasted_iota(jnp.int32, (qb, span), 0)
            r = b * qb + lax.broadcasted_iota(jnp.int32, (qb, span), 1)
            s = jnp.where((c >= firstq[:, rows_at]) & (c <= r), s - st[0:1, rows_at], -1e30)
            p = jnp.exp(s)
            dqkv[at, 2 * HDIM :] = plain(p.astype(BF16), da).astype(BF16)
            dpr = against(wins[slots + reach, at, :], da)
            ds = (p * (dpr - st[1:2, rows_at])).astype(BF16)
            dqkv[at, HDIM : 2 * HDIM] = turn(plain(ds, q), tabs, at, -1).astype(BF16)
            return 0

        lax.fori_loop(n * nb // parts, (n + 1) * nb // parts, block, 0)

    def rs(g):
        return rs_a.at[g] if g < 2 else rs_f.at[g - 2]

    def grad_part(g, p, c):
        cols = pl.ds(pl.multiple_of(p * pf + c * fb, fb), fb)
        z = (xs[:, cols].astype(F32) - norms[:, 0:1]) * norms[:, 1:2]
        n = 0 if g < 2 else 2
        h = (z * vecs[n : n + 1, cols] + vecs[n + 1 : n + 2, cols]).astype(BF16)
        if g == 0:
            return inner(h, dqkv[:, :HDIM]), inner(gs[:, cols], att[...])
        if g == 1:
            return (inner(h, dqkv[:, HDIM:]),)
        mine = slice((g - 2) * hu, (g - 1) * hu)
        return inner(h, dpre[:, mine]), inner(gs[:, cols], act[:, mine])

    def add_part(g, p, second=None):
        def block(c, _):
            at = pl.ds(pl.multiple_of(c * fb, fb), fb)
            left = 0
            for v in grad_part(g, p, c):
                cols = slice(left, left + v.shape[1])
                left += v.shape[1]
                v = rs(g)[p, at, cols].astype(F32) + v
                if second is not None:
                    v = v + rs(g)[second, at, cols].astype(F32)
                rs(g)[p, at, cols] = v.astype(BF16)
            return 0

        lax.fori_loop(0, pf // fb, block, 0)

    def rs_copy(g, k, way):
        p = d + k * (1 - 2 * way)
        to = jnp.where((way == 1) & (k == 1), dp, p)
        return rc(rs(g).at[p], rs(g).at[to], ssem.at[g, k, way], rsem.at[g, to], toward(way))

    def rs_wait(g, p):
        return rc(rs(g).at[p], rs(g).at[p], ssem.at[g, 0, 0], rsem.at[g, p], mate)

    def clear(g, p):
        rs(g)[p] = jnp.zeros(rs(g).shape[1:], BF16)

    def stage(g, k, io):
        way = ways[io]
        p = d + k * (1 - 2 * way)
        came = open_way(1 - way)

        @pl.when((p >= 0) & (p < dp))
        def _():
            @pl.when(came)
            def _():
                rs_wait(g, p).wait_recv()

            @pl.when(jnp.logical_not(came))
            def _():
                clear(g, p)

            add_part(g, p)
            rs_copy(g, k, way).start()

    def final_copies(g):
        lo = pl.multiple_of(i * HDIM, HDIM)
        pieces = []
        for j in range(2):
            at = pl.ds((i if j == 0 else 1 - i) * feats, feats)
            src = rs(g).at[d, at]
            if g == 0:
                dst = (dq_o.at[0, :, pl.ds(lo, HDIM)], dd_o.at[pl.ds(lo, HDIM), :])
                src = (src.at[:, pl.ds(0, HDIM)], tra.at[j])
            elif g == 1:
                dst = tuple(dq_o.at[n, :, pl.ds(lo, HDIM)] for n in (1, 2))
                src = tuple(src.at[:, pl.ds(n * HDIM, HDIM)] for n in (0, 1))
            else:
                u = pl.multiple_of(i * gw + (g - 2) * hu, hu)
                dst = (di_o.at[:, pl.ds(u, hu)], do_o.at[pl.ds(u, hu), :])
                src = (src.at[:, pl.ds(0, hu)], trf.at[g - 2, j])
            for n in range(2):
                if j == 0:
                    pieces.append(pltpu.make_async_copy(src[n], dst[n], fsem.at[g, n, 0]))
                else:
                    pieces.append(rc(src[n], dst[n], fsem.at[g, n, 1], fsem.at[g, n, 2], mate))
        return pieces

    def final(g):
        for p, came in ((d, has[1]), (dp, has[0])):
            @pl.when(came)
            def _():
                rs_wait(g, p).wait_recv()

            @pl.when(jnp.logical_not(came))
            def _():
                clear(g, p)

        add_part(g, d, dp)
        if g != 1:
            cut = HDIM if g == 0 else hu
            for j in range(2):
                at = pl.ds(pl.multiple_of((i if j == 0 else 1 - i) * feats, feats), feats)
                turned = rs(g)[d, at, cut:].astype(F32).T.astype(BF16)
                if g == 0:
                    tra[j] = turned
                else:
                    trf[g - 2, j] = turned
        for c in final_copies(g):
            c.start()

    def out_step(up):
        def dense(b, _):
            at = rows(b)
            for c in range(T):
                y = against(att[at, :], wbuf[c * pw : (c + 1) * pw, :HDIM])
                for e in range(2):
                    v = up[2 * c + e, at, :].astype(F32) + y[:, e * HDIM : (e + 1) * HDIM]
                    up[2 * c + e, at, :] = v.astype(BF16)
            return 0

        def block(b, _):
            at = rows(b)
            sums[4:5, :] += jnp.sum(gs[at, :].astype(F32), axis=0, keepdims=True)
            for c in range(T):
                cols = slice(c * pw, (c + 1) * pw)
                y = against(act[at, :], wbuf[cols, :])
                for e in range(2):
                    up[2 * c + e, at, :] = y[:, e * HDIM : (e + 1) * HDIM].astype(BF16)
            return 0

        load(
            *[(outs[1 + h].at[:, pl.ds(hu, hu)], wbuf.at[:, pl.ds(h * hu, hu)]) for h in range(NB)],
        )
        lax.fori_loop(0, nb, block, 0)
        load((outs[0].at[:, pl.ds(3 * HDIM, HDIM)], wbuf.at[:, pl.ds(0, HDIM)]))
        lax.fori_loop(0, nb, dense, 0)
        tp_near(up, False)

    def hidden_step():
        def block(b, _):
            at = rows(b)
            e2 = against(dpre[at, :], wbuf[...])
            z = hat(at)
            sums[2:3, :] += jnp.sum(e2 * z, axis=0, keepdims=True)
            sums[3:4, :] += jnp.sum(e2, axis=0, keepdims=True)
            u = (e2 * vecs[2:3, :]).astype(BF16)
            for c in range(2 * T):
                wins[c, at, :] = u[:, c * HDIM : (c + 1) * HDIM]
            return 0

        for k in range(reach):
            for h in range(2):
                @pl.when((d >= k) & has[0])
                def _():
                    kv_copy(h, k).wait_send()

                @pl.when((d + k < dp) & has[1])
                def _():
                    qd_copy(h, k).wait_send()

        pl.semaphore_signal(far_ok, 1, device_id=far, device_id_type=MESH)
        pl.semaphore_signal(mate_ok, 1, device_id=mate, device_id_type=MESH)
        load(
            *[(outs[1 + h].at[:, pl.ds(0, hu)], wbuf.at[:, pl.ds(h * hu, hu)]) for h in range(NB)],
        )
        lax.fori_loop(0, nb, block, 0)

    def qkv_step():
        def block(b, _):
            at = rows(b)
            e1 = against(dqkv[at, :], wbuf[:, : 3 * HDIM])
            z = hat(at)
            sums[0:1, :] += jnp.sum(e1 * z, axis=0, keepdims=True)
            sums[1:2, :] += jnp.sum(e1, axis=0, keepdims=True)
            bsum[1:2, : 3 * HDIM] += jnp.sum(dqkv[at, :].astype(F32), axis=0, keepdims=True)
            u = e1 * vecs[0:1, :]
            for c in range(2 * T):
                wins[c, at, :] = (wins[c, at, :].astype(F32) + u[:, c * HDIM : (c + 1) * HDIM]).astype(BF16)
            return 0

        load((outs[0], wbuf))
        lax.fori_loop(0, nb, block, 0)
        tp_near(wins, True)
        for s in range(F):
            sum_s[s] = sums[:, s * feats : (s + 1) * feats]
        for s in range(1, F):
            sum_copy(s).start()
            bias_copy(s).start()
        sum_r[f] = sum_s[f]
        bias_o[f] = bsum[...]

    def half(h):
        return pl.ds(pl.multiple_of((1 - i if h == 0 else i) * R, R), R)

    def half_block(h, b):
        return pl.ds(pl.multiple_of((1 - i if h == 0 else i) * R + b * qb, qb), qb)

    def near_copy(up, second, h, j):
        blk = tn if j == 0 else lax.rem(tn + 2, T)
        n = 2 * h + j
        src = up.at[pl.ds(2 * blk, 2), half(h), :]
        return rc(src, tpr0.at[j, :, half(h), :], usem.at[int(second), 0, n], usem.at[int(second), 1, n], near)

    def landing(second):
        return (wins.at[pl.ds(2 * T, 2)], wins.at[pl.ds(2 * T + 2, 2), pl.ds(0, R), :]) if second else (tpr1, tpr2)

    def far_copy(up, h, second):
        src, dst = up.at[pl.ds(2 * tf, 2), half(h), :], landing(second)[0].at[:, half(h), :]
        return rc(src, dst, usem.at[int(second), 0, 4 + h], usem.at[int(second), 1, 4 + h], far)

    def mate_copy(up, second):
        n = int(second)
        src = up.at[pl.ds(2 * t, 2), half(0), :]
        return rc(src, landing(second)[1], usem.at[n, 0, 6], usem.at[n, 1, 6], mate)

    def tp_near(up, second):
        if second:
            pl.semaphore_wait(near_ok, 1)
        for h in range(2):
            for j in (1, 0):
                near_copy(up, second, h, j).start()

    def tp_far(up, second, h):
        def block(b, _):
            at = half_block(h, b)
            for blk, j in ((tf, 1), (t, 0)):
                for e in range(2):
                    v = up[2 * blk + e, at, :].astype(F32) + tpr0[j, e, at, :].astype(F32)
                    up[2 * blk + e, at, :] = v.astype(BF16)
            return 0

        near_copy(up, second, h, 1).wait_recv()
        near_copy(up, second, h, 0).wait_recv()
        lax.fori_loop(0, R // qb, block, 0)
        far_steps.append((second, h))
        if second and (True, 1 - h) not in far_steps:
            pl.semaphore_wait(far_ok, 1)
        if not second and (False, 1 - h) in far_steps:
            pl.semaphore_signal(near_ok, 1, device_id=near, device_id_type=MESH)
        far_copy(up, h, second).start()

    def came_far(second, e, at):
        return (wins[2 * T + e, at, :] if second else tpr1[e, at, :]).astype(F32)

    def tp_mate(up, second):
        def block(b, _):
            at = half_block(0, b)
            for e in range(2):
                v = up[2 * t + e, at, :].astype(F32) + came_far(second, e, at)
                up[2 * t + e, at, :] = v.astype(BF16)
            return 0

        far_copy(up, 0, second).wait_recv()
        lax.fori_loop(0, R // qb, block, 0)
        if second:
            pl.semaphore_wait(mate_ok, 1)
        mate_copy(up, second).start()

    def tp_last(up, second):
        far_copy(up, 1, second).wait_recv()
        mate_copy(up, second).wait_recv()
        here = half(1)
        v = []
        for e in range(2):
            last = wins[2 * T + 2 + e, :R, :] if second else tpr2[e]
            v.append(up[2 * t + e, here, :].astype(F32) + came_far(second, e, here) + last.astype(F32))
        v = jnp.concatenate(v, axis=1)
        x = xs[here, pl.ds(pl.multiple_of(t * pw, pw), pw)].astype(F32)
        if second:
            u = v
            z = (x - norms[here, 0:1]) * norms[here, 1:2]
            lane = lax.broadcasted_iota(jnp.int32, (R, 128), 1)
            one, two = jnp.sum(u, axis=1, keepdims=True), jnp.sum(u * z, axis=1, keepdims=True)
            row_r[t] = jnp.where(lane == 0, one, jnp.where(lane == 1, two, 0.0)).T[:8]
            for s in range(1, T):
                row_copy(s).start()
            for s in range(1, T):
                row_copy(s).wait()
            both = row_r[0]
            for s in range(1, T):
                both = both + row_r[s]
            both = jnp.concatenate([both, jnp.zeros((120, R), F32)], axis=0).T * (1.0 / D)
            dx = norms[here, 1:2] * (u - both[:, 0:1] - z * both[:, 1:2])
            kept = env["up"]
            load((cot, kept.at[pl.ds(0, 2), pl.ds(0, R), :]))
            c = jnp.concatenate([kept[0, :R, :], kept[1, :R, :]], axis=1).astype(F32)
            c = c * jnp.broadcast_to(row_scale[...], (128, R)).T[:, 0:1]
            dtok_o[...] = (c + dx).astype(BF16)
        else:
            mixed_o[...] = (x + v + bias[...]).astype(BF16)
        for h in range(2):
            near_copy(up, second, h, 0).wait_send()
            near_copy(up, second, h, 1).wait_send()
            far_copy(up, h, second).wait_send()
        mate_copy(up, second).wait_send()

    def row_copy(s):
        return rc(row_r.at[t], row_r.at[t], xsem.at[0, 0, s], xsem.at[0, 1, s], (f, lax.rem(t + s, T)))

    def norm_copy(s):
        return rc(nrm_r.at[t], nrm_r.at[t], xsem.at[1, 0, s], xsem.at[1, 1, s], (f, lax.rem(t + s, T)))

    def sum_copy(s):
        to = lax.rem(f + s, F)
        return rc(sum_s.at[to], sum_r.at[f], xsem.at[2, 0, s], xsem.at[2, 1, s], (to, t))

    def bias_copy(s):
        return rc(bsum, bias_o.at[f], xsem.at[3, 0, s], xsem.at[3, 1, s], (lax.rem(f + s, F), t))

    def small_sums():
        for s in range(1, F):
            sum_copy(s).wait()
            bias_copy(s).wait()
        v = sum_r[0]
        for s in range(1, F):
            v = v + sum_r[s]
        nrm_r[t] = v
        for s in range(1, T):
            norm_copy(s).start()
        for s in range(1, T):
            norm_copy(s).wait()
        both = nrm_r[0]
        for s in range(1, T):
            both = both + nrm_r[s]
        row = lax.broadcasted_iota(jnp.int32, both.shape, 0)
        norm_o[...] = jnp.where(row == 4, v * 0.5, both)

    env = {}
    far_out = tuple(range(dp - 1, 2, -1))
    groups = {"a": 0, "b": 1} | {str(n + 1): 2 + n for n in range(NB)}
    paired, far_steps = set(), []

    def step(name):
        kind, rest = name.rstrip("0123456789abiokv"), ""
        rest = name[len(kind):]
        if kind == "pair":
            pair_copy(int(rest)).start()
            mine_copy(int(rest)).start()
        elif kind == "own":
            send_own(int(rest[0]), rest[1])
        elif kind == "mate":
            send_mate(int(rest[0]), rest[1], rest[0] not in paired)
            paired.add(rest[0])
        elif kind == "arr":
            g, k = int(rest[0]), int(rest[1])
            for n in range(k, dp if k == 3 else k + 1):
                arrive(g, n)
        elif kind == "rx":
            rows_x(int(rest)).start()
            rows_own(int(rest)).start()
        elif kind == "rc":
            rows_on(int(rest))
        elif kind == "stats":
            stats()
        elif kind == "proj":
            proj()
        elif kind == "datt":
            datt()
        elif kind == "ffn":
            ffn(int(rest))
        elif kind == "att":
            attention(int(rest))
        elif kind == "qd":
            for k in range(1, reach) if rest == "1" else (reach,):
                qd_step(k)
        elif kind == "ls":
            stat_send() if rest == "0" else stat_wait()
        elif kind == "d":
            key_grads(int(rest[-1]))
        elif kind == "st":
            g, k, io = groups[rest[0]], int(rest[1]), rest[2]
            if k == 3:
                for n in far_out:
                    stage(g, n, io)
            elif k == 2 and io == "o":
                for n in far_out + (2,):
                    stage(g, n, io)
            else:
                stage(g, k, io)
        elif kind == "fin":
            final(groups[rest])
        elif kind == "out":
            out_step(env["up"])
        elif kind == "far":
            tp_far(env["up"] if rest[0] == "0" else wins, rest[0] == "1", int(rest[1]))
        elif kind == "mt":
            tp_mate(env["up"] if rest == "0" else wins, rest == "1")
        elif kind == "last":
            tp_last(env["up"] if rest == "0" else wins, rest == "1")
        elif kind == "hid":
            hidden_step()
        elif kind == "q":
            qkv_step()
        elif kind == "small":
            small_sums()
        else:
            hop = int(rest[-2])
            for k in range(1, reach) if hop == 1 else (reach,):
                kv_step("kv".index(rest[-1]), k)

    def finish_scope(up):
        env["up"] = up
        for name in ORDER[ORDER.index("out") :]:
            step(name)

    sums[...] = jnp.zeros_like(sums)
    bsum[...] = jnp.zeros_like(bsum)
    for name in ORDER[: ORDER.index("out")]:
        step(name)
    pl.run_scoped(finish_scope, pltpu.VMEM((2 * T, plane, HDIM), BF16))

    for k in range(reach):
        @pl.when(d >= k + 1)
        def _():
            stat_copy(k + 1).wait_send()
    for a in range(2):
        rows_x(a).wait_send()
        rows_c(a).wait_send()
    for g in range(GROUPS):
        gather_sent(g)
    for g in range(2 + NB):
        for k in range(1, dp):
            for way in range(2):
                @pl.when(from_dist(k, 1 - way))
                def _():
                    rs_copy(g, k, way).wait_send()
        for c in final_copies(g):
            c.wait()


def block(tok, gh, w2, vecs, bq, b_in, bias, cot, row_scale, tabs, firstq, dims):
    R, D, feats, dp, reach = dims
    plane, pf, F, T = 2 * R, 2 * feats, 2 * dp, lax.axis_size("tp")
    aw = 4 * HDIM
    gw = (w2.shape[2] - aw) // 2
    hu = gw // NB
    pw = D // T
    sds = jax.ShapeDtypeStruct
    vm = pltpu.VMEM
    dma = pltpu.SemaphoreType.DMA
    reg = pltpu.SemaphoreType.REGULAR
    return pl.pallas_call(
        functools.partial(block_kernel, dims),
        out_shape=[sds((D, aw), BF16)] + [sds((D, 2 * hu), BF16)] * NB
        + [sds((R, pw), BF16), sds((R, pw), BF16), sds((8, feats), F32), sds((F, 8, gw), F32)]
        + [sds((3, feats, 2 * HDIM), BF16), sds((2 * HDIM, feats), BF16)]
        + [sds((feats, 2 * gw), BF16), sds((2 * gw, feats), BF16)],
        in_specs=[ANY] * 3 + [VMEM] * 4 + [ANY] + [VMEM] * 3,
        out_specs=[ANY] * GROUPS + [VMEM] * 4 + [ANY] * 4,
        scratch_shapes=[
            vm((plane, D), BF16), vm((plane, D), BF16), vm((D, max(aw, gw)), BF16),
            vm((4 * (reach + 1), plane, HDIM), BF16), vm((8, (reach + 1) * plane), F32),
            vm((plane, gw), BF16), vm((plane, gw), BF16), vm((plane, 3 * HDIM), BF16), vm((plane, HDIM), BF16),
            vm((2, 2, plane, HDIM), BF16), vm((2, plane, HDIM), BF16), vm((2, R, HDIM), BF16),
            vm((2, dp + 1, pf, 2 * HDIM), BF16), vm((NB, dp + 1, pf, 2 * hu), BF16),
            vm((plane, 2), F32),
            vm((2, HDIM, feats), BF16), vm((NB, 2, hu, feats), BF16),
            vm((8, D), F32), vm((8, gw), F32), vm((F, 8, feats), F32), vm((F, 8, feats), F32),
            vm((T, 8, R), F32), vm((T, 8, feats), F32),
            dma((GROUPS + 2,)), dma((4, 4)), dma((2, GROUPS)), dma((GROUPS, dp, 2, 2)), dma((GROUPS, F)),
            dma((2, 2, reach + 1)), dma((2, 2, reach + 1)), dma((2, reach + 1)), dma((2 + NB, dp, 2)), dma((2 + NB, dp + 1)), dma((2 + NB, 2, 3)),
            dma((NB + 2,)), dma((4, 2, F)), dma((2, 2, 7)), reg, reg, reg,
        ],
        compiler_params=pltpu.CompilerParams(
            collective_id=4, has_side_effects=True, vmem_limit_bytes=63 << 20
        ),
        name="block",
    )(tok, gh, w2, vecs, bq, b_in, bias, cot, row_scale, tabs, firstq)


def on_device(
    tokens,
    qkv_weight,
    qkv_bias,
    dense_weight,
    dense_bias,
    fc_in_weight,
    fc_in_bias,
    fc_out_weight,
    fc_out_bias,
    norm1_gain,
    norm1_shift,
    norm2_gain,
    norm2_shift,
    cotangent,
    subset_ids,
    seq_starts,
):
    rows, width = tokens.shape
    shards = lax.axis_size("fsdp")
    tps = lax.axis_size("tp")
    dp = shards // 2
    f = lax.axis_index("fsdp")
    t = lax.axis_index("tp")
    i = lax.rem(f, 2)
    d = f // 2
    total = rows * shards
    scale = 1.0 / math.sqrt(HDIM)
    feats = qkv_weight.shape[0]
    units = fc_in_weight.shape[1]
    head_cols = qkv_weight.shape[2]
    heads_here = head_cols // HDIM
    hd = qkv_bias.shape[2]
    ub = fc_in_bias.shape

    match = subset_ids[:, None] == jnp.arange(SUBSETS, dtype=jnp.int32)[None, :]
    counts = jnp.sum(match.astype(F32), axis=0)
    vecs = [norm1_gain, norm1_shift, norm2_gain, norm2_shift, dense_bias, fc_out_bias]
    pack = jnp.concatenate(
        [v.astype(F32) for v in vecs]
        + [qkv_bias.astype(F32).reshape(-1), fc_in_bias.astype(F32).reshape(-1), counts]
    )
    size = pack.shape[0]
    lanes = -(-size // 1024) * 128
    got = exchange(jnp.pad(pack, (0, 8 * lanes - size)).reshape(8, lanes), "fsdp", False, 1)
    got = got.reshape(shards, 8 * lanes)
    gain1, shift1, gain2, shift2, b_dense, b_out = [
        got[:, k * feats : (k + 1) * feats].reshape(width) for k in range(6)
    ]
    at = 6 * feats
    nq = 3 * heads_here * hd
    b_qkv = got[:, at : at + nq].reshape(shards, 3, heads_here, hd)
    b_qkv = b_qkv.transpose(1, 2, 0, 3).reshape(3, heads_here, HDIM)
    b_qkv = lax.dynamic_index_in_dim(b_qkv, i, 1, keepdims=False).reshape(3 * HDIM)
    at += nq
    b_in = got[:, at : at + units // shards].reshape(shards, ub[0], ub[1])
    b_in = half_of(b_in.transpose(1, 0, 2).reshape(units), i, 0)
    at += units // shards
    counts = jnp.sum(got[:, at : at + SUBSETS], axis=0)
    table = total / (SUBSETS * counts)
    row_scale = jnp.sum(jnp.where(match, table[None, :], 0.0), axis=1)
    carried = cotangent.astype(F32) * row_scale[:, None]
    grad_here = carried.astype(BF16)

    hu = units // 2 // NB
    wi = fc_in_weight.reshape(feats, 2, NB, hu).transpose(1, 0, 2, 3)
    wo = fc_out_weight.reshape(2, NB, hu, feats).transpose(0, 3, 1, 2)
    w2 = jnp.concatenate(
        [
            qkv_weight.reshape(feats, 3, heads_here, HDIM).transpose(2, 0, 1, 3).reshape(2, feats, 3 * HDIM),
            dense_weight.reshape(heads_here, HDIM, feats).transpose(0, 2, 1),
            jnp.stack([wi, wo], axis=3).reshape(2, feats, 2 * NB * hu),
        ],
        axis=2,
    )
    plane = 2 * rows
    start_row = d * plane
    reach = min(dp - 1, -(-(SEQ_LEN - 1) // plane))
    here = start_row + jnp.arange(plane, dtype=jnp.int32)
    docs_here, pos_here = locate(here, seq_starts)
    later = start_row + jnp.arange((reach + 1) * plane, dtype=jnp.int32)
    _, pos_later = locate(later, seq_starts)
    first_later = later - pos_later.astype(jnp.int32) - start_row
    first_later = jnp.where(later < total, first_later, 1 << 30)[None, :]
    cosine, sine = rotary_tables(pos_here)
    ones = jnp.ones((plane, 128 - ROT), F32)
    none = jnp.zeros((plane, 128 - ROT), F32)
    tabs = jnp.stack(
        [
            jnp.concatenate([cosine, cosine, ones], 1),
            jnp.concatenate([-sine, sine, none], 1),
        ]
    )
    vecs = jnp.stack([gain1, shift1, gain2, shift2] + [jnp.zeros_like(gain1)] * 4)
    dims = (rows, width, feats, dp, reach)
    part_w = width // tps
    offset = t * part_w
    cut = lambda vec: lax.dynamic_slice_in_dim(vec, offset, part_w, vec.ndim - 1)
    bias = (cut(b_dense) + cut(b_out)).reshape(1, -1)
    cot_here = cut(cotangent).reshape(rows, 2, part_w // 2).transpose(1, 0, 2)
    mixed, tokens_grad, norm_grads, bias_sums, g_qkv, g_dense, g_in, g_out = block(
        tokens, grad_here, w2, vecs, b_qkv.reshape(1, -1), b_in.reshape(1, -1), bias, cot_here, row_scale[None, :], tabs,
        first_later, dims,
    )[GROUPS:]
    qkv_weight_grad = g_qkv.transpose(1, 0, 2).astype(F32)
    dense_weight_grad = g_dense.astype(F32)
    fc_in_weight_grad = g_in.astype(F32)
    fc_out_weight_grad = g_out.astype(F32)
    bias_grad = norm_grads[4]

    bias_sums = jnp.sum(bias_sums.reshape(dp, 2, 8, units // 2), axis=0)
    in_bias_grad = bias_sums[:, 0].reshape(ub[0], shards * ub[1])
    in_bias_grad = lax.dynamic_slice_in_dim(in_bias_grad, f * ub[1], ub[1], 1)
    qkv_bias_grad = bias_sums[:, 1, : 3 * HDIM].reshape(2, 3, HDIM).transpose(1, 0, 2)
    qkv_bias_grad = lax.dynamic_slice_in_dim(qkv_bias_grad, f * hd, hd, 2)
    return (
        mixed,
        tokens_grad,
        qkv_weight_grad,
        qkv_bias_grad,
        dense_weight_grad,
        bias_grad,
        fc_in_weight_grad,
        in_bias_grad,
        fc_out_weight_grad,
        bias_grad,
        norm_grads[0],
        norm_grads[1],
        norm_grads[2],
        norm_grads[3],
    )


def solution(mesh):
    in_specs = (
        P("fsdp", None),
        P("fsdp", None, "tp"),
        P(None, "tp", "fsdp"),
        P("tp", "fsdp"),
        P("fsdp"),
        P("fsdp", "tp"),
        P("tp", "fsdp"),
        P("tp", "fsdp"),
        P("fsdp"),
        P("fsdp"),
        P("fsdp"),
        P("fsdp"),
        P("fsdp"),
        P("fsdp", None),
        P("fsdp"),
        P(),
    )
    out_specs = (
        P("fsdp", "tp"),
        P("fsdp", "tp"),
        P("fsdp", None, "tp"),
        P(None, "tp", "fsdp"),
        P("tp", "fsdp"),
        P("fsdp"),
        P("fsdp", "tp"),
        P("tp", "fsdp"),
        P("tp", "fsdp"),
        P("fsdp"),
        P("fsdp"),
        P("fsdp"),
        P("fsdp"),
        P("fsdp"),
    )
    return jax.shard_map(
        on_device, mesh=mesh, in_specs=in_specs, out_specs=out_specs, check_vma=False
    )
```

```python
import functools
import math

import jax
import jax.numpy as jnp
from jax import lax
from jax.experimental import pallas as pl
from jax.experimental.pallas import tpu as pltpu
from jax.sharding import PartitionSpec as P

HDIM = 256
ROT = 64
SUBSETS = 22
SEQ_LEN = 2048
EPS = 1e-05
F32 = jnp.float32
BF16 = jnp.bfloat16
MESH = pl.DeviceIdType.MESH
ANY = pl.BlockSpec(memory_space=pl.ANY)
VMEM = pl.BlockSpec(memory_space=pltpu.VMEM)


def mm(left, right, dims):
    return lax.dot_general(left, right, (dims, ((), ())), preferred_element_type=F32)


def plain(left, right):
    return mm(left, right, ((1,), (0,)))


def inner(left, right):
    return mm(left, right, ((0,), (0,)))


def against(left, right):
    return mm(left, right, ((1,), (1,)))


def rotary_tables(positions):
    half = ROT // 2
    steps = jnp.arange(half, dtype=F32)
    freq = 1.0 / 10000.0 ** (steps * 2.0 / ROT)
    angle = positions[:, None] * freq[None, :]
    return jnp.cos(angle), jnp.sin(angle)


def locate(indices, starts):
    above = indices[:, None] >= starts[None, :]
    doc_ids = jnp.sum(above.astype(jnp.int32), axis=1) - 1
    pick = doc_ids[:, None] == jnp.arange(starts.shape[0], dtype=jnp.int32)[None, :]
    first = jnp.sum(jnp.where(pick, starts[None, :], 0), axis=1)
    return (doc_ids, (indices - first).astype(F32))


def half_of(value, which, axis):
    size = value.shape[axis] // 2
    return lax.dynamic_slice_in_dim(value, which * size, size, axis)


def exchange_kernel(axis, spread, v_ref, o_ref, ssem, rsem):
    count = o_ref.shape[0]
    me = lax.axis_index(axis)

    def peer(step):
        return lax.rem(me + step, count)

    barrier = pltpu.get_barrier_semaphore()
    for step in range(1, count):
        pl.semaphore_signal(barrier, 1, device_id={axis: peer(step)}, device_id_type=MESH)
    pl.semaphore_wait(barrier, count - 1)

    def copy(step):
        return pltpu.make_async_remote_copy(
            src_ref=v_ref.at[peer(step)] if spread else v_ref,
            dst_ref=o_ref.at[me],
            send_sem=ssem.at[step],
            recv_sem=rsem.at[step],
            device_id={axis: peer(step)},
            device_id_type=MESH,
        )

    for step in range(1, count):
        copy(step).start()
    o_ref[me] = v_ref[me] if spread else v_ref[...]
    for step in range(1, count):
        copy(step).wait()


def exchange(value, axis, spread, cid):
    count = lax.axis_size(axis)
    block = value.shape[1:] if spread else value.shape
    return pl.pallas_call(
        functools.partial(exchange_kernel, axis, spread),
        out_shape=jax.ShapeDtypeStruct((count,) + block, value.dtype),
        in_specs=[VMEM],
        out_specs=VMEM,
        scratch_shapes=[pltpu.SemaphoreType.DMA((count,)), pltpu.SemaphoreType.DMA((count,))],
        compiler_params=pltpu.CompilerParams(collective_id=cid, has_side_effects=True),
        name="exchange",
    )(value)


NB = 4
GROUPS = 1 + NB
ORDER = (
    "pair0", "own0i", "own0o", "own1o", "mate0o", "pair1", "pair4", "rx0", "pair3", "mate0i", "mate1i",
    "mate1o", "own3i", "arr01", "own1i", "rc0", "pair2", "mate3i", "arr02", "own2i", "rx1", "arr11", "arr03",
    "mate2i", "rc1", "stats", "arr12", "own4i", "proj", "mate4i", "datt", "arr13", "ffn0", "kv1k", "kv1v",
    "qd1", "mate2o", "st13i", "st12o", "st12i", "own2o", "st11i", "mate3o", "kv2v", "own4o", "kv2k", "att0",
    "att1", "att2", "att3", "ls0", "sta3i", "arr21", "sta2i", "qd2", "ls1", "dkv0", "mate4o", "sta2o", "dkv1",
    "dkv2", "arr22", "dkv3", "sta1i", "arr41", "stb3i", "arr23", "own3o", "ffn1", "st23i", "arr31", "st22o",
    "st22i", "arr32", "stb2i", "arr33", "stb2o", "arr42", "st21i", "ffn2", "st33i", "st11o", "arr43", "ffn3",
    "out", "stb1i", "st43i", "st32o", "hid", "stb1o", "far00", "far01", "qk", "sta1o", "st21o", "st32i",
    "far10", "finb", "st42o", "mt0", "far11", "fina", "fin1", "st42i", "st31i", "st31o", "last0", "small",
    "mt1", "st41i", "fin2", "st41o", "fin3", "last1", "fin4",
)


def turn(u, tabs, at, sign):
    lo, hi = u[:, :128], u[:, 128:]
    lane = lax.broadcasted_iota(jnp.int32, lo.shape, 1)
    other = jnp.where(lane < ROT // 2, pltpu.roll(lo, 128 - ROT // 2, 1), pltpu.roll(lo, ROT // 2, 1))
    a = other * tabs[1, at, :]
    lo = lo * tabs[0, at, :] + (a if sign > 0 else -a)
    return jnp.concatenate([lo, hi], axis=1)


def block_kernel(
    dims,
    tok, gh, w_att, w_fc, vecs, bq, bin_, bias, cot, row_scale, tabs, firstq,
    *refs,
):
    outs, refs = refs[:GROUPS], refs[GROUPS:]
    (
        mixed_o, dtok_o, norm_o, bias_o, dq_o, dd_o, di_o, do_o, xs, gs, wbuf, wins, st,
        act, dpre, dqkv, att, tpr0, tpr1, tpr2, rs_a, rs_f, norms, tra, trf, sums, bsum, sum_s, sum_r, row_r, nrm_r,
        lsem, tsem, psem, zsem, zrec, ksem, qsem, lssem, ssem, rsem, fsem, bsem, xsem, usem, near_ok, far_ok, mate_ok,
    ) = refs
    R, D, feats, dp, reach = dims
    F, T = 2 * dp, row_r.shape[0]
    f = lax.axis_index("fsdp")
    t = lax.axis_index("tp")
    d, i = f // 2, lax.rem(f, 2)
    core = lax.rem(t, 2)
    plane, pf = 2 * R, 2 * feats
    qb = min(256, plane)
    nb = plane // qb
    fb = min(256, pf)
    aw = 4 * HDIM
    gw = act.shape[1]
    hu = gw // NB
    pw = D // T
    slots = reach + 1
    tn, tf = t + 1 - 2 * core, lax.rem(t + 2, T)
    mate, near, far = (f + 1 - 2 * i, t), (f, tn), (f, tf)
    has = (d + 1 < dp, d >= 1)
    inward = jnp.where(d < dp // 2, 0, 1)
    ways = {"i": inward, "o": 1 - inward}
    scale = 1.0 / math.sqrt(HDIM)

    barrier = pltpu.get_barrier_semaphore()
    for s in range(1, F):
        pl.semaphore_signal(barrier, 1, device_id=(lax.rem(f + s, F), t), device_id_type=MESH)
    for s in range(1, T):
        pl.semaphore_signal(barrier, 1, device_id=(f, lax.rem(t + s, T)), device_id_type=MESH)
    pl.semaphore_wait(barrier, F + T - 2)

    def rc(src, dst, ss, rv, who):
        return pltpu.make_async_remote_copy(
            src_ref=src, dst_ref=dst, send_sem=ss, recv_sem=rv, device_id=who, device_id_type=MESH
        )

    def rows(b):
        return pl.ds(pl.multiple_of(b * qb, qb), qb)

    def toward(way):
        return (f + 2 - 4 * way, t)

    def open_way(way):
        return jnp.where(way == 0, d + 1 < dp, d >= 1)

    def slot(g, s):
        return outs[g].at[pl.ds(s * feats, feats), :]

    def part(half, g):
        return w_att.at[half] if g == 0 else w_fc.at[g - 1, half]

    def pair_copy(g):
        return rc(part(1 - i, g), slot(g, f), psem.at[0, g], psem.at[1, g], mate)

    def mine_copy(g):
        return pltpu.make_async_copy(part(i, g), slot(g, f), lsem.at[g])

    def z_own(g, way):
        return rc(part(i, g), slot(g, f), zsem.at[g, 0, way, 0], zrec.at[g, f], toward(way))

    def z_mate(g, way):
        s = f + 1 - 2 * i
        return rc(slot(g, s), slot(g, s), zsem.at[g, 0, way, 1], zrec.at[g, s], toward(way))

    def z_fwd(g, k, way, j):
        s = (d - k) * 2 + j if way == 0 else (d + k) * 2 + j
        return rc(slot(g, s), slot(g, s), zsem.at[g, k, way, j], zrec.at[g, s], toward(way))

    def send_own(g, io):
        @pl.when(open_way(ways[io]))
        def _():
            z_own(g, ways[io]).start()

    def send_mate(g, io, wait):
        if wait:
            pair_copy(g).wait_recv()

        @pl.when(open_way(ways[io]))
        def _():
            z_mate(g, ways[io]).start()

    def from_dist(k, way):
        return d >= k if way == 0 else d + k < dp

    def arrive(g, k):
        for way in range(2):
            @pl.when(from_dist(k, way))
            def _():
                for j in range(2):
                    z_fwd(g, k, way, j).wait_recv()

                    @pl.when(has[way])
                    def _():
                        z_fwd(g, k, way, j).start()

    def gather_sent(g):
        pair_copy(g).wait_send()
        for way in range(2):
            @pl.when(has[way])
            def _():
                z_own(g, way).wait_send()
                z_mate(g, way).wait_send()
            for k in range(1, dp - 1):
                @pl.when(from_dist(k, way) & has[way])
                def _():
                    for j in range(2):
                        z_fwd(g, k, way, j).wait_send()

    def load(*pairs):
        copies = [pltpu.make_async_copy(src, dst, bsem.at[n]) for n, (src, dst) in enumerate(pairs)]
        for c in copies:
            c.start()
        for c in copies:
            c.wait()

    hr = R // 2
    given = ((tok, xs), (gh, gs))

    def rows_x(a):
        ref, out = given[a]
        return rc(
            ref.at[pl.ds(core * hr, hr), :], out.at[pl.ds(i * R + core * hr, hr), :],
            tsem.at[a, 0], tsem.at[a, 1], mate,
        )

    def rows_c(a):
        at = given[a][1].at[pl.ds((1 - i) * R + core * hr, hr), :]
        return rc(at, at, tsem.at[a, 2], tsem.at[a, 3], near)

    def rows_own(a):
        ref, out = given[a]
        return pltpu.make_async_copy(ref, out.at[pl.ds(i * R, R), :], lsem.at[GROUPS + a])

    def rows_on(a):
        rows_x(a).wait_recv()
        rows_c(a).start()

    def rows_done(a):
        rows_c(a).wait_recv()
        rows_own(a).wait()

    def hat(at):
        return (xs[at, :].astype(F32) - norms[at, 0:1]) * norms[at, 1:2]

    def stats():
        def block(b, _):
            x = xs[rows(b), :].astype(F32)
            m = jnp.mean(x, axis=-1, keepdims=True)
            c = x - m
            norms[rows(b), 0:1] = m
            norms[rows(b), 1:2] = lax.rsqrt(jnp.mean(c * c, axis=-1, keepdims=True) + EPS)
            return 0

        rows_done(0)
        lax.fori_loop(0, nb, block, 0)

    def proj():
        def block(b, _):
            at = rows(b)
            h1 = (hat(at) * vecs[0:1, :] + vecs[1:2, :]).astype(BF16)
            y = plain(h1, wbuf[:, : 3 * HDIM]) + bq[...]
            wins[2 * slots, at, :] = (turn(y[:, :HDIM], tabs, at, 1).astype(BF16).astype(F32) * scale).astype(BF16)
            wins[reach, at, :] = turn(y[:, HDIM : 2 * HDIM], tabs, at, 1).astype(BF16)
            wins[slots + reach, at, :] = y[:, 2 * HDIM :].astype(BF16)
            return 0

        mine_copy(0).wait()
        load((outs[0], wbuf))
        lax.fori_loop(0, nb, block, 0)

        @pl.when(has[0])
        def _():
            kv_copy(0, 0).start()
            kv_copy(1, 0).start()

    def datt():
        def block(b, _):
            at = rows(b)
            wins[3 * slots, at, :] = plain(gs[at, :], wbuf[:, 3 * HDIM :]).astype(BF16)
            return 0

        rows_done(1)
        lax.fori_loop(0, nb, block, 0)

        @pl.when(has[1])
        def _():
            qd_copy(0, 0).start()
            qd_copy(1, 0).start()

    def ffn(h):
        mine = slice(h * hu, (h + 1) * hu)

        def block(b, _):
            at = rows(b)
            h2 = (hat(at) * vecs[2:3, :] + vecs[3:4, :]).astype(BF16)
            pre = plain(h2, wbuf[:, :hu]) + bin_[:, mine]
            cdf = 0.5 * (1.0 + lax.erf(pre * (1.0 / math.sqrt(2.0))))
            act[at, mine] = (pre * cdf).astype(BF16)
            slope = cdf + pre * jnp.exp(-0.5 * pre * pre) * (1.0 / math.sqrt(2.0 * math.pi))
            dp_b = (plain(gs[at, :], wbuf[:, hu : 2 * hu]) * slope).astype(BF16)
            dpre[at, mine] = dp_b
            bsum[0:1, mine] += jnp.sum(dp_b.astype(F32), axis=0, keepdims=True)
            return 0

        mine_copy(1 + h).wait()
        load((outs[1 + h], wbuf.at[:, pl.ds(0, 2 * hu)]))
        lax.fori_loop(0, nb, block, 0)

    def kv_copy(h, k):
        w = wins.at[h * slots + reach - k]
        return rc(w, wins.at[h * slots + reach - k - 1], ksem.at[h, 0, k], ksem.at[h, 1, k + 1], toward(0))

    def kv_recv(h, k):
        w = wins.at[h * slots + reach - k]
        return rc(w, w, ksem.at[h, 0, k - 1], ksem.at[h, 1, k], toward(0))

    def kv_step(h, k):
        @pl.when(d >= k)
        def _():
            kv_recv(h, k).wait_recv()
            if k < reach:
                @pl.when(has[0])
                def _():
                    kv_copy(h, k).start()

        @pl.when(d < k)
        def _():
            wins[h * slots + reach - k] = jnp.zeros((plane, HDIM), BF16)

    def qd_copy(h, k):
        w = wins.at[(2 + h) * slots + k]
        return rc(w, wins.at[(2 + h) * slots + k + 1], qsem.at[h, 0, k], qsem.at[h, 1, k + 1], toward(1))

    def qd_recv(h, k):
        w = wins.at[(2 + h) * slots + k]
        return rc(w, w, qsem.at[h, 0, k - 1], qsem.at[h, 1, k], toward(1))

    def qd_step(k):
        @pl.when(d + k < dp)
        def _():
            for h in range(2):
                qd_recv(h, k).wait_recv()
                if k < reach:
                    @pl.when(has[1])
                    def _():
                        qd_copy(h, k).start()

        @pl.when(d + k >= dp)
        def _():
            for h in range(2):
                wins[(2 + h) * slots + k] = jnp.zeros((plane, HDIM), BF16)

    def stat_at(k):
        return st.at[:, pl.ds(k * plane, plane)]

    def stat_copy(k):
        return rc(stat_at(0), stat_at(k), lssem.at[0, k], lssem.at[1, k], (f - 2 * k, t))

    def stat_send():
        for k in range(1, reach + 1):
            @pl.when(d >= k)
            def _():
                stat_copy(k).start()

    def stat_wait():
        for k in range(1, reach + 1):
            @pl.when(d + k < dp)
            def _():
                stat_copy(k).wait_recv()

            @pl.when(d + k >= dp)
            def _():
                st[:, k * plane : (k + 1) * plane] = jnp.zeros((8, plane), F32)

    span = SEQ_LEN + qb
    base = reach * plane - SEQ_LEN
    parts = 4

    def wide(n, start):
        flat = wins.reshape(wins.shape[0] * plane, HDIM)
        return flat[pl.ds(pl.multiple_of(n * slots * plane + start, qb), span), :]

    def attention(n):
        def block(b, _):
            at = rows(b)
            keys_at = base + b * qb
            keys = wide(0, keys_at)
            vals = wide(1, keys_at)
            s = against(wins[2 * slots, at, :], keys)
            c = base + b * qb + lax.broadcasted_iota(jnp.int32, (qb, span), 1)
            r = reach * plane + b * qb + lax.broadcasted_iota(jnp.int32, (qb, span), 0)
            low = jnp.broadcast_to(firstq[:, at].astype(F32), (128, qb)).T[:, 0:1] + float(reach * plane)
            s = jnp.where((c.astype(F32) >= low) & (c <= r), s, -1e30)
            top = jnp.max(s, axis=1, keepdims=True)
            e = jnp.exp(s - top)
            total = jnp.sum(e, axis=1, keepdims=True)
            p = e * (1.0 / total)
            att[at, :] = plain(p.astype(BF16), vals).astype(BF16)
            dpr = against(wins[3 * slots, at, :], vals)
            delta = jnp.sum(p * dpr, axis=1, keepdims=True)
            ds = (p * (dpr - delta)).astype(BF16)
            dq = plain(ds, keys) * scale
            dqkv[at, :HDIM] = turn(dq, tabs, at, -1).astype(BF16)
            lane = lax.broadcasted_iota(jnp.int32, (qb, 128), 1)
            both = jnp.where(lane == 0, top + jnp.log(total), jnp.where(lane == 1, delta, 0.0))
            st[:, at] = both.T[:8]
            return 0

        lax.fori_loop(n * nb // parts, (n + 1) * nb // parts, block, 0)

    def key_grads(n):
        def block(b, _):
            at = rows(b)
            rows_at = pl.ds(pl.multiple_of(b * qb, qb), span)
            q = wide(2, b * qb)
            da = wide(3, b * qb)
            s = against(wins[reach, at, :], q)
            c = b * qb + lax.broadcasted_iota(jnp.int32, (qb, span), 0)
            r = b * qb + lax.broadcasted_iota(jnp.int32, (qb, span), 1)
            s = jnp.where((c >= firstq[:, rows_at]) & (c <= r), s - st[0:1, rows_at], -1e30)
            p = jnp.exp(s)
            dqkv[at, 2 * HDIM :] = plain(p.astype(BF16), da).astype(BF16)
            dpr = against(wins[slots + reach, at, :], da)
            ds = (p * (dpr - st[1:2, rows_at])).astype(BF16)
            dqkv[at, HDIM : 2 * HDIM] = turn(plain(ds, q), tabs, at, -1).astype(BF16)
            return 0

        lax.fori_loop(n * nb // parts, (n + 1) * nb // parts, block, 0)

    def rs(g):
        return rs_a.at[g] if g < 2 else rs_f.at[g - 2]

    def grad_part(g, p, c):
        cols = pl.ds(pl.multiple_of(p * pf + c * fb, fb), fb)
        z = (xs[:, cols].astype(F32) - norms[:, 0:1]) * norms[:, 1:2]
        n = 0 if g < 2 else 2
        h = (z * vecs[n : n + 1, cols] + vecs[n + 1 : n + 2, cols]).astype(BF16)
        if g == 0:
            return inner(h, dqkv[:, :HDIM]), inner(gs[:, cols], att[...])
        if g == 1:
            return (inner(h, dqkv[:, HDIM:]),)
        mine = slice((g - 2) * hu, (g - 1) * hu)
        return inner(h, dpre[:, mine]), inner(gs[:, cols], act[:, mine])

    def add_part(g, p, second=None):
        def block(c, _):
            at = pl.ds(pl.multiple_of(c * fb, fb), fb)
            left = 0
            for v in grad_part(g, p, c):
                cols = slice(left, left + v.shape[1])
                left += v.shape[1]
                v = rs(g)[p, at, cols].astype(F32) + v
                if second is not None:
                    v = v + rs(g)[second, at, cols].astype(F32)
                rs(g)[p, at, cols] = v.astype(BF16)
            return 0

        lax.fori_loop(0, pf // fb, block, 0)

    def rs_copy(g, k, way):
        p = d + k * (1 - 2 * way)
        to = jnp.where((way == 1) & (k == 1), dp, p)
        return rc(rs(g).at[p], rs(g).at[to], ssem.at[g, k, way], rsem.at[g, to], toward(way))

    def rs_wait(g, p):
        return rc(rs(g).at[p], rs(g).at[p], ssem.at[g, 0, 0], rsem.at[g, p], mate)

    def clear(g, p):
        rs(g)[p] = jnp.zeros(rs(g).shape[1:], BF16)

    def stage(g, k, io):
        way = ways[io]
        p = d + k * (1 - 2 * way)
        came = open_way(1 - way)

        @pl.when((p >= 0) & (p < dp))
        def _():
            @pl.when(came)
            def _():
                rs_wait(g, p).wait_recv()

            @pl.when(jnp.logical_not(came))
            def _():
                clear(g, p)

            add_part(g, p)
            rs_copy(g, k, way).start()

    def final_copies(g):
        lo = pl.multiple_of(i * HDIM, HDIM)
        pieces = []
        for j in range(2):
            at = pl.ds((i if j == 0 else 1 - i) * feats, feats)
            src = rs(g).at[d, at]
            if g == 0:
                dst = (dq_o.at[0, :, pl.ds(lo, HDIM)], dd_o.at[pl.ds(lo, HDIM), :])
                src = (src.at[:, pl.ds(0, HDIM)], tra.at[j])
            elif g == 1:
                dst = tuple(dq_o.at[n, :, pl.ds(lo, HDIM)] for n in (1, 2))
                src = tuple(src.at[:, pl.ds(n * HDIM, HDIM)] for n in (0, 1))
            else:
                u = pl.multiple_of(i * gw + (g - 2) * hu, hu)
                dst = (di_o.at[:, pl.ds(u, hu)], do_o.at[pl.ds(u, hu), :])
                src = (src.at[:, pl.ds(0, hu)], trf.at[g - 2, j])
            for n in range(2):
                if j == 0:
                    pieces.append(pltpu.make_async_copy(src[n], dst[n], fsem.at[g, n, 0]))
                else:
                    pieces.append(rc(src[n], dst[n], fsem.at[g, n, 1], fsem.at[g, n, 2], mate))
        return pieces

    def final(g):
        for p, came in ((d, has[1]), (dp, has[0])):
            @pl.when(came)
            def _():
                rs_wait(g, p).wait_recv()

            @pl.when(jnp.logical_not(came))
            def _():
                clear(g, p)

        add_part(g, d, dp)
        if g != 1:
            cut = HDIM if g == 0 else hu
            for j in range(2):
                at = pl.ds(pl.multiple_of((i if j == 0 else 1 - i) * feats, feats), feats)
                turned = rs(g)[d, at, cut:].astype(F32).T.astype(BF16)
                if g == 0:
                    tra[j] = turned
                else:
                    trf[g - 2, j] = turned
        for c in final_copies(g):
            c.start()

    def out_step(up):
        def dense(b, _):
            at = rows(b)
            for c in range(T):
                y = against(att[at, :], wbuf[c * pw : (c + 1) * pw, :HDIM])
                for e in range(2):
                    v = up[2 * c + e, at, :].astype(F32) + y[:, e * HDIM : (e + 1) * HDIM]
                    up[2 * c + e, at, :] = v.astype(BF16)
            return 0

        def block(b, _):
            at = rows(b)
            sums[4:5, :] += jnp.sum(gs[at, :].astype(F32), axis=0, keepdims=True)
            for c in range(T):
                cols = slice(c * pw, (c + 1) * pw)
                y = against(act[at, :], wbuf[cols, :])
                for e in range(2):
                    up[2 * c + e, at, :] = y[:, e * HDIM : (e + 1) * HDIM].astype(BF16)
            return 0

        load(
            *[(outs[1 + h].at[:, pl.ds(hu, hu)], wbuf.at[:, pl.ds(h * hu, hu)]) for h in range(NB)],
        )
        lax.fori_loop(0, nb, block, 0)
        load((outs[0].at[:, pl.ds(3 * HDIM, HDIM)], wbuf.at[:, pl.ds(0, HDIM)]))
        lax.fori_loop(0, nb, dense, 0)
        tp_near(up, False)

    def hidden_step():
        def block(b, _):
            at = rows(b)
            e2 = against(dpre[at, :], wbuf[...])
            z = hat(at)
            sums[2:3, :] += jnp.sum(e2 * z, axis=0, keepdims=True)
            sums[3:4, :] += jnp.sum(e2, axis=0, keepdims=True)
            u = (e2 * vecs[2:3, :]).astype(BF16)
            for c in range(2 * T):
                wins[c, at, :] = u[:, c * HDIM : (c + 1) * HDIM]
            return 0

        for k in range(reach):
            for h in range(2):
                @pl.when((d >= k) & has[0])
                def _():
                    kv_copy(h, k).wait_send()

                @pl.when((d + k < dp) & has[1])
                def _():
                    qd_copy(h, k).wait_send()

        pl.semaphore_signal(far_ok, 1, device_id=far, device_id_type=MESH)
        pl.semaphore_signal(mate_ok, 1, device_id=mate, device_id_type=MESH)
        load(
            *[(outs[1 + h].at[:, pl.ds(0, hu)], wbuf.at[:, pl.ds(h * hu, hu)]) for h in range(NB)],
        )
        lax.fori_loop(0, nb, block, 0)

    def qkv_step():
        def block(b, _):
            at = rows(b)
            e1 = against(dqkv[at, :], wbuf[:, : 3 * HDIM])
            z = hat(at)
            sums[0:1, :] += jnp.sum(e1 * z, axis=0, keepdims=True)
            sums[1:2, :] += jnp.sum(e1, axis=0, keepdims=True)
            bsum[1:2, : 3 * HDIM] += jnp.sum(dqkv[at, :].astype(F32), axis=0, keepdims=True)
            u = e1 * vecs[0:1, :]
            for c in range(2 * T):
                wins[c, at, :] = (wins[c, at, :].astype(F32) + u[:, c * HDIM : (c + 1) * HDIM]).astype(BF16)
            return 0

        load((outs[0], wbuf))
        lax.fori_loop(0, nb, block, 0)
        tp_near(wins, True)
        for s in range(F):
            sum_s[s] = sums[:, s * feats : (s + 1) * feats]
        for s in range(1, F):
            sum_copy(s).start()
            bias_copy(s).start()
        sum_r[f] = sum_s[f]
        bias_o[f] = bsum[...]

    def half(h):
        return pl.ds(pl.multiple_of((1 - i if h == 0 else i) * R, R), R)

    def half_block(h, b):
        return pl.ds(pl.multiple_of((1 - i if h == 0 else i) * R + b * qb, qb), qb)

    def near_copy(up, second, h, j):
        blk = tn if j == 0 else lax.rem(tn + 2, T)
        n = 2 * h + j
        src = up.at[pl.ds(2 * blk, 2), half(h), :]
        return rc(src, tpr0.at[j, :, half(h), :], usem.at[int(second), 0, n], usem.at[int(second), 1, n], near)

    def landing(second):
        return (wins.at[pl.ds(2 * T, 2)], wins.at[pl.ds(2 * T + 2, 2), pl.ds(0, R), :]) if second else (tpr1, tpr2)

    def far_copy(up, h, second):
        src, dst = up.at[pl.ds(2 * tf, 2), half(h), :], landing(second)[0].at[:, half(h), :]
        return rc(src, dst, usem.at[int(second), 0, 4 + h], usem.at[int(second), 1, 4 + h], far)

    def mate_copy(up, second):
        n = int(second)
        src = up.at[pl.ds(2 * t, 2), half(0), :]
        return rc(src, landing(second)[1], usem.at[n, 0, 6], usem.at[n, 1, 6], mate)

    def tp_near(up, second):
        if second:
            pl.semaphore_wait(near_ok, 1)
        for h in range(2):
            for j in (1, 0):
                near_copy(up, second, h, j).start()

    def tp_far(up, second, h):
        def block(b, _):
            at = half_block(h, b)
            for blk, j in ((tf, 1), (t, 0)):
                for e in range(2):
                    v = up[2 * blk + e, at, :].astype(F32) + tpr0[j, e, at, :].astype(F32)
                    up[2 * blk + e, at, :] = v.astype(BF16)
            return 0

        near_copy(up, second, h, 1).wait_recv()
        near_copy(up, second, h, 0).wait_recv()
        lax.fori_loop(0, R // qb, block, 0)
        far_steps.append((second, h))
        if second and (True, 1 - h) not in far_steps:
            pl.semaphore_wait(far_ok, 1)
        if not second and (False, 1 - h) in far_steps:
            pl.semaphore_signal(near_ok, 1, device_id=near, device_id_type=MESH)
        far_copy(up, h, second).start()

    def came_far(second, e, at):
        return (wins[2 * T + e, at, :] if second else tpr1[e, at, :]).astype(F32)

    def tp_mate(up, second):
        def block(b, _):
            at = half_block(0, b)
            for e in range(2):
                v = up[2 * t + e, at, :].astype(F32) + came_far(second, e, at)
                up[2 * t + e, at, :] = v.astype(BF16)
            return 0

        far_copy(up, 0, second).wait_recv()
        lax.fori_loop(0, R // qb, block, 0)
        if second:
            pl.semaphore_wait(mate_ok, 1)
        mate_copy(up, second).start()

    def tp_last(up, second):
        far_copy(up, 1, second).wait_recv()
        mate_copy(up, second).wait_recv()
        here = half(1)
        v = []
        for e in range(2):
            last = wins[2 * T + 2 + e, :R, :] if second else tpr2[e]
            v.append(up[2 * t + e, here, :].astype(F32) + came_far(second, e, here) + last.astype(F32))
        v = jnp.concatenate(v, axis=1)
        x = xs[here, pl.ds(pl.multiple_of(t * pw, pw), pw)].astype(F32)
        if second:
            u = v
            z = (x - norms[here, 0:1]) * norms[here, 1:2]
            lane = lax.broadcasted_iota(jnp.int32, (R, 128), 1)
            one, two = jnp.sum(u, axis=1, keepdims=True), jnp.sum(u * z, axis=1, keepdims=True)
            row_r[t] = jnp.where(lane == 0, one, jnp.where(lane == 1, two, 0.0)).T[:8]
            for s in range(1, T):
                row_copy(s).start()
            for s in range(1, T):
                row_copy(s).wait()
            both = row_r[0]
            for s in range(1, T):
                both = both + row_r[s]
            both = jnp.concatenate([both, jnp.zeros((120, R), F32)], axis=0).T * (1.0 / D)
            dx = norms[here, 1:2] * (u - both[:, 0:1] - z * both[:, 1:2])
            kept = env["up"]
            load((cot, kept.at[pl.ds(0, 2), pl.ds(0, R), :]))
            c = jnp.concatenate([kept[0, :R, :], kept[1, :R, :]], axis=1).astype(F32)
            c = c * jnp.broadcast_to(row_scale[...], (128, R)).T[:, 0:1]
            dtok_o[...] = (c + dx).astype(BF16)
        else:
            mixed_o[...] = (x + v + bias[...]).astype(BF16)
        for h in range(2):
            near_copy(up, second, h, 0).wait_send()
            near_copy(up, second, h, 1).wait_send()
            far_copy(up, h, second).wait_send()
        mate_copy(up, second).wait_send()

    def row_copy(s):
        return rc(row_r.at[t], row_r.at[t], xsem.at[0, 0, s], xsem.at[0, 1, s], (f, lax.rem(t + s, T)))

    def norm_copy(s):
        return rc(nrm_r.at[t], nrm_r.at[t], xsem.at[1, 0, s], xsem.at[1, 1, s], (f, lax.rem(t + s, T)))

    def sum_copy(s):
        to = lax.rem(f + s, F)
        return rc(sum_s.at[to], sum_r.at[f], xsem.at[2, 0, s], xsem.at[2, 1, s], (to, t))

    def bias_copy(s):
        return rc(bsum, bias_o.at[f], xsem.at[3, 0, s], xsem.at[3, 1, s], (lax.rem(f + s, F), t))

    def small_sums():
        for s in range(1, F):
            sum_copy(s).wait()
            bias_copy(s).wait()
        v = sum_r[0]
        for s in range(1, F):
            v = v + sum_r[s]
        nrm_r[t] = v
        for s in range(1, T):
            norm_copy(s).start()
        for s in range(1, T):
            norm_copy(s).wait()
        both = nrm_r[0]
        for s in range(1, T):
            both = both + nrm_r[s]
        row = lax.broadcasted_iota(jnp.int32, both.shape, 0)
        norm_o[...] = jnp.where(row == 4, v * 0.5, both)

    env = {}
    far_out = tuple(range(dp - 1, 2, -1))
    groups = {"a": 0, "b": 1} | {str(n + 1): 2 + n for n in range(NB)}
    paired, far_steps = set(), []

    def step(name):
        kind, rest = name.rstrip("0123456789abiokv"), ""
        rest = name[len(kind):]
        if kind == "pair":
            pair_copy(int(rest)).start()
            mine_copy(int(rest)).start()
        elif kind == "own":
            send_own(int(rest[0]), rest[1])
        elif kind == "mate":
            send_mate(int(rest[0]), rest[1], rest[0] not in paired)
            paired.add(rest[0])
        elif kind == "arr":
            g, k = int(rest[0]), int(rest[1])
            for n in range(k, dp if k == 3 else k + 1):
                arrive(g, n)
        elif kind == "rx":
            rows_x(int(rest)).start()
            rows_own(int(rest)).start()
        elif kind == "rc":
            rows_on(int(rest))
        elif kind == "stats":
            stats()
        elif kind == "proj":
            proj()
        elif kind == "datt":
            datt()
        elif kind == "ffn":
            ffn(int(rest))
        elif kind == "att":
            attention(int(rest))
        elif kind == "qd":
            for k in range(1, reach) if rest == "1" else (reach,):
                qd_step(k)
        elif kind == "ls":
            stat_send() if rest == "0" else stat_wait()
        elif kind == "d":
            key_grads(int(rest[-1]))
        elif kind == "st":
            g, k, io = groups[rest[0]], int(rest[1]), rest[2]
            if k == 3:
                for n in far_out:
                    stage(g, n, io)
            elif k == 2 and io == "o":
                for n in far_out + (2,):
                    stage(g, n, io)
            else:
                stage(g, k, io)
        elif kind == "fin":
            final(groups[rest])
        elif kind == "out":
            out_step(env["up"])
        elif kind == "far":
            tp_far(env["up"] if rest[0] == "0" else wins, rest[0] == "1", int(rest[1]))
        elif kind == "mt":
            tp_mate(env["up"] if rest == "0" else wins, rest == "1")
        elif kind == "last":
            tp_last(env["up"] if rest == "0" else wins, rest == "1")
        elif kind == "hid":
            hidden_step()
        elif kind == "q":
            qkv_step()
        elif kind == "small":
            small_sums()
        else:
            hop = int(rest[-2])
            for k in range(1, reach) if hop == 1 else (reach,):
                kv_step("kv".index(rest[-1]), k)

    def finish_scope(up):
        env["up"] = up
        for name in ORDER[ORDER.index("out") :]:
            step(name)

    sums[...] = jnp.zeros_like(sums)
    bsum[...] = jnp.zeros_like(bsum)
    for name in ORDER[: ORDER.index("out")]:
        step(name)
    pl.run_scoped(finish_scope, pltpu.VMEM((2 * T, plane, HDIM), BF16))

    for k in range(reach):
        @pl.when(d >= k + 1)
        def _():
            stat_copy(k + 1).wait_send()
    for a in range(2):
        rows_x(a).wait_send()
        rows_c(a).wait_send()
    for g in range(GROUPS):
        gather_sent(g)
    for g in range(2 + NB):
        for k in range(1, dp):
            for way in range(2):
                @pl.when(from_dist(k, 1 - way))
                def _():
                    rs_copy(g, k, way).wait_send()
        for c in final_copies(g):
            c.wait()


def block(tok, gh, w_att, w_fc, vecs, bq, b_in, bias, cot, row_scale, tabs, firstq, dims):
    R, D, feats, dp, reach = dims
    plane, pf, F, T = 2 * R, 2 * feats, 2 * dp, lax.axis_size("tp")
    aw = 4 * HDIM
    hu = w_fc.shape[3] // 2
    gw = hu * NB
    pw = D // T
    sds = jax.ShapeDtypeStruct
    vm = pltpu.VMEM
    dma = pltpu.SemaphoreType.DMA
    reg = pltpu.SemaphoreType.REGULAR
    return pl.pallas_call(
        functools.partial(block_kernel, dims),
        out_shape=[sds((D, aw), BF16)] + [sds((D, 2 * hu), BF16)] * NB
        + [sds((R, pw), BF16), sds((R, pw), BF16), sds((8, feats), F32), sds((F, 8, gw), F32)]
        + [sds((3, feats, 2 * HDIM), BF16), sds((2 * HDIM, feats), BF16)]
        + [sds((feats, 2 * gw), BF16), sds((2 * gw, feats), BF16)],
        in_specs=[ANY] * 4 + [VMEM] * 4 + [ANY] + [VMEM] * 3,
        out_specs=[ANY] * GROUPS + [VMEM] * 4 + [ANY] * 4,
        scratch_shapes=[
            vm((plane, D), BF16), vm((plane, D), BF16), vm((D, max(aw, gw)), BF16),
            vm((4 * (reach + 1), plane, HDIM), BF16), vm((8, (reach + 1) * plane), F32),
            vm((plane, gw), BF16), vm((plane, gw), BF16), vm((plane, 3 * HDIM), BF16), vm((plane, HDIM), BF16),
            vm((2, 2, plane, HDIM), BF16), vm((2, plane, HDIM), BF16), vm((2, R, HDIM), BF16),
            vm((2, dp + 1, pf, 2 * HDIM), BF16), vm((NB, dp + 1, pf, 2 * hu), BF16),
            vm((plane, 2), F32),
            vm((2, HDIM, feats), BF16), vm((NB, 2, hu, feats), BF16),
            vm((8, D), F32), vm((8, gw), F32), vm((F, 8, feats), F32), vm((F, 8, feats), F32),
            vm((T, 8, R), F32), vm((T, 8, feats), F32),
            dma((GROUPS + 2,)), dma((4, 4)), dma((2, GROUPS)), dma((GROUPS, dp, 2, 2)), dma((GROUPS, F)),
            dma((2, 2, reach + 1)), dma((2, 2, reach + 1)), dma((2, reach + 1)), dma((2 + NB, dp, 2)), dma((2 + NB, dp + 1)), dma((2 + NB, 2, 3)),
            dma((NB + 2,)), dma((4, 2, F)), dma((2, 2, 7)), reg, reg, reg,
        ],
        compiler_params=pltpu.CompilerParams(
            collective_id=4, has_side_effects=True, vmem_limit_bytes=63 << 20
        ),
        name="block",
    )(tok, gh, w_att, w_fc, vecs, bq, b_in, bias, cot, row_scale, tabs, firstq)


def on_device(
    tokens,
    qkv_weight,
    qkv_bias,
    dense_weight,
    dense_bias,
    fc_in_weight,
    fc_in_bias,
    fc_out_weight,
    fc_out_bias,
    norm1_gain,
    norm1_shift,
    norm2_gain,
    norm2_shift,
    cotangent,
    subset_ids,
    seq_starts,
):
    rows, width = tokens.shape
    shards = lax.axis_size("fsdp")
    tps = lax.axis_size("tp")
    dp = shards // 2
    f = lax.axis_index("fsdp")
    t = lax.axis_index("tp")
    i = lax.rem(f, 2)
    d = f // 2
    total = rows * shards
    scale = 1.0 / math.sqrt(HDIM)
    feats = qkv_weight.shape[0]
    units = fc_in_weight.shape[1]
    head_cols = qkv_weight.shape[2]
    heads_here = head_cols // HDIM
    hd = qkv_bias.shape[2]
    ub = fc_in_bias.shape

    match = subset_ids[:, None] == jnp.arange(SUBSETS, dtype=jnp.int32)[None, :]
    counts = jnp.sum(match.astype(F32), axis=0)
    vecs = [norm1_gain, norm1_shift, norm2_gain, norm2_shift, dense_bias, fc_out_bias]
    pack = jnp.concatenate(
        [v.astype(F32) for v in vecs]
        + [qkv_bias.astype(F32).reshape(-1), fc_in_bias.astype(F32).reshape(-1), counts]
    )
    size = pack.shape[0]
    lanes = -(-size // 1024) * 128
    got = exchange(jnp.pad(pack, (0, 8 * lanes - size)).reshape(8, lanes), "fsdp", False, 1)
    got = got.reshape(shards, 8 * lanes)
    gain1, shift1, gain2, shift2, b_dense, b_out = [
        got[:, k * feats : (k + 1) * feats].reshape(width) for k in range(6)
    ]
    at = 6 * feats
    nq = 3 * heads_here * hd
    b_qkv = got[:, at : at + nq].reshape(shards, 3, heads_here, hd)
    b_qkv = b_qkv.transpose(1, 2, 0, 3).reshape(3, heads_here, HDIM)
    b_qkv = lax.dynamic_index_in_dim(b_qkv, i, 1, keepdims=False).reshape(3 * HDIM)
    at += nq
    b_in = got[:, at : at + units // shards].reshape(shards, ub[0], ub[1])
    b_in = half_of(b_in.transpose(1, 0, 2).reshape(units), i, 0)
    at += units // shards
    counts = jnp.sum(got[:, at : at + SUBSETS], axis=0)
    table = total / (SUBSETS * counts)
    row_scale = jnp.sum(jnp.where(match, table[None, :], 0.0), axis=1)
    carried = cotangent.astype(F32) * row_scale[:, None]
    grad_here = carried.astype(BF16)

    hu = units // 2 // NB
    w_att = jnp.concatenate(
        [
            qkv_weight.reshape(feats, 3, heads_here, HDIM).transpose(2, 0, 1, 3).reshape(2, feats, 3 * HDIM),
            dense_weight.reshape(heads_here, HDIM, feats).transpose(0, 2, 1),
        ],
        axis=2,
    )
    w_fc = jnp.concatenate(
        [
            fc_in_weight.reshape(feats, 2, NB, hu).transpose(2, 1, 0, 3),
            fc_out_weight.reshape(2, NB, hu, feats).transpose(1, 0, 3, 2),
        ],
        axis=3,
    )
    plane = 2 * rows
    start_row = d * plane
    reach = min(dp - 1, -(-(SEQ_LEN - 1) // plane))
    here = start_row + jnp.arange(plane, dtype=jnp.int32)
    docs_here, pos_here = locate(here, seq_starts)
    later = start_row + jnp.arange((reach + 1) * plane, dtype=jnp.int32)
    _, pos_later = locate(later, seq_starts)
    first_later = later - pos_later.astype(jnp.int32) - start_row
    first_later = jnp.where(later < total, first_later, 1 << 30)[None, :]
    cosine, sine = rotary_tables(pos_here)
    ones = jnp.ones((plane, 128 - ROT), F32)
    none = jnp.zeros((plane, 128 - ROT), F32)
    tabs = jnp.stack(
        [
            jnp.concatenate([cosine, cosine, ones], 1),
            jnp.concatenate([-sine, sine, none], 1),
        ]
    )
    vecs = jnp.stack([gain1, shift1, gain2, shift2] + [jnp.zeros_like(gain1)] * 4)
    dims = (rows, width, feats, dp, reach)
    part_w = width // tps
    offset = t * part_w
    cut = lambda vec: lax.dynamic_slice_in_dim(vec, offset, part_w, vec.ndim - 1)
    bias = (cut(b_dense) + cut(b_out)).reshape(1, -1)
    cot_here = cut(cotangent).reshape(rows, 2, part_w // 2).transpose(1, 0, 2)
    mixed, tokens_grad, norm_grads, bias_sums, g_qkv, g_dense, g_in, g_out = block(
        tokens, grad_here, w_att, w_fc, vecs, b_qkv.reshape(1, -1), b_in.reshape(1, -1), bias, cot_here, row_scale[None, :], tabs,
        first_later, dims,
    )[GROUPS:]
    qkv_weight_grad = g_qkv.transpose(1, 0, 2).astype(F32)
    dense_weight_grad = g_dense.astype(F32)
    fc_in_weight_grad = g_in.astype(F32)
    fc_out_weight_grad = g_out.astype(F32)
    bias_grad = norm_grads[4]

    bias_sums = jnp.sum(bias_sums.reshape(dp, 2, 8, units // 2), axis=0)
    in_bias_grad = bias_sums[:, 0].reshape(ub[0], shards * ub[1])
    in_bias_grad = lax.dynamic_slice_in_dim(in_bias_grad, f * ub[1], ub[1], 1)
    qkv_bias_grad = bias_sums[:, 1, : 3 * HDIM].reshape(2, 3, HDIM).transpose(1, 0, 2)
    qkv_bias_grad = lax.dynamic_slice_in_dim(qkv_bias_grad, f * hd, hd, 2)
    return (
        mixed,
        tokens_grad,
        qkv_weight_grad,
        qkv_bias_grad,
        dense_weight_grad,
        bias_grad,
        fc_in_weight_grad,
        in_bias_grad,
        fc_out_weight_grad,
        bias_grad,
        norm_grads[0],
        norm_grads[1],
        norm_grads[2],
        norm_grads[3],
    )


def solution(mesh):
    in_specs = (
        P("fsdp", None),
        P("fsdp", None, "tp"),
        P(None, "tp", "fsdp"),
        P("tp", "fsdp"),
        P("fsdp"),
        P("fsdp", "tp"),
        P("tp", "fsdp"),
        P("tp", "fsdp"),
        P("fsdp"),
        P("fsdp"),
        P("fsdp"),
        P("fsdp"),
        P("fsdp"),
        P("fsdp", None),
        P("fsdp"),
        P(),
    )
    out_specs = (
        P("fsdp", "tp"),
        P("fsdp", "tp"),
        P("fsdp", None, "tp"),
        P(None, "tp", "fsdp"),
        P("tp", "fsdp"),
        P("fsdp"),
        P("fsdp", "tp"),
        P("tp", "fsdp"),
        P("tp", "fsdp"),
        P("fsdp"),
        P("fsdp"),
        P("fsdp"),
        P("fsdp"),
        P("fsdp"),
    )
    return jax.shard_map(
        on_device, mesh=mesh, in_specs=in_specs, out_specs=out_specs, check_vma=False
    )
```

```python
import functools
import math

import jax
import jax.numpy as jnp
from jax import lax
from jax.experimental import pallas as pl
from jax.experimental.pallas import tpu as pltpu
from jax.sharding import PartitionSpec as P

HDIM = 256
ROT = 64
SUBSETS = 22
SEQ_LEN = 2048
EPS = 1e-05
F32 = jnp.float32
BF16 = jnp.bfloat16
MESH = pl.DeviceIdType.MESH
ANY = pl.BlockSpec(memory_space=pl.ANY)
VMEM = pl.BlockSpec(memory_space=pltpu.VMEM)


def mm(left, right, dims):
    return lax.dot_general(left, right, (dims, ((), ())), preferred_element_type=F32)


def plain(left, right):
    return mm(left, right, ((1,), (0,)))


def inner(left, right):
    return mm(left, right, ((0,), (0,)))


def against(left, right):
    return mm(left, right, ((1,), (1,)))


def rotary_tables(positions):
    half = ROT // 2
    steps = jnp.arange(half, dtype=F32)
    freq = 1.0 / 10000.0 ** (steps * 2.0 / ROT)
    angle = positions[:, None] * freq[None, :]
    return jnp.cos(angle), jnp.sin(angle)


def locate(indices, starts):
    above = indices[:, None] >= starts[None, :]
    doc_ids = jnp.sum(above.astype(jnp.int32), axis=1) - 1
    pick = doc_ids[:, None] == jnp.arange(starts.shape[0], dtype=jnp.int32)[None, :]
    first = jnp.sum(jnp.where(pick, starts[None, :], 0), axis=1)
    return (doc_ids, (indices - first).astype(F32))


def half_of(value, which, axis):
    size = value.shape[axis] // 2
    return lax.dynamic_slice_in_dim(value, which * size, size, axis)


def exchange_kernel(axis, spread, v_ref, o_ref, ssem, rsem):
    count = o_ref.shape[0]
    me = lax.axis_index(axis)

    def peer(step):
        return lax.rem(me + step, count)

    barrier = pltpu.get_barrier_semaphore()
    for step in range(1, count):
        pl.semaphore_signal(barrier, 1, device_id={axis: peer(step)}, device_id_type=MESH)
    pl.semaphore_wait(barrier, count - 1)

    def copy(step):
        return pltpu.make_async_remote_copy(
            src_ref=v_ref.at[peer(step)] if spread else v_ref,
            dst_ref=o_ref.at[me],
            send_sem=ssem.at[step],
            recv_sem=rsem.at[step],
            device_id={axis: peer(step)},
            device_id_type=MESH,
        )

    for step in range(1, count):
        copy(step).start()
    o_ref[me] = v_ref[me] if spread else v_ref[...]
    for step in range(1, count):
        copy(step).wait()


def exchange(value, axis, spread, cid):
    count = lax.axis_size(axis)
    block = value.shape[1:] if spread else value.shape
    return pl.pallas_call(
        functools.partial(exchange_kernel, axis, spread),
        out_shape=jax.ShapeDtypeStruct((count,) + block, value.dtype),
        in_specs=[VMEM],
        out_specs=VMEM,
        scratch_shapes=[pltpu.SemaphoreType.DMA((count,)), pltpu.SemaphoreType.DMA((count,))],
        compiler_params=pltpu.CompilerParams(collective_id=cid, has_side_effects=True),
        name="exchange",
    )(value)


NB = 4
GROUPS = 1 + NB
ORDER = (
    "pair0", "pair2", "own4i", "own0o", "pair1", "rx0", "own0i", "own1o", "mate0i", "mate0o", "arr01",
    "pair3", "mate1o", "rc0", "pair4", "mate2i", "arr02", "rx1", "own1i", "mate1i", "arr11", "own3i",
    "mate4i", "mate3i", "own2i", "stats", "rc1", "arr03", "arr12", "proj", "datt", "kv1k", "arr13", "ffn0",
    "st13i", "kv1v", "st12o", "own3o", "qd1", "st12i", "kv2k", "mate3o", "own2o", "st11i", "kv2v", "att0",
    "att1", "att2", "att3", "mate2o", "ls0", "sta3i", "arr21", "sta2i", "qd2", "ls1", "dkv0", "sta2o",
    "arr22", "arr31", "sta1i", "own4o", "dkv1", "dkv2", "dkv3", "mate4o", "stb3i", "arr23", "ffn1", "st23i",
    "stb2o", "arr32", "arr41", "st22o", "st22i", "arr33", "stb2i", "ffn2", "arr42", "st21i", "arr43", "st33i",
    "ffn3", "out", "st11o", "stb1o", "st43i", "st32o", "hid", "far00", "st42o", "st21o", "st32i", "far01",
    "qk", "mt0", "st42i", "sta1o", "fin2", "stb1i", "fina", "far10", "far11", "st31o", "st41o", "st41i",
    "fin1", "small", "mt1", "st31i", "last0", "fin4", "finb", "last1", "fin3",
)


def turn(u, tabs, at, sign):
    lo, hi = u[:, :128], u[:, 128:]
    lane = lax.broadcasted_iota(jnp.int32, lo.shape, 1)
    other = jnp.where(lane < ROT // 2, pltpu.roll(lo, 128 - ROT // 2, 1), pltpu.roll(lo, ROT // 2, 1))
    a = other * tabs[1, at, :]
    lo = lo * tabs[0, at, :] + (a if sign > 0 else -a)
    return jnp.concatenate([lo, hi], axis=1)


def block_kernel(
    dims,
    tok, gh, w_att, w_fc, vecs, bq, bin_, bias, cot, row_scale, tabs, firstq,
    *refs,
):
    outs, refs = refs[:GROUPS], refs[GROUPS:]
    (
        mixed_o, dtok_o, norm_o, bias_o, dq_o, dd_o, di_o, do_o, xs, gs, wbuf, wins, st,
        act, dpre, dqkv, att, tpr0, tpr1, tpr2, rs_a, rs_f, norms, tra, trf, sums, bsum, sum_s, sum_r, row_r, nrm_r,
        lsem, tsem, psem, zsem, zrec, ksem, qsem, lssem, ssem, rsem, fsem, bsem, xsem, usem, near_ok, far_ok, mate_ok,
    ) = refs
    R, D, feats, dp, reach = dims
    F, T = 2 * dp, row_r.shape[0]
    f = lax.axis_index("fsdp")
    t = lax.axis_index("tp")
    d, i = f // 2, lax.rem(f, 2)
    core = lax.rem(t, 2)
    plane, pf = 2 * R, 2 * feats
    qb = min(256, plane)
    nb = plane // qb
    fb = min(256, pf)
    aw = 4 * HDIM
    gw = act.shape[1]
    hu = gw // NB
    pw = D // T
    slots = reach + 1
    tn, tf = t + 1 - 2 * core, lax.rem(t + 2, T)
    mate, near, far = (f + 1 - 2 * i, t), (f, tn), (f, tf)
    has = (d + 1 < dp, d >= 1)
    inward = jnp.where(d < dp // 2, 0, 1)
    ways = {"i": inward, "o": 1 - inward}
    scale = 1.0 / math.sqrt(HDIM)

    barrier = pltpu.get_barrier_semaphore()
    for s in range(1, F):
        pl.semaphore_signal(barrier, 1, device_id=(lax.rem(f + s, F), t), device_id_type=MESH)
    for s in range(1, T):
        pl.semaphore_signal(barrier, 1, device_id=(f, lax.rem(t + s, T)), device_id_type=MESH)
    pl.semaphore_wait(barrier, F + T - 2)

    def rc(src, dst, ss, rv, who):
        return pltpu.make_async_remote_copy(
            src_ref=src, dst_ref=dst, send_sem=ss, recv_sem=rv, device_id=who, device_id_type=MESH
        )

    def rows(b):
        return pl.ds(pl.multiple_of(b * qb, qb), qb)

    def toward(way):
        return (f + 2 - 4 * way, t)

    def open_way(way):
        return jnp.where(way == 0, d + 1 < dp, d >= 1)

    def slot(g, s):
        return outs[g].at[pl.ds(s * feats, feats), :]

    def part(half, g):
        return w_att.at[half] if g == 0 else w_fc.at[g - 1, half]

    def pair_copy(g):
        return rc(part(1 - i, g), slot(g, f), psem.at[0, g], psem.at[1, g], mate)

    def mine_copy(g):
        return pltpu.make_async_copy(part(i, g), slot(g, f), lsem.at[g])

    def z_own(g, way):
        return rc(part(i, g), slot(g, f), zsem.at[g, 0, way, 0], zrec.at[g, f], toward(way))

    def z_mate(g, way):
        s = f + 1 - 2 * i
        return rc(slot(g, s), slot(g, s), zsem.at[g, 0, way, 1], zrec.at[g, s], toward(way))

    def z_fwd(g, k, way, j):
        s = (d - k) * 2 + j if way == 0 else (d + k) * 2 + j
        return rc(slot(g, s), slot(g, s), zsem.at[g, k, way, j], zrec.at[g, s], toward(way))

    def send_own(g, io):
        @pl.when(open_way(ways[io]))
        def _():
            z_own(g, ways[io]).start()

    def send_mate(g, io, wait):
        if wait:
            pair_copy(g).wait_recv()

        @pl.when(open_way(ways[io]))
        def _():
            z_mate(g, ways[io]).start()

    def from_dist(k, way):
        return d >= k if way == 0 else d + k < dp

    def arrive(g, k):
        for way in range(2):
            @pl.when(from_dist(k, way))
            def _():
                for j in range(2):
                    z_fwd(g, k, way, j).wait_recv()

                    @pl.when(has[way])
                    def _():
                        z_fwd(g, k, way, j).start()

    def gather_sent(g):
        pair_copy(g).wait_send()
        for way in range(2):
            @pl.when(has[way])
            def _():
                z_own(g, way).wait_send()
                z_mate(g, way).wait_send()
            for k in range(1, dp - 1):
                @pl.when(from_dist(k, way) & has[way])
                def _():
                    for j in range(2):
                        z_fwd(g, k, way, j).wait_send()

    def load(*pairs):
        copies = [pltpu.make_async_copy(src, dst, bsem.at[n]) for n, (src, dst) in enumerate(pairs)]
        for c in copies:
            c.start()
        for c in copies:
            c.wait()

    hr = R // 2
    given = ((tok, xs), (gh, gs))

    def rows_x(a):
        ref, out = given[a]
        return rc(
            ref.at[pl.ds(core * hr, hr), :], out.at[pl.ds(i * R + core * hr, hr), :],
            tsem.at[a, 0], tsem.at[a, 1], mate,
        )

    def rows_c(a):
        at = given[a][1].at[pl.ds((1 - i) * R + core * hr, hr), :]
        return rc(at, at, tsem.at[a, 2], tsem.at[a, 3], near)

    def rows_own(a):
        ref, out = given[a]
        return pltpu.make_async_copy(ref, out.at[pl.ds(i * R, R), :], lsem.at[GROUPS + a])

    def rows_on(a):
        rows_x(a).wait_recv()
        rows_c(a).start()

    def rows_done(a):
        rows_c(a).wait_recv()
        rows_own(a).wait()

    def hat(at):
        return (xs[at, :].astype(F32) - norms[at, 0:1]) * norms[at, 1:2]

    def stats():
        def block(b, _):
            x = xs[rows(b), :].astype(F32)
            m = jnp.mean(x, axis=-1, keepdims=True)
            c = x - m
            norms[rows(b), 0:1] = m
            norms[rows(b), 1:2] = lax.rsqrt(jnp.mean(c * c, axis=-1, keepdims=True) + EPS)
            return 0

        rows_done(0)
        lax.fori_loop(0, nb, block, 0)

    def proj():
        def block(b, _):
            at = rows(b)
            h1 = (hat(at) * vecs[0:1, :] + vecs[1:2, :]).astype(BF16)
            y = plain(h1, wbuf[:, : 3 * HDIM]) + bq[...]
            wins[2 * slots, at, :] = (turn(y[:, :HDIM], tabs, at, 1).astype(BF16).astype(F32) * scale).astype(BF16)
            wins[reach, at, :] = turn(y[:, HDIM : 2 * HDIM], tabs, at, 1).astype(BF16)
            wins[slots + reach, at, :] = y[:, 2 * HDIM :].astype(BF16)
            return 0

        mine_copy(0).wait()
        load((outs[0], wbuf))
        lax.fori_loop(0, nb, block, 0)

        @pl.when(has[0])
        def _():
            kv_copy(0, 0).start()
            kv_copy(1, 0).start()

    def datt():
        def block(b, _):
            at = rows(b)
            wins[3 * slots, at, :] = plain(gs[at, :], wbuf[:, 3 * HDIM :]).astype(BF16)
            return 0

        rows_done(1)
        lax.fori_loop(0, nb, block, 0)

        @pl.when(has[1])
        def _():
            qd_copy(0, 0).start()
            qd_copy(1, 0).start()

    def ffn(h):
        mine = slice(h * hu, (h + 1) * hu)

        def block(b, _):
            at = rows(b)
            h2 = (hat(at) * vecs[2:3, :] + vecs[3:4, :]).astype(BF16)
            pre = plain(h2, wbuf[:, :hu]) + bin_[:, mine]
            cdf = 0.5 * (1.0 + lax.erf(pre * (1.0 / math.sqrt(2.0))))
            act[at, mine] = (pre * cdf).astype(BF16)
            slope = cdf + pre * jnp.exp(-0.5 * pre * pre) * (1.0 / math.sqrt(2.0 * math.pi))
            dp_b = (plain(gs[at, :], wbuf[:, hu : 2 * hu]) * slope).astype(BF16)
            dpre[at, mine] = dp_b
            bsum[0:1, mine] += jnp.sum(dp_b.astype(F32), axis=0, keepdims=True)
            return 0

        mine_copy(1 + h).wait()
        load((outs[1 + h], wbuf.at[:, pl.ds(0, 2 * hu)]))
        lax.fori_loop(0, nb, block, 0)

    def kv_copy(h, k):
        w = wins.at[h * slots + reach - k]
        return rc(w, wins.at[h * slots + reach - k - 1], ksem.at[h, 0, k], ksem.at[h, 1, k + 1], toward(0))

    def kv_recv(h, k):
        w = wins.at[h * slots + reach - k]
        return rc(w, w, ksem.at[h, 0, k - 1], ksem.at[h, 1, k], toward(0))

    def kv_step(h, k):
        @pl.when(d >= k)
        def _():
            kv_recv(h, k).wait_recv()
            if k < reach:
                @pl.when(has[0])
                def _():
                    kv_copy(h, k).start()

        @pl.when(d < k)
        def _():
            wins[h * slots + reach - k] = jnp.zeros((plane, HDIM), BF16)

    def qd_copy(h, k):
        w = wins.at[(2 + h) * slots + k]
        return rc(w, wins.at[(2 + h) * slots + k + 1], qsem.at[h, 0, k], qsem.at[h, 1, k + 1], toward(1))

    def qd_recv(h, k):
        w = wins.at[(2 + h) * slots + k]
        return rc(w, w, qsem.at[h, 0, k - 1], qsem.at[h, 1, k], toward(1))

    def qd_step(k):
        @pl.when(d + k < dp)
        def _():
            for h in range(2):
                qd_recv(h, k).wait_recv()
                if k < reach:
                    @pl.when(has[1])
                    def _():
                        qd_copy(h, k).start()

        @pl.when(d + k >= dp)
        def _():
            for h in range(2):
                wins[(2 + h) * slots + k] = jnp.zeros((plane, HDIM), BF16)

    def stat_at(k):
        return st.at[:, pl.ds(k * plane, plane)]

    def stat_copy(k):
        return rc(stat_at(0), stat_at(k), lssem.at[0, k], lssem.at[1, k], (f - 2 * k, t))

    def stat_send():
        for k in range(1, reach + 1):
            @pl.when(d >= k)
            def _():
                stat_copy(k).start()

    def stat_wait():
        for k in range(1, reach + 1):
            @pl.when(d + k < dp)
            def _():
                stat_copy(k).wait_recv()

            @pl.when(d + k >= dp)
            def _():
                st[:, k * plane : (k + 1) * plane] = jnp.zeros((8, plane), F32)

    span = SEQ_LEN + qb
    base = reach * plane - SEQ_LEN
    parts = 4

    def wide(n, start):
        flat = wins.reshape(wins.shape[0] * plane, HDIM)
        return flat[pl.ds(pl.multiple_of(n * slots * plane + start, qb), span), :]

    def attention(n):
        def block(b, _):
            at = rows(b)
            keys_at = base + b * qb
            keys = wide(0, keys_at)
            vals = wide(1, keys_at)
            s = against(wins[2 * slots, at, :], keys)
            c = base + b * qb + lax.broadcasted_iota(jnp.int32, (qb, span), 1)
            r = reach * plane + b * qb + lax.broadcasted_iota(jnp.int32, (qb, span), 0)
            low = jnp.broadcast_to(firstq[:, at].astype(F32), (128, qb)).T[:, 0:1] + float(reach * plane)
            s = jnp.where((c.astype(F32) >= low) & (c <= r), s, -1e30)
            top = jnp.max(s, axis=1, keepdims=True)
            e = jnp.exp(s - top)
            total = jnp.sum(e, axis=1, keepdims=True)
            p = e * (1.0 / total)
            att[at, :] = plain(p.astype(BF16), vals).astype(BF16)
            dpr = against(wins[3 * slots, at, :], vals)
            delta = jnp.sum(p * dpr, axis=1, keepdims=True)
            ds = (p * (dpr - delta)).astype(BF16)
            dq = plain(ds, keys) * scale
            dqkv[at, :HDIM] = turn(dq, tabs, at, -1).astype(BF16)
            lane = lax.broadcasted_iota(jnp.int32, (qb, 128), 1)
            both = jnp.where(lane == 0, top + jnp.log(total), jnp.where(lane == 1, delta, 0.0))
            st[:, at] = both.T[:8]
            return 0

        lax.fori_loop(n * nb // parts, (n + 1) * nb // parts, block, 0)

    def key_grads(n):
        def block(b, _):
            at = rows(b)
            rows_at = pl.ds(pl.multiple_of(b * qb, qb), span)
            q = wide(2, b * qb)
            da = wide(3, b * qb)
            s = against(wins[reach, at, :], q)
            c = b * qb + lax.broadcasted_iota(jnp.int32, (qb, span), 0)
            r = b * qb + lax.broadcasted_iota(jnp.int32, (qb, span), 1)
            s = jnp.where((c >= firstq[:, rows_at]) & (c <= r), s - st[0:1, rows_at], -1e30)
            p = jnp.exp(s)
            dqkv[at, 2 * HDIM :] = plain(p.astype(BF16), da).astype(BF16)
            dpr = against(wins[slots + reach, at, :], da)
            ds = (p * (dpr - st[1:2, rows_at])).astype(BF16)
            dqkv[at, HDIM : 2 * HDIM] = turn(plain(ds, q), tabs, at, -1).astype(BF16)
            return 0

        lax.fori_loop(n * nb // parts, (n + 1) * nb // parts, block, 0)

    def rs(g):
        return rs_a.at[g] if g < 2 else rs_f.at[g - 2]

    def grad_part(g, p, c):
        cols = pl.ds(pl.multiple_of(p * pf + c * fb, fb), fb)
        z = (xs[:, cols].astype(F32) - norms[:, 0:1]) * norms[:, 1:2]
        n = 0 if g < 2 else 2
        h = (z * vecs[n : n + 1, cols] + vecs[n + 1 : n + 2, cols]).astype(BF16)
        if g == 0:
            return inner(h, dqkv[:, :HDIM]), inner(gs[:, cols], att[...])
        if g == 1:
            return (inner(h, dqkv[:, HDIM:]),)
        mine = slice((g - 2) * hu, (g - 1) * hu)
        return inner(h, dpre[:, mine]), inner(gs[:, cols], act[:, mine])

    def add_part(g, p, second=None):
        def block(c, _):
            at = pl.ds(pl.multiple_of(c * fb, fb), fb)
            left = 0
            for v in grad_part(g, p, c):
                cols = slice(left, left + v.shape[1])
                left += v.shape[1]
                v = rs(g)[p, at, cols].astype(F32) + v
                if second is not None:
                    v = v + rs(g)[second, at, cols].astype(F32)
                rs(g)[p, at, cols] = v.astype(BF16)
            return 0

        lax.fori_loop(0, pf // fb, block, 0)

    def rs_copy(g, k, way):
        p = d + k * (1 - 2 * way)
        to = jnp.where((way == 1) & (k == 1), dp, p)
        return rc(rs(g).at[p], rs(g).at[to], ssem.at[g, k, way], rsem.at[g, to], toward(way))

    def rs_wait(g, p):
        return rc(rs(g).at[p], rs(g).at[p], ssem.at[g, 0, 0], rsem.at[g, p], mate)

    def clear(g, p):
        rs(g)[p] = jnp.zeros(rs(g).shape[1:], BF16)

    def stage(g, k, io):
        way = ways[io]
        p = d + k * (1 - 2 * way)
        came = open_way(1 - way)

        @pl.when((p >= 0) & (p < dp))
        def _():
            @pl.when(came)
            def _():
                rs_wait(g, p).wait_recv()

            @pl.when(jnp.logical_not(came))
            def _():
                clear(g, p)

            add_part(g, p)
            rs_copy(g, k, way).start()

    def final_copies(g):
        lo = pl.multiple_of(i * HDIM, HDIM)
        pieces = []
        for j in range(2):
            at = pl.ds((i if j == 0 else 1 - i) * feats, feats)
            src = rs(g).at[d, at]
            if g == 0:
                dst = (dq_o.at[0, :, pl.ds(lo, HDIM)], dd_o.at[pl.ds(lo, HDIM), :])
                src = (src.at[:, pl.ds(0, HDIM)], tra.at[j])
            elif g == 1:
                dst = tuple(dq_o.at[n, :, pl.ds(lo, HDIM)] for n in (1, 2))
                src = tuple(src.at[:, pl.ds(n * HDIM, HDIM)] for n in (0, 1))
            else:
                u = pl.multiple_of(i * gw + (g - 2) * hu, hu)
                dst = (di_o.at[:, pl.ds(u, hu)], do_o.at[pl.ds(u, hu), :])
                src = (src.at[:, pl.ds(0, hu)], trf.at[g - 2, j])
            for n in range(2):
                if j == 0:
                    pieces.append(pltpu.make_async_copy(src[n], dst[n], fsem.at[g, n, 0]))
                else:
                    pieces.append(rc(src[n], dst[n], fsem.at[g, n, 1], fsem.at[g, n, 2], mate))
        return pieces

    def final(g):
        for p, came in ((d, has[1]), (dp, has[0])):
            @pl.when(came)
            def _():
                rs_wait(g, p).wait_recv()

            @pl.when(jnp.logical_not(came))
            def _():
                clear(g, p)

        add_part(g, d, dp)
        if g != 1:
            cut = HDIM if g == 0 else hu
            for j in range(2):
                at = pl.ds(pl.multiple_of((i if j == 0 else 1 - i) * feats, feats), feats)
                turned = rs(g)[d, at, cut:].astype(F32).T.astype(BF16)
                if g == 0:
                    tra[j] = turned
                else:
                    trf[g - 2, j] = turned
        for c in final_copies(g):
            c.start()

    def out_step(up):
        def dense(b, _):
            at = rows(b)
            for c in range(T):
                y = against(att[at, :], wbuf[c * pw : (c + 1) * pw, :HDIM])
                for e in range(2):
                    v = up[2 * c + e, at, :].astype(F32) + y[:, e * HDIM : (e + 1) * HDIM]
                    up[2 * c + e, at, :] = v.astype(BF16)
            return 0

        def block(b, _):
            at = rows(b)
            sums[4:5, :] += jnp.sum(gs[at, :].astype(F32), axis=0, keepdims=True)
            for c in range(T):
                cols = slice(c * pw, (c + 1) * pw)
                y = against(act[at, :], wbuf[cols, :])
                for e in range(2):
                    up[2 * c + e, at, :] = y[:, e * HDIM : (e + 1) * HDIM].astype(BF16)
            return 0

        load(
            *[(outs[1 + h].at[:, pl.ds(hu, hu)], wbuf.at[:, pl.ds(h * hu, hu)]) for h in range(NB)],
        )
        lax.fori_loop(0, nb, block, 0)
        load((outs[0].at[:, pl.ds(3 * HDIM, HDIM)], wbuf.at[:, pl.ds(0, HDIM)]))
        lax.fori_loop(0, nb, dense, 0)
        tp_near(up, False)

    def hidden_step():
        def block(b, _):
            at = rows(b)
            e2 = against(dpre[at, :], wbuf[...])
            z = hat(at)
            sums[2:3, :] += jnp.sum(e2 * z, axis=0, keepdims=True)
            sums[3:4, :] += jnp.sum(e2, axis=0, keepdims=True)
            u = (e2 * vecs[2:3, :]).astype(BF16)
            for c in range(2 * T):
                wins[c, at, :] = u[:, c * HDIM : (c + 1) * HDIM]
            return 0

        for k in range(reach):
            for h in range(2):
                @pl.when((d >= k) & has[0])
                def _():
                    kv_copy(h, k).wait_send()

                @pl.when((d + k < dp) & has[1])
                def _():
                    qd_copy(h, k).wait_send()

        pl.semaphore_signal(far_ok, 1, device_id=far, device_id_type=MESH)
        pl.semaphore_signal(mate_ok, 1, device_id=mate, device_id_type=MESH)
        load(
            *[(outs[1 + h].at[:, pl.ds(0, hu)], wbuf.at[:, pl.ds(h * hu, hu)]) for h in range(NB)],
        )
        lax.fori_loop(0, nb, block, 0)

    def qkv_step():
        def block(b, _):
            at = rows(b)
            e1 = against(dqkv[at, :], wbuf[:, : 3 * HDIM])
            z = hat(at)
            sums[0:1, :] += jnp.sum(e1 * z, axis=0, keepdims=True)
            sums[1:2, :] += jnp.sum(e1, axis=0, keepdims=True)
            bsum[1:2, : 3 * HDIM] += jnp.sum(dqkv[at, :].astype(F32), axis=0, keepdims=True)
            u = e1 * vecs[0:1, :]
            for c in range(2 * T):
                wins[c, at, :] = (wins[c, at, :].astype(F32) + u[:, c * HDIM : (c + 1) * HDIM]).astype(BF16)
            return 0

        load((outs[0], wbuf))
        lax.fori_loop(0, nb, block, 0)
        tp_near(wins, True)
        for s in range(F):
            sum_s[s] = sums[:, s * feats : (s + 1) * feats]
        for s in range(1, F):
            sum_copy(s).start()
            bias_copy(s).start()
        sum_r[f] = sum_s[f]
        bias_o[f] = bsum[...]

    def half(h):
        return pl.ds(pl.multiple_of((1 - i if h == 0 else i) * R, R), R)

    def half_block(h, b):
        return pl.ds(pl.multiple_of((1 - i if h == 0 else i) * R + b * qb, qb), qb)

    def near_copy(up, second, h, j):
        blk = tn if j == 0 else lax.rem(tn + 2, T)
        n = 2 * h + j
        src = up.at[pl.ds(2 * blk, 2), half(h), :]
        return rc(src, tpr0.at[j, :, half(h), :], usem.at[int(second), 0, n], usem.at[int(second), 1, n], near)

    def landing(second):
        return (wins.at[pl.ds(2 * T, 2)], wins.at[pl.ds(2 * T + 2, 2), pl.ds(0, R), :]) if second else (tpr1, tpr2)

    def far_copy(up, h, second):
        src, dst = up.at[pl.ds(2 * tf, 2), half(h), :], landing(second)[0].at[:, half(h), :]
        return rc(src, dst, usem.at[int(second), 0, 4 + h], usem.at[int(second), 1, 4 + h], far)

    def mate_copy(up, second):
        n = int(second)
        src = up.at[pl.ds(2 * t, 2), half(0), :]
        return rc(src, landing(second)[1], usem.at[n, 0, 6], usem.at[n, 1, 6], mate)

    def tp_near(up, second):
        if second:
            pl.semaphore_wait(near_ok, 1)
        for h in range(2):
            for j in (1, 0):
                near_copy(up, second, h, j).start()

    def tp_far(up, second, h):
        def block(b, _):
            at = half_block(h, b)
            for blk, j in ((tf, 1), (t, 0)):
                for e in range(2):
                    v = up[2 * blk + e, at, :].astype(F32) + tpr0[j, e, at, :].astype(F32)
                    up[2 * blk + e, at, :] = v.astype(BF16)
            return 0

        near_copy(up, second, h, 1).wait_recv()
        near_copy(up, second, h, 0).wait_recv()
        lax.fori_loop(0, R // qb, block, 0)
        far_steps.append((second, h))
        if second and (True, 1 - h) not in far_steps:
            pl.semaphore_wait(far_ok, 1)
        if not second and (False, 1 - h) in far_steps:
            pl.semaphore_signal(near_ok, 1, device_id=near, device_id_type=MESH)
        far_copy(up, h, second).start()

    def came_far(second, e, at):
        return (wins[2 * T + e, at, :] if second else tpr1[e, at, :]).astype(F32)

    def tp_mate(up, second):
        def block(b, _):
            at = half_block(0, b)
            for e in range(2):
                v = up[2 * t + e, at, :].astype(F32) + came_far(second, e, at)
                up[2 * t + e, at, :] = v.astype(BF16)
            return 0

        far_copy(up, 0, second).wait_recv()
        lax.fori_loop(0, R // qb, block, 0)
        if second:
            pl.semaphore_wait(mate_ok, 1)
        mate_copy(up, second).start()

    def tp_last(up, second):
        far_copy(up, 1, second).wait_recv()
        mate_copy(up, second).wait_recv()
        here = half(1)
        v = []
        for e in range(2):
            last = wins[2 * T + 2 + e, :R, :] if second else tpr2[e]
            v.append(up[2 * t + e, here, :].astype(F32) + came_far(second, e, here) + last.astype(F32))
        v = jnp.concatenate(v, axis=1)
        x = xs[here, pl.ds(pl.multiple_of(t * pw, pw), pw)].astype(F32)
        if second:
            u = v
            z = (x - norms[here, 0:1]) * norms[here, 1:2]
            lane = lax.broadcasted_iota(jnp.int32, (R, 128), 1)
            one, two = jnp.sum(u, axis=1, keepdims=True), jnp.sum(u * z, axis=1, keepdims=True)
            row_r[t] = jnp.where(lane == 0, one, jnp.where(lane == 1, two, 0.0)).T[:8]
            for s in range(1, T):
                row_copy(s).start()
            for s in range(1, T):
                row_copy(s).wait()
            both = row_r[0]
            for s in range(1, T):
                both = both + row_r[s]
            both = jnp.concatenate([both, jnp.zeros((120, R), F32)], axis=0).T * (1.0 / D)
            dx = norms[here, 1:2] * (u - both[:, 0:1] - z * both[:, 1:2])
            kept = env["up"]
            load((cot, kept.at[pl.ds(0, 2), pl.ds(0, R), :]))
            c = jnp.concatenate([kept[0, :R, :], kept[1, :R, :]], axis=1).astype(F32)
            c = c * jnp.broadcast_to(row_scale[...], (128, R)).T[:, 0:1]
            dtok_o[...] = (c + dx).astype(BF16)
        else:
            mixed_o[...] = (x + v + bias[...]).astype(BF16)
        for h in range(2):
            near_copy(up, second, h, 0).wait_send()
            near_copy(up, second, h, 1).wait_send()
            far_copy(up, h, second).wait_send()
        mate_copy(up, second).wait_send()

    def row_copy(s):
        return rc(row_r.at[t], row_r.at[t], xsem.at[0, 0, s], xsem.at[0, 1, s], (f, lax.rem(t + s, T)))

    def norm_copy(s):
        return rc(nrm_r.at[t], nrm_r.at[t], xsem.at[1, 0, s], xsem.at[1, 1, s], (f, lax.rem(t + s, T)))

    def sum_copy(s):
        to = lax.rem(f + s, F)
        return rc(sum_s.at[to], sum_r.at[f], xsem.at[2, 0, s], xsem.at[2, 1, s], (to, t))

    def bias_copy(s):
        return rc(bsum, bias_o.at[f], xsem.at[3, 0, s], xsem.at[3, 1, s], (lax.rem(f + s, F), t))

    def small_sums():
        for s in range(1, F):
            sum_copy(s).wait()
            bias_copy(s).wait()
        v = sum_r[0]
        for s in range(1, F):
            v = v + sum_r[s]
        nrm_r[t] = v
        for s in range(1, T):
            norm_copy(s).start()
        for s in range(1, T):
            norm_copy(s).wait()
        both = nrm_r[0]
        for s in range(1, T):
            both = both + nrm_r[s]
        row = lax.broadcasted_iota(jnp.int32, both.shape, 0)
        norm_o[...] = jnp.where(row == 4, v * 0.5, both)

    env = {}
    far_out = tuple(range(dp - 1, 2, -1))
    groups = {"a": 0, "b": 1} | {str(n + 1): 2 + n for n in range(NB)}
    paired, far_steps = set(), []

    def step(name):
        kind, rest = name.rstrip("0123456789abiokv"), ""
        rest = name[len(kind):]
        if kind == "pair":
            pair_copy(int(rest)).start()
            mine_copy(int(rest)).start()
        elif kind == "own":
            send_own(int(rest[0]), rest[1])
        elif kind == "mate":
            send_mate(int(rest[0]), rest[1], rest[0] not in paired)
            paired.add(rest[0])
        elif kind == "arr":
            g, k = int(rest[0]), int(rest[1])
            for n in range(k, dp if k == 3 else k + 1):
                arrive(g, n)
        elif kind == "rx":
            rows_x(int(rest)).start()
            rows_own(int(rest)).start()
        elif kind == "rc":
            rows_on(int(rest))
        elif kind == "stats":
            stats()
        elif kind == "proj":
            proj()
        elif kind == "datt":
            datt()
        elif kind == "ffn":
            ffn(int(rest))
        elif kind == "att":
            attention(int(rest))
        elif kind == "qd":
            for k in range(1, reach) if rest == "1" else (reach,):
                qd_step(k)
        elif kind == "ls":
            stat_send() if rest == "0" else stat_wait()
        elif kind == "d":
            key_grads(int(rest[-1]))
        elif kind == "st":
            g, k, io = groups[rest[0]], int(rest[1]), rest[2]
            if k == 3:
                for n in far_out:
                    stage(g, n, io)
            elif k == 2 and io == "o":
                for n in far_out + (2,):
                    stage(g, n, io)
            else:
                stage(g, k, io)
        elif kind == "fin":
            final(groups[rest])
        elif kind == "out":
            out_step(env["up"])
        elif kind == "far":
            tp_far(env["up"] if rest[0] == "0" else wins, rest[0] == "1", int(rest[1]))
        elif kind == "mt":
            tp_mate(env["up"] if rest == "0" else wins, rest == "1")
        elif kind == "last":
            tp_last(env["up"] if rest == "0" else wins, rest == "1")
        elif kind == "hid":
            hidden_step()
        elif kind == "q":
            qkv_step()
        elif kind == "small":
            small_sums()
        else:
            hop = int(rest[-2])
            for k in range(1, reach) if hop == 1 else (reach,):
                kv_step("kv".index(rest[-1]), k)

    def finish_scope(up):
        env["up"] = up
        for name in ORDER[ORDER.index("out") :]:
            step(name)

    sums[...] = jnp.zeros_like(sums)
    bsum[...] = jnp.zeros_like(bsum)
    for name in ORDER[: ORDER.index("out")]:
        step(name)
    pl.run_scoped(finish_scope, pltpu.VMEM((2 * T, plane, HDIM), BF16))

    for k in range(reach):
        @pl.when(d >= k + 1)
        def _():
            stat_copy(k + 1).wait_send()
    for a in range(2):
        rows_x(a).wait_send()
        rows_c(a).wait_send()
    for g in range(GROUPS):
        gather_sent(g)
    for g in range(2 + NB):
        for k in range(1, dp):
            for way in range(2):
                @pl.when(from_dist(k, 1 - way))
                def _():
                    rs_copy(g, k, way).wait_send()
        for c in final_copies(g):
            c.wait()


def block(tok, gh, w_att, w_fc, vecs, bq, b_in, bias, cot, row_scale, tabs, firstq, dims):
    R, D, feats, dp, reach = dims
    plane, pf, F, T = 2 * R, 2 * feats, 2 * dp, lax.axis_size("tp")
    aw = 4 * HDIM
    hu = w_fc.shape[3] // 2
    gw = hu * NB
    pw = D // T
    sds = jax.ShapeDtypeStruct
    vm = pltpu.VMEM
    dma = pltpu.SemaphoreType.DMA
    reg = pltpu.SemaphoreType.REGULAR
    return pl.pallas_call(
        functools.partial(block_kernel, dims),
        out_shape=[sds((D, aw), BF16)] + [sds((D, 2 * hu), BF16)] * NB
        + [sds((R, pw), BF16), sds((R, pw), BF16), sds((8, feats), F32), sds((F, 8, gw), F32)]
        + [sds((3, feats, 2 * HDIM), BF16), sds((2 * HDIM, feats), BF16)]
        + [sds((feats, 2 * gw), BF16), sds((2 * gw, feats), BF16)],
        in_specs=[ANY] * 4 + [VMEM] * 4 + [ANY] + [VMEM] * 3,
        out_specs=[ANY] * GROUPS + [VMEM] * 4 + [ANY] * 4,
        scratch_shapes=[
            vm((plane, D), BF16), vm((plane, D), BF16), vm((D, max(aw, gw)), BF16),
            vm((4 * (reach + 1), plane, HDIM), BF16), vm((8, (reach + 1) * plane), F32),
            vm((plane, gw), BF16), vm((plane, gw), BF16), vm((plane, 3 * HDIM), BF16), vm((plane, HDIM), BF16),
            vm((2, 2, plane, HDIM), BF16), vm((2, plane, HDIM), BF16), vm((2, R, HDIM), BF16),
            vm((2, dp + 1, pf, 2 * HDIM), BF16), vm((NB, dp + 1, pf, 2 * hu), BF16),
            vm((plane, 2), F32),
            vm((2, HDIM, feats), BF16), vm((NB, 2, hu, feats), BF16),
            vm((8, D), F32), vm((8, gw), F32), vm((F, 8, feats), F32), vm((F, 8, feats), F32),
            vm((T, 8, R), F32), vm((T, 8, feats), F32),
            dma((GROUPS + 2,)), dma((4, 4)), dma((2, GROUPS)), dma((GROUPS, dp, 2, 2)), dma((GROUPS, F)),
            dma((2, 2, reach + 1)), dma((2, 2, reach + 1)), dma((2, reach + 1)), dma((2 + NB, dp, 2)), dma((2 + NB, dp + 1)), dma((2 + NB, 2, 3)),
            dma((NB + 2,)), dma((4, 2, F)), dma((2, 2, 7)), reg, reg, reg,
        ],
        compiler_params=pltpu.CompilerParams(
            collective_id=4, has_side_effects=True, vmem_limit_bytes=63 << 20
        ),
        name="block",
    )(tok, gh, w_att, w_fc, vecs, bq, b_in, bias, cot, row_scale, tabs, firstq)


def on_device(
    tokens,
    qkv_weight,
    qkv_bias,
    dense_weight,
    dense_bias,
    fc_in_weight,
    fc_in_bias,
    fc_out_weight,
    fc_out_bias,
    norm1_gain,
    norm1_shift,
    norm2_gain,
    norm2_shift,
    cotangent,
    subset_ids,
    seq_starts,
):
    rows, width = tokens.shape
    shards = lax.axis_size("fsdp")
    tps = lax.axis_size("tp")
    dp = shards // 2
    f = lax.axis_index("fsdp")
    t = lax.axis_index("tp")
    i = lax.rem(f, 2)
    d = f // 2
    total = rows * shards
    scale = 1.0 / math.sqrt(HDIM)
    feats = qkv_weight.shape[0]
    units = fc_in_weight.shape[1]
    head_cols = qkv_weight.shape[2]
    heads_here = head_cols // HDIM
    hd = qkv_bias.shape[2]
    ub = fc_in_bias.shape

    match = subset_ids[:, None] == jnp.arange(SUBSETS, dtype=jnp.int32)[None, :]
    counts = jnp.sum(match.astype(F32), axis=0)
    vecs = [norm1_gain, norm1_shift, norm2_gain, norm2_shift, dense_bias, fc_out_bias]
    pack = jnp.concatenate(
        [v.astype(F32) for v in vecs]
        + [qkv_bias.astype(F32).reshape(-1), fc_in_bias.astype(F32).reshape(-1), counts]
    )
    size = pack.shape[0]
    lanes = -(-size // 1024) * 128
    got = exchange(jnp.pad(pack, (0, 8 * lanes - size)).reshape(8, lanes), "fsdp", False, 1)
    got = got.reshape(shards, 8 * lanes)
    gain1, shift1, gain2, shift2, b_dense, b_out = [
        got[:, k * feats : (k + 1) * feats].reshape(width) for k in range(6)
    ]
    at = 6 * feats
    nq = 3 * heads_here * hd
    b_qkv = got[:, at : at + nq].reshape(shards, 3, heads_here, hd)
    b_qkv = b_qkv.transpose(1, 2, 0, 3).reshape(3, heads_here, HDIM)
    b_qkv = lax.dynamic_index_in_dim(b_qkv, i, 1, keepdims=False).reshape(3 * HDIM)
    at += nq
    b_in = got[:, at : at + units // shards].reshape(shards, ub[0], ub[1])
    b_in = half_of(b_in.transpose(1, 0, 2).reshape(units), i, 0)
    at += units // shards
    counts = jnp.sum(got[:, at : at + SUBSETS], axis=0)
    table = total / (SUBSETS * counts)
    row_scale = jnp.sum(jnp.where(match, table[None, :], 0.0), axis=1)
    carried = cotangent.astype(F32) * row_scale[:, None]
    grad_here = carried.astype(BF16)

    hu = units // 2 // NB
    w_att = jnp.concatenate(
        [
            qkv_weight.reshape(feats, 3, heads_here, HDIM).transpose(2, 0, 1, 3).reshape(2, feats, 3 * HDIM),
            dense_weight.reshape(heads_here, HDIM, feats).transpose(0, 2, 1),
        ],
        axis=2,
    )
    w_fc = jnp.concatenate(
        [
            fc_in_weight.reshape(feats, 2, NB, hu).transpose(2, 1, 0, 3),
            fc_out_weight.reshape(2, NB, hu, feats).transpose(1, 0, 3, 2),
        ],
        axis=3,
    )
    plane = 2 * rows
    start_row = d * plane
    reach = min(dp - 1, -(-(SEQ_LEN - 1) // plane))
    here = start_row + jnp.arange(plane, dtype=jnp.int32)
    docs_here, pos_here = locate(here, seq_starts)
    later = start_row + jnp.arange((reach + 1) * plane, dtype=jnp.int32)
    _, pos_later = locate(later, seq_starts)
    first_later = later - pos_later.astype(jnp.int32) - start_row
    first_later = jnp.where(later < total, first_later, 1 << 30)[None, :]
    cosine, sine = rotary_tables(pos_here)
    ones = jnp.ones((plane, 128 - ROT), F32)
    none = jnp.zeros((plane, 128 - ROT), F32)
    tabs = jnp.stack(
        [
            jnp.concatenate([cosine, cosine, ones], 1),
            jnp.concatenate([-sine, sine, none], 1),
        ]
    )
    vecs = jnp.stack([gain1, shift1, gain2, shift2] + [jnp.zeros_like(gain1)] * 4)
    dims = (rows, width, feats, dp, reach)
    part_w = width // tps
    offset = t * part_w
    cut = lambda vec: lax.dynamic_slice_in_dim(vec, offset, part_w, vec.ndim - 1)
    bias = (cut(b_dense) + cut(b_out)).reshape(1, -1)
    cot_here = cut(cotangent).reshape(rows, 2, part_w // 2).transpose(1, 0, 2)
    mixed, tokens_grad, norm_grads, bias_sums, g_qkv, g_dense, g_in, g_out = block(
        tokens, grad_here, w_att, w_fc, vecs, b_qkv.reshape(1, -1), b_in.reshape(1, -1), bias, cot_here, row_scale[None, :], tabs,
        first_later, dims,
    )[GROUPS:]
    qkv_weight_grad = g_qkv.transpose(1, 0, 2).astype(F32)
    dense_weight_grad = g_dense.astype(F32)
    fc_in_weight_grad = g_in.astype(F32)
    fc_out_weight_grad = g_out.astype(F32)
    bias_grad = norm_grads[4]

    bias_sums = jnp.sum(bias_sums.reshape(dp, 2, 8, units // 2), axis=0)
    in_bias_grad = bias_sums[:, 0].reshape(ub[0], shards * ub[1])
    in_bias_grad = lax.dynamic_slice_in_dim(in_bias_grad, f * ub[1], ub[1], 1)
    qkv_bias_grad = bias_sums[:, 1, : 3 * HDIM].reshape(2, 3, HDIM).transpose(1, 0, 2)
    qkv_bias_grad = lax.dynamic_slice_in_dim(qkv_bias_grad, f * hd, hd, 2)
    return (
        mixed,
        tokens_grad,
        qkv_weight_grad,
        qkv_bias_grad,
        dense_weight_grad,
        bias_grad,
        fc_in_weight_grad,
        in_bias_grad,
        fc_out_weight_grad,
        bias_grad,
        norm_grads[0],
        norm_grads[1],
        norm_grads[2],
        norm_grads[3],
    )


def solution(mesh):
    in_specs = (
        P("fsdp", None),
        P("fsdp", None, "tp"),
        P(None, "tp", "fsdp"),
        P("tp", "fsdp"),
        P("fsdp"),
        P("fsdp", "tp"),
        P("tp", "fsdp"),
        P("tp", "fsdp"),
        P("fsdp"),
        P("fsdp"),
        P("fsdp"),
        P("fsdp"),
        P("fsdp"),
        P("fsdp", None),
        P("fsdp"),
        P(),
    )
    out_specs = (
        P("fsdp", "tp"),
        P("fsdp", "tp"),
        P("fsdp", None, "tp"),
        P(None, "tp", "fsdp"),
        P("tp", "fsdp"),
        P("fsdp"),
        P("fsdp", "tp"),
        P("tp", "fsdp"),
        P("tp", "fsdp"),
        P("fsdp"),
        P("fsdp"),
        P("fsdp"),
        P("fsdp"),
        P("fsdp"),
    )
    return jax.shard_map(
        on_device, mesh=mesh, in_specs=in_specs, out_specs=out_specs, check_vma=False
    )
```
